512 devices in a mesh: dp: 64 (over z, y), tensor: 8 (over x, core).
Axes of the slice: x: 4, y: 4, z: 16, core: 2. Of those that a mesh axis runs over, the one named last changes fastest.
Arguments:
- normed: bfloat16 [32768, 4096], P('dp', 'tensor'), may hold values from -6 to 6
- output_gradient: bfloat16 [32768, 4096], P('dp', 'tensor'), may hold values from -480 to 480
- gate_preactivation: bfloat16 [32768, 7168], P('dp', 'tensor'), may hold values from -48 to 48
- upward_preactivation: bfloat16 [32768, 7168], P('dp', 'tensor'), may hold values from -48 to 48
- frozen_down_weight: bfloat16 [7168, 4096], P('tensor', 'dp'), may hold values from -0.0625 to 0.0625
- adapter_width_factors: bfloat16 [3, 16, 4096], replicated, may hold values from -0.09375 to 0.09375
- adapter_hidden_factors: bfloat16 [3, 16, 7168], P(None, None, 'tensor'), may hold values from -0.0625 to 0.0625
- clipping_limit: float32 [1], replicated, may hold values from 1000 to 3000
- width_noise_draw: float32 [3, 16, 4096], P(None, None, 'tensor'), may hold values from -0.3 to 0.3
- hidden_noise_draw: float32 [3, 16, 7168], P(None, None, 'tensor'), may hold values from -0.3 to 0.3
Outputs:
- grad_wide: float32 [3, 16, 4096], P(None, None, 'tensor')
- grad_hidden: float32 [3, 16, 7168], P(None, None, 'tensor')
The draws below stay inside these ranges and needn't reach their ends.
All inputs are finite; a program needn't handle non-finite values.
Results may differ from the reference program's by a relative error of at most 0.0011.
The reference program's roundings to bfloat16 on the way count: a program that leaves them out, or rounds other values in their place, can miss the bound.
Values may be sent and summed in bfloat16 or wider, within the bound.
No kernel may reach another device: no remote copies, remote signals or barrier semaphores. Data moves between devices by JAX's collectives and lax.ppermute only.
A program may use at most 64 MiB of HBM per device.

```python
import math
import jax
import jax.numpy as jnp
from jax import lax

MODEL_WIDTH = 4096
HIDDEN_SHARE = 7168
ADAPTER_RANK = 16
SEQUENCE_TOKENS = 128
SEQS = 256
TOKENS = 32768


def column_scales(key, count):
    rough = jax.random.uniform(key, (count,), jnp.float32)
    place = jnp.arange(count, dtype=jnp.float32) / count
    return jnp.exp(jnp.log(3.0) * place + jnp.log(4.0) * rough)


def draw_gate_preactivation(key, part):
    key = jax.random.fold_in(key, 11)
    key_base, key_cols = jax.random.split(key)
    base = jnp.clip(jax.random.normal(key_base, (TOKENS, HIDDEN_SHARE), jnp.float32), -4.0, 4.0)
    return (base * column_scales(key_cols, HIDDEN_SHARE)[None, :]).astype(jnp.bfloat16)


def draw_upward_preactivation(key, part):
    key = jax.random.fold_in(key, 12)
    key_base, key_cols = jax.random.split(key)
    base = jnp.clip(jax.random.normal(key_base, (TOKENS, HIDDEN_SHARE), jnp.float32), -4.0, 4.0)
    return (base * column_scales(key_cols, HIDDEN_SHARE)[None, :]).astype(jnp.bfloat16)


def draw_output_gradient(key, part):
    key = jax.random.fold_in(key, 13)
    key_base, key_cols, key_rows = jax.random.split(key, 3)
    count = TOKENS // SEQUENCE_TOKENS
    row_scales = jnp.exp(jnp.log(10.0) * jax.random.uniform(key_rows, (count,), jnp.float32, -4.0, 1.0))
    base = jnp.clip(jax.random.normal(key_base, (count, SEQUENCE_TOKENS, MODEL_WIDTH), jnp.float32), -4.0, 4.0)
    values = base * row_scales[:, None, None] * column_scales(key_cols, MODEL_WIDTH)[None, None, :]
    return values.reshape(TOKENS, MODEL_WIDTH).astype(jnp.bfloat16)


def level_of(own_key, extent, shards, low, largest):
    factor_of = 1.0
    for axis_at, shards_of in shards:
        draws = jax.random.uniform(jax.random.fold_in(jax.random.fold_in(own_key, 6), axis_at), (shards_of,), jnp.float32, low / len(shards), largest / len(shards))
        factor_of = factor_of * jnp.repeat(jnp.exp(draws), extent[axis_at] // shards_of).reshape((-1,) + (1,) * (len(extent) - 1 - axis_at))
    return factor_of


def scatter_about(own_key, dims, scale, most, pieces=(), kind=jnp.bfloat16):
    gain = level_of(own_key, dims, pieces, -0.22, 0.18) if pieces else 1.0
    entries = jax.random.normal(own_key, dims, jnp.float32) * scale * gain
    return jnp.minimum(jnp.maximum(entries, -most), most).astype(kind)


def setup_inputs(seed: int = 0) -> dict:
    streams_of = jax.random.split(jax.random.key(seed), 11)
    return {
        "normed": scatter_about(streams_of[0], (TOKENS, MODEL_WIDTH), 1.0, 6.0, ((0, 64), (1, 8))),
        "output_gradient": draw_output_gradient(jax.random.fold_in(streams_of[10], 71), 0),
        "gate_preactivation": draw_gate_preactivation(jax.random.fold_in(streams_of[10], 71), 0),
        "upward_preactivation": draw_upward_preactivation(jax.random.fold_in(streams_of[10], 71), 0),
        "frozen_down_weight": scatter_about(streams_of[4], (HIDDEN_SHARE, MODEL_WIDTH), HIDDEN_SHARE ** -0.5, 0.0625, ((0, 8), (1, 64))),
        "adapter_width_factors": scatter_about(streams_of[5], (3, ADAPTER_RANK, MODEL_WIDTH), MODEL_WIDTH ** -0.5, 0.09375),
        "adapter_hidden_factors": scatter_about(streams_of[6], (3, ADAPTER_RANK, HIDDEN_SHARE), HIDDEN_SHARE ** -0.5, 0.0625, ((2, 8),)),
        "clipping_limit": jnp.clip(jnp.exp(jax.random.uniform(streams_of[7], (1,), jnp.float32, math.log(1000.0), math.log(3000.0))), 1000.0, 3000.0),
        "width_noise_draw": scatter_about(streams_of[8], (3, ADAPTER_RANK, MODEL_WIDTH), 0.05, 0.3, ((2, 8),), jnp.float32),
        "hidden_noise_draw": scatter_about(streams_of[9], (3, ADAPTER_RANK, HIDDEN_SHARE), 0.05, 0.3, ((2, 8),), jnp.float32),
    }


adapter_scale = 2.0

def reference(normed, output_gradient, gate_preactivation, upward_preactivation, frozen_down_weight, adapter_width_factors, adapter_hidden_factors, clipping_limit, width_noise_draw, hidden_noise_draw):
    bound = clipping_limit[0]

    def one_sequence(carry, index):
        wide_total, hidden_total = carry
        start = (index * SEQUENCE_TOKENS).astype(jnp.int32)
        input_rows = lax.dynamic_slice_in_dim(normed, start, SEQUENCE_TOKENS, 0)
        output_gradient_rows = lax.dynamic_slice_in_dim(output_gradient, start, SEQUENCE_TOKENS, 0)
        gate_rows = lax.dynamic_slice_in_dim(gate_preactivation, start, SEQUENCE_TOKENS, 0).astype(jnp.float32)
        up_rows = lax.dynamic_slice_in_dim(upward_preactivation, start, SEQUENCE_TOKENS, 0).astype(jnp.float32)
        adapter_backward = jnp.dot(output_gradient_rows, adapter_width_factors[2].T, preferred_element_type=jnp.float32).astype(jnp.bfloat16)
        hidden_gradient = jnp.dot(output_gradient_rows, frozen_down_weight.T, preferred_element_type=jnp.float32)
        hidden_gradient = hidden_gradient + adapter_scale * jnp.dot(adapter_backward, adapter_hidden_factors[2], preferred_element_type=jnp.float32)
        sigmoid = jax.nn.sigmoid(gate_rows)
        silu_value = gate_rows * sigmoid
        silu_slope = sigmoid * (1.0 + gate_rows * (1.0 - sigmoid))
        gated_activation = (silu_value * up_rows).astype(jnp.bfloat16)
        gate_gradient = (hidden_gradient * up_rows * silu_slope).astype(jnp.bfloat16)
        upward_gradient = (hidden_gradient * silu_value).astype(jnp.bfloat16)
        input_gate = jnp.dot(input_rows, adapter_width_factors[0].T, preferred_element_type=jnp.float32).astype(jnp.bfloat16)
        input_upward = jnp.dot(input_rows, adapter_width_factors[1].T, preferred_element_type=jnp.float32).astype(jnp.bfloat16)
        down_middle = jnp.dot(gated_activation, adapter_hidden_factors[2].T, preferred_element_type=jnp.float32).astype(jnp.bfloat16)
        gate_middle = jnp.dot(gate_gradient, adapter_hidden_factors[0].T, preferred_element_type=jnp.float32).astype(jnp.bfloat16)
        upward_middle = jnp.dot(upward_gradient, adapter_hidden_factors[1].T, preferred_element_type=jnp.float32).astype(jnp.bfloat16)
        hidden_norm_terms = adapter_scale * jnp.stack([jnp.dot(input_gate.T, gate_gradient, preferred_element_type=jnp.float32), jnp.dot(input_upward.T, upward_gradient, preferred_element_type=jnp.float32), jnp.dot(adapter_backward.T, gated_activation, preferred_element_type=jnp.float32)])
        width_norm_terms = adapter_scale * jnp.stack([jnp.dot(gate_middle.T, input_rows, preferred_element_type=jnp.float32), jnp.dot(upward_middle.T, input_rows, preferred_element_type=jnp.float32), jnp.dot(down_middle.T, output_gradient_rows, preferred_element_type=jnp.float32)])
        squares = jnp.sum(hidden_norm_terms * hidden_norm_terms) + jnp.sum(width_norm_terms * width_norm_terms)
        norm_value = jnp.sqrt(squares)
        weight_value = bound / jnp.maximum(norm_value, bound)
        return ((wide_total + weight_value * width_norm_terms, hidden_total + weight_value * hidden_norm_terms), None)
    initial = (jnp.zeros((3, ADAPTER_RANK, MODEL_WIDTH), jnp.float32), jnp.zeros((3, ADAPTER_RANK, HIDDEN_SHARE), jnp.float32))
    (wide_total, hidden_total), _ = lax.scan(one_sequence, initial, jnp.arange(SEQS, dtype=jnp.int32))
    grad_wide = (wide_total + bound * width_noise_draw) / SEQS
    grad_hidden = (hidden_total + bound * hidden_noise_draw) / SEQS
    return (grad_wide, grad_hidden)
```

```python
import functools

import jax
import jax.numpy as jnp
from jax import lax
from jax.experimental import pallas as pl
from jax.experimental.pallas import tpu as pltpu
from jax.sharding import Mesh
from jax.sharding import PartitionSpec as P

SEQUENCE_TOKENS = 128
RANK = 16
SCALE = 2.0
F32 = jnp.float32
BF16 = jnp.bfloat16


def contract(left, right, left_dim, right_dim):
    return lax.dot_general(
        left, right, (((left_dim,), (right_dim,)), ((), ())), preferred_element_type=F32
    )


def hidden_kernel(
    n_blocks,
    place_ref,
    gradient_ref,
    *refs,
):
    block_refs = refs[:n_blocks]
    (gate_ref, up_ref, factors_ref, in_ref, lora_ref, lora_t_ref) = refs[n_blocks : n_blocks + 6]
    sums_ref, mids_ref = refs[n_blocks + 6 : n_blocks + 8]
    weight, gradient, total, sems = refs[n_blocks + 8 :]
    tokens, hidden = gate_ref.shape
    sequences = tokens // SEQUENCE_TOKENS

    copies = [pltpu.make_async_copy(gradient_ref, gradient, sems.at[n_blocks])]
    for i, block in enumerate(block_refs):
        rows = block.shape[0]
        start = pl.multiple_of(place_ref[i] * 128, 128)
        copies.append(
            pltpu.make_async_copy(block, weight.at[pl.ds(start, rows), :], sems.at[i])
        )
    for copy in copies:
        copy.start()
    mids_ref[...] = jnp.zeros_like(mids_ref)
    for copy in copies:
        copy.wait()

    def tile(start, width):
        cols = pl.ds(start, width)
        factors = factors_ref[:, cols]
        total[:, :width] = jnp.dot(
            gradient[...], weight[:, cols], preferred_element_type=F32
        ) + SCALE * jnp.dot(lora_ref[...], factors[2 * RANK :], preferred_element_type=F32)
        for e in range(sequences):
            rows = slice(e * SEQUENCE_TOKENS, (e + 1) * SEQUENCE_TOKENS)
            hidden_grad = total[rows, :width]
            gate = gate_ref[rows, cols].astype(F32)
            up = up_ref[rows, cols].astype(F32)
            sigmoid = jax.nn.sigmoid(gate)
            silu = gate * sigmoid
            slope = sigmoid * (1.0 + gate * (1.0 - sigmoid))
            activation = (silu * up).astype(BF16)
            gate_grad = (hidden_grad * up * slope).astype(BF16)
            up_grad = (hidden_grad * silu).astype(BF16)
            left = (in_ref[:RANK, rows], in_ref[RANK:, rows], lora_t_ref[:, rows])
            for j, right in enumerate((gate_grad, up_grad, activation)):
                part = slice(j * RANK, (j + 1) * RANK)
                sums_ref[e, part, cols] = SCALE * jnp.dot(
                    left[j], right, preferred_element_type=F32
                )
                mids_ref[part, rows] += contract(factors[part], right, 1, 1)

    step = 256
    whole = hidden // step

    def body(i, carry):
        tile(pl.multiple_of(i * step, step), step)
        return carry

    lax.fori_loop(0, whole, body, 0)
    if hidden > whole * step:
        tile(whole * step, hidden - whole * step)
    for e in range(sequences):
        square = sums_ref[e] * sums_ref[e]
        line = jnp.sum(jnp.sum(square, axis=0, keepdims=True), axis=1, keepdims=True)
        mids_ref[3 * RANK + e : 3 * RANK + e + 1, :] = jnp.broadcast_to(line, (1, tokens))


def clip_kernel(
    place_ref,
    clip_ref,
    mids_ref,
    sums_ref,
    normed_ref,
    gradient_ref,
    out_ref,
    wide,
):
    sequences, _, hidden = sums_ref.shape
    tokens, width = normed_ref.shape
    local = wide.shape[1]
    place = place_ref[0]
    bound = clip_ref[0]
    wide[...] = jnp.zeros_like(wide)
    weights = []
    for e in range(sequences):
        rows = slice(e * SEQUENCE_TOKENS, (e + 1) * SEQUENCE_TOKENS)
        mids = mids_ref[: 3 * RANK, rows].astype(BF16)
        squares = jnp.zeros((RANK, local), F32)

        def body(i, squares, rows=rows, mids=mids):
            cols = pl.ds(pl.multiple_of(i * local, local), local)
            first = SCALE * jnp.dot(
                mids[: 2 * RANK], normed_ref[rows, cols], preferred_element_type=F32
            )
            second = SCALE * jnp.dot(
                mids[2 * RANK :], gradient_ref[rows, cols], preferred_element_type=F32
            )
            return (
                squares
                + first[:RANK] * first[:RANK]
                + first[RANK:] * first[RANK:]
                + second * second
            )

        squares = lax.fori_loop(0, width // local, body, squares)
        total = jnp.sum(jnp.sum(squares, axis=0, keepdims=True), axis=1, keepdims=True)
        total = total + mids_ref[3 * RANK + e : 3 * RANK + e + 1, 0:1]
        weight = bound / jnp.maximum(jnp.sqrt(total), bound)
        weights.append(weight)
        cols = pl.ds(pl.multiple_of(place * local, local), local)
        wide[: 2 * RANK] += weight * (
            SCALE
            * jnp.dot(mids[: 2 * RANK], normed_ref[rows, cols], preferred_element_type=F32)
        )
        wide[2 * RANK :] += weight * (
            SCALE
            * jnp.dot(mids[2 * RANK :], gradient_ref[rows, cols], preferred_element_type=F32)
        )
    lanes = out_ref.shape[0] // 6
    for t in range(out_ref.shape[0]):
        r, c = divmod(t, lanes)
        rows = slice(8 * r, 8 * r + 8)
        at = c * 128
        if at < local:
            value = wide[rows, at : at + 128]
        elif at < local + hidden:
            at = at - local
            value = weights[0] * sums_ref[0, rows, at : at + 128]
            for e in range(1, sequences):
                value = value + weights[e] * sums_ref[e, rows, at : at + 128]
        else:
            value = jnp.zeros((8, 128), F32)
        out_ref[t] = value


def ring(size, by):
    return [(i, (i + by) % size) for i in range(size)]


def per_device(
    sizes,
    normed,
    output_gradient,
    gate_preactivation,
    upward_preactivation,
    frozen_down_weight,
    adapter_width_factors,
    adapter_hidden_factors,
    clipping_limit,
    width_noise_draw,
    hidden_noise_draw,
):
    tokens, local_width = normed.shape
    hidden = gate_preactivation.shape[1]
    sequences = tokens // SEQUENCE_TOKENS
    n_z = sizes["zh"] * sizes["zl"]
    n_tensor = sizes["x"] * sizes["c"]
    z_axes, tensor_axes = ("zh", "zl"), ("x", "c")
    z = lax.axis_index(z_axes)
    tensor = lax.axis_index(tensor_axes)

    gradient = lax.all_gather(output_gradient, tensor_axes, axis=1, tiled=True)
    block = lax.all_gather(frozen_down_weight.T, "y", axis=0, tiled=True)
    normed_all = lax.all_gather(normed, tensor_axes, axis=1, tiled=True)

    rows = block.shape[0]
    half = rows // 2
    units = rows // 128
    blocks, places = [block], [z * units]
    low = high = block
    for k in range(1, n_z // 2):
        low = lax.ppermute(low, z_axes, ring(n_z, 1))
        high = lax.ppermute(high, z_axes, ring(n_z, -1))
        blocks += [low, high]
        places += [((z + n_z - k) % n_z) * units, ((z + k) % n_z) * units]
    far = ((z + n_z // 2) % n_z) * units
    blocks.append(lax.ppermute(low[:half], z_axes, ring(n_z, 1)))
    blocks.append(lax.ppermute(high[half:], z_axes, ring(n_z, -1)))
    places += [far, far + units // 2]

    lora_t = contract(adapter_width_factors[2], gradient, 1, 1).astype(BF16)
    in_t = contract(
        adapter_width_factors[:2].reshape(2 * RANK, -1), normed_all, 1, 1
    ).astype(BF16)

    vmem = pl.BlockSpec(memory_space=pltpu.VMEM)
    smem = pl.BlockSpec(memory_space=pltpu.SMEM)
    anywhere = pl.BlockSpec(memory_space=pl.ANY)
    sums, mids = pl.pallas_call(
        functools.partial(hidden_kernel, len(blocks)),
        out_shape=(
            jax.ShapeDtypeStruct((sequences, 3 * RANK, hidden), F32),
            jax.ShapeDtypeStruct((8 * n_tensor, tokens), F32),
        ),
        in_specs=[smem, anywhere] + [anywhere] * len(blocks) + [vmem] * 6,
        out_specs=(vmem, vmem),
        scratch_shapes=[
            pltpu.VMEM((n_z * rows, hidden), BF16),
            pltpu.VMEM(gradient.shape, BF16),
            pltpu.VMEM((tokens, 256), F32),
            pltpu.SemaphoreType.DMA((len(blocks) + 1,)),
        ],
        compiler_params=pltpu.CompilerParams(vmem_limit_bytes=40 * 2**20),
        name="hidden_side",
    )(
        jnp.stack(places).astype(jnp.int32),
        gradient,
        *blocks,
        gate_preactivation,
        upward_preactivation,
        adapter_hidden_factors.reshape(3 * RANK, hidden),
        in_t,
        lora_t.T,
        lora_t,
    )

    pieces = lax.all_to_all(mids.reshape(n_tensor, 8, tokens), tensor_axes, 0, 0)
    piece = jnp.sum(pieces, axis=0)
    mids = lax.all_to_all(
        jnp.broadcast_to(piece, (n_tensor,) + piece.shape), tensor_axes, 0, 0
    ).reshape(8 * n_tensor, tokens)

    lanes = 12
    out = pl.pallas_call(
        clip_kernel,
        out_shape=jax.ShapeDtypeStruct((6 * lanes, 8, 128), F32),
        in_specs=[smem, smem, vmem, vmem, vmem, vmem],
        out_specs=vmem,
        scratch_shapes=[pltpu.VMEM((3 * RANK, local_width), F32)],
        compiler_params=pltpu.CompilerParams(vmem_limit_bytes=40 * 2**20),
        name="clip_side",
    )(tensor.reshape(1).astype(jnp.int32), clipping_limit, mids, sums, normed_all, gradient)

    first_axes, second_axes = ("zl", "y"), "zh"
    n_first, n_second = sizes["zl"] * sizes["y"], sizes["zh"]
    part = jnp.sum(
        lax.all_to_all(out.reshape(n_first, -1, 128), first_axes, 0, 0), axis=0
    )
    part = jnp.sum(
        lax.all_to_all(part.reshape(n_second, -1, 128), second_axes, 0, 0), axis=0
    )
    part = lax.all_to_all(
        jnp.broadcast_to(part, (n_second,) + part.shape), second_axes, 0, 0
    ).reshape(-1, 128)
    part = lax.all_to_all(
        jnp.broadcast_to(part, (n_first,) + part.shape), first_axes, 0, 0
    )
    total = (
        part.reshape(6, lanes, 8, 128)
        .transpose(0, 2, 1, 3)
        .reshape(3, RANK, lanes * 128)
    )
    count = sequences * n_z * sizes["y"]
    bound = clipping_limit[0]
    wide = total[:, :, :local_width]
    inner = total[:, :, local_width : local_width + hidden]
    return (
        (wide + bound * width_noise_draw) / count,
        (inner + bound * hidden_noise_draw) / count,
    )


def solution(mesh):
    names = ("zh", "zl", "y", "x", "c")
    extents = (8, 2, 4, 4, 2)
    fine = Mesh(mesh.devices.reshape(extents), names)
    dp, tensor = ("zh", "zl", "y"), ("x", "c")
    placed = (
        P(dp, tensor),
        P(dp, tensor),
        P(dp, tensor),
        P(dp, tensor),
        P(tensor, dp),
        P(),
        P(None, None, tensor),
        P(),
        P(None, None, tensor),
        P(None, None, tensor),
    )
    return jax.shard_map(
        functools.partial(per_device, dict(zip(names, extents, strict=True))),
        mesh=fine,
        in_specs=placed,
        out_specs=(P(None, None, tensor), P(None, None, tensor)),
        check_vma=False,
    )
```

```python
import functools

import jax
import jax.numpy as jnp
from jax import lax
from jax.experimental import pallas as pl
from jax.experimental.pallas import tpu as pltpu
from jax.sharding import Mesh
from jax.sharding import PartitionSpec as P

SEQUENCE_TOKENS = 128
RANK = 16
SCALE = 2.0
F32 = jnp.float32
BF16 = jnp.bfloat16


def contract(left, right, left_dim, right_dim):
    return lax.dot_general(
        left, right, (((left_dim,), (right_dim,)), ((), ())), preferred_element_type=F32
    )


def column_tiles(hidden, step, tile):
    whole = hidden // step

    def body(i, carry):
        tile(pl.multiple_of(i * step, step), step)
        return carry

    lax.fori_loop(0, whole, body, 0)
    if hidden > whole * step:
        tile(whole * step, hidden - whole * step)


def block_product(place_ref, gradient_ref, block_refs, cols):
    left = jnp.concatenate(
        [
            gradient_ref[:, pl.ds(pl.multiple_of(place_ref[i] * 128, 128), block.shape[0])]
            for i, block in enumerate(block_refs)
        ],
        axis=1,
    )
    right = jnp.concatenate([block[:, cols] for block in block_refs], axis=0)
    return jnp.dot(left, right, preferred_element_type=F32)


def gram_of(rows_ref, out_ref):
    for e in range(out_ref.shape[0]):
        rows = rows_ref[e * SEQUENCE_TOKENS : (e + 1) * SEQUENCE_TOKENS, :]
        out_ref[e] = contract(rows, rows, 1, 1)


def first_kernel(n_blocks, place_ref, gradient_ref, *refs):
    block_refs = refs[:n_blocks]
    factor_ref, total_ref, lora_ref, gram_ref = refs[n_blocks:]

    def tile(start, width):
        cols = pl.ds(start, width)
        total_ref[:, cols] = block_product(place_ref, gradient_ref, block_refs, cols)

    column_tiles(total_ref.shape[1], 256, tile)
    lora_ref[...] = contract(factor_ref[...], gradient_ref[...], 1, 1).astype(BF16)
    gram_of(gradient_ref, gram_ref)


def more_kernel(n_blocks, place_ref, gradient_ref, *refs):
    block_refs = refs[:n_blocks]
    before_ref, total_ref = refs[n_blocks:]

    def tile(start, width):
        cols = pl.ds(start, width)
        total_ref[:, cols] = before_ref[:, cols] + block_product(
            place_ref, gradient_ref, block_refs, cols
        )

    column_tiles(total_ref.shape[1], 256, tile)


def normed_kernel(normed_ref, factors_ref, in_ref, gram_ref):
    in_ref[...] = contract(factors_ref[...], normed_ref[...], 1, 1).astype(BF16)
    gram_of(normed_ref, gram_ref)


def hidden_kernel(n_blocks, place_ref, gradient_ref, *refs):
    block_refs = refs[:n_blocks]
    (before_ref, gate_ref, up_ref, factors_ref, in_ref, lora_ref, lora_t_ref) = refs[
        n_blocks : n_blocks + 7
    ]
    sums_ref, mids_ref, total = refs[n_blocks + 7 :]
    tokens, hidden = gate_ref.shape
    sequences = tokens // SEQUENCE_TOKENS
    mids_ref[...] = jnp.zeros_like(mids_ref)

    def tile(start, width):
        cols = pl.ds(start, width)
        factors = factors_ref[:, cols]
        total[:, :width] = (
            before_ref[:, cols]
            + block_product(place_ref, gradient_ref, block_refs, cols)
            + SCALE * jnp.dot(lora_ref[...], factors[2 * RANK :], preferred_element_type=F32)
        )
        for e in range(sequences):
            rows = slice(e * SEQUENCE_TOKENS, (e + 1) * SEQUENCE_TOKENS)
            hidden_grad = total[rows, :width]
            gate = gate_ref[rows, cols].astype(F32)
            up = up_ref[rows, cols].astype(F32)
            sigmoid = jax.nn.sigmoid(gate)
            silu = gate * sigmoid
            slope = sigmoid * (1.0 + gate * (1.0 - sigmoid))
            activation = (silu * up).astype(BF16)
            gate_grad = (hidden_grad * up * slope).astype(BF16)
            up_grad = (hidden_grad * silu).astype(BF16)
            left = (in_ref[:RANK, rows], in_ref[RANK:, rows], lora_t_ref[:, rows])
            for j, right in enumerate((gate_grad, up_grad, activation)):
                part = slice(j * RANK, (j + 1) * RANK)
                sums_ref[e, part, cols] = SCALE * jnp.dot(
                    left[j], right, preferred_element_type=F32
                )
                mids_ref[part, rows] += contract(factors[part], right, 1, 1)

    column_tiles(hidden, 256, tile)
    for e in range(sequences):
        square = sums_ref[e] * sums_ref[e]
        line = jnp.sum(jnp.sum(square, axis=0, keepdims=True), axis=1, keepdims=True)
        mids_ref[3 * RANK + e : 3 * RANK + e + 1, :] = jnp.broadcast_to(line, (1, tokens))


def quadratic(left, gram):
    product = jnp.zeros((left.shape[0], gram.shape[1]), F32)
    rest = gram
    for _ in range(3):
        part = rest.astype(BF16)
        product = product + jnp.dot(left, part, preferred_element_type=F32)
        rest = rest - part.astype(F32)
    return product * left.astype(F32)


def total_of(values):
    return jnp.sum(jnp.sum(values, axis=0, keepdims=True), axis=1, keepdims=True)


def clip_kernel(
    clip_ref,
    mids_ref,
    sums_ref,
    normed_ref,
    gradient_ref,
    normed_gram_ref,
    gradient_gram_ref,
    out_ref,
    wide,
):
    sequences, _, hidden = sums_ref.shape
    local = wide.shape[1]
    bound = clip_ref[0]
    weights = []
    for e in range(sequences):
        rows = slice(e * SEQUENCE_TOKENS, (e + 1) * SEQUENCE_TOKENS)
        mids = mids_ref[: 3 * RANK, rows].astype(BF16)
        square = total_of(quadratic(mids[: 2 * RANK], normed_gram_ref[e])) + total_of(
            quadratic(mids[2 * RANK :], gradient_gram_ref[e])
        )
        square = SCALE * SCALE * jnp.maximum(square, 0.0)
        square = square + mids_ref[3 * RANK + e : 3 * RANK + e + 1, 0:1]
        weight = bound / jnp.maximum(jnp.sqrt(square), bound)
        weights.append(weight)
        first = weight * (
            SCALE * jnp.dot(mids[: 2 * RANK], normed_ref[rows, :], preferred_element_type=F32)
        )
        second = weight * (
            SCALE * jnp.dot(mids[2 * RANK :], gradient_ref[rows, :], preferred_element_type=F32)
        )
        if e == 0:
            wide[: 2 * RANK] = first
            wide[2 * RANK :] = second
        else:
            wide[: 2 * RANK] += first
            wide[2 * RANK :] += second
    lanes = out_ref.shape[0] // 6
    for t in range(out_ref.shape[0]):
        r, c = divmod(t, lanes)
        rows = slice(8 * r, 8 * r + 8)
        at = c * 128
        if at < local:
            value = wide[rows, at : at + 128]
        elif at < local + hidden:
            at = at - local
            value = weights[0] * sums_ref[0, rows, at : at + 128]
            for e in range(1, sequences):
                value = value + weights[e] * sums_ref[e, rows, at : at + 128]
        else:
            value = jnp.zeros((8, 128), F32)
        out_ref[t] = value


def ring(size, by):
    return [(i, (i + by) % size) for i in range(size)]


def per_device(
    sizes,
    normed,
    output_gradient,
    gate_preactivation,
    upward_preactivation,
    frozen_down_weight,
    adapter_width_factors,
    adapter_hidden_factors,
    clipping_limit,
    width_noise_draw,
    hidden_noise_draw,
):
    tokens, local_width = normed.shape
    hidden = gate_preactivation.shape[1]
    sequences = tokens // SEQUENCE_TOKENS
    n_z = sizes["z"]
    n_tensor = sizes["x"] * sizes["c"]
    z_axes, tensor_axes = "z", ("x", "c")
    z = lax.axis_index(z_axes)

    gradient = lax.all_gather(output_gradient, tensor_axes, axis=1, tiled=True)
    block = lax.all_gather(frozen_down_weight.T, "y", axis=0, tiled=True)
    normed_all = lax.all_gather(normed, tensor_axes, axis=1, tiled=True)

    rows = block.shape[0]
    half = rows // 2
    units = rows // 128
    vmem = pl.BlockSpec(memory_space=pltpu.VMEM)
    smem = pl.BlockSpec(memory_space=pltpu.SMEM)
    params = pltpu.CompilerParams(vmem_limit_bytes=32 * 2**20)

    def place(offsets):
        at = [((z + offset) % n_z) * units for offset in offsets]
        return jnp.stack(at).astype(jnp.int32)

    low, high = {0: block}, {0: block}

    def step(k, low_from, high_from):
        low[k] = lax.ppermute(low_from, z_axes, ring(n_z, 1))
        high[k] = lax.ppermute(high_from, z_axes, ring(n_z, -1))

    def product_cost(n_rows, read):
        return pl.CostEstimate(
            flops=2 * tokens * n_rows * hidden, bytes_accessed=read, transcendentals=0
        )

    last = n_z // 2
    for k in range(1, last - 2):
        step(k, low[k - 1], high[k - 1])
    offsets = [0] + [sign * k for k in range(1, last - 4) for sign in (-1, 1)]
    blocks = [block] + [side[k] for k in range(1, last - 4) for side in (low, high)]
    total, lora_t, gradient_gram = pl.pallas_call(
        functools.partial(first_kernel, len(blocks)),
        out_shape=(
            jax.ShapeDtypeStruct((tokens, hidden), F32),
            jax.ShapeDtypeStruct((RANK, tokens), BF16),
            jax.ShapeDtypeStruct((sequences, SEQUENCE_TOKENS, SEQUENCE_TOKENS), F32),
        ),
        in_specs=[smem] + [vmem] * (len(blocks) + 2),
        out_specs=(vmem, vmem, vmem),
        compiler_params=params,
        cost_estimate=product_cost(rows * len(blocks), 8 * 2**20),
        name="first_blocks",
    )(place(offsets), gradient, *blocks, adapter_width_factors[2])

    at = last - 3
    low_in, high_in, total = lax.optimization_barrier((low[at], high[at], total))
    step(last - 2, low_in, high_in)
    offsets = [sign * k for k in range(last - 4, last - 2) for sign in (-1, 1)]
    blocks = [side[k] for k in range(last - 4, last - 2) for side in (low, high)]
    total = pl.pallas_call(
        functools.partial(more_kernel, len(blocks)),
        out_shape=jax.ShapeDtypeStruct((tokens, hidden), F32),
        in_specs=[smem] + [vmem] * (len(blocks) + 2),
        out_specs=vmem,
        input_output_aliases={len(blocks) + 2: 0},
        compiler_params=params,
        cost_estimate=product_cost(rows * len(blocks), 6 * 2**20),
        name="more_blocks",
    )(place(offsets), gradient, *blocks, total)
    step(last - 1, low[last - 2], high[last - 2])

    in_t, normed_gram = pl.pallas_call(
        normed_kernel,
        out_shape=(
            jax.ShapeDtypeStruct((2 * RANK, tokens), BF16),
            jax.ShapeDtypeStruct((sequences, SEQUENCE_TOKENS, SEQUENCE_TOKENS), F32),
        ),
        in_specs=[vmem, vmem],
        out_specs=(vmem, vmem),
        compiler_params=params,
        cost_estimate=pl.CostEstimate(
            flops=2 * tokens * 4096 * 160, bytes_accessed=5 * 2**20, transcendentals=0
        ),
        name="normed_side",
    )(normed_all, adapter_width_factors[:2].reshape(2 * RANK, -1))

    low_in, high_in, total, in_t = lax.optimization_barrier(
        (low[last - 1], high[last - 1], total, in_t)
    )
    step(last, low_in[:half], high_in[half:])
    far = ((z + last) % n_z) * units
    offsets = [sign * k for k in range(last - 2, last) for sign in (-1, 1)]
    blocks = [side[k] for k in range(last - 2, last) for side in (low, high)]
    blocks += [low[last], high[last]]
    places = jnp.concatenate(
        [place(offsets), jnp.stack([far, far + units // 2]).astype(jnp.int32)]
    )
    sums, mids = pl.pallas_call(
        functools.partial(hidden_kernel, len(blocks)),
        out_shape=(
            jax.ShapeDtypeStruct((sequences, 3 * RANK, hidden), F32),
            jax.ShapeDtypeStruct((8 * n_tensor, tokens), F32),
        ),
        in_specs=[smem] + [vmem] * (len(blocks) + 8),
        out_specs=(vmem, vmem),
        scratch_shapes=[pltpu.VMEM((tokens, 256), F32)],
        compiler_params=params,
        name="hidden_side",
    )(
        places,
        gradient,
        *blocks,
        total,
        gate_preactivation,
        upward_preactivation,
        adapter_hidden_factors.reshape(3 * RANK, hidden),
        in_t,
        lora_t.T,
        lora_t,
    )

    pieces = lax.all_to_all(mids.reshape(n_tensor, 8, tokens), tensor_axes, 0, 0)
    piece = jnp.sum(pieces, axis=0)
    mids = lax.all_to_all(
        jnp.broadcast_to(piece, (n_tensor,) + piece.shape), tensor_axes, 0, 0
    ).reshape(8 * n_tensor, tokens)

    lanes = 12
    out = pl.pallas_call(
        clip_kernel,
        out_shape=jax.ShapeDtypeStruct((6 * lanes, 8, 128), F32),
        in_specs=[smem] + [vmem] * 6,
        out_specs=vmem,
        scratch_shapes=[pltpu.VMEM((3 * RANK, local_width), F32)],
        compiler_params=params,
        name="clip_side",
    )(
        clipping_limit,
        mids,
        sums,
        normed,
        output_gradient,
        normed_gram,
        gradient_gram,
    )

    n_y = sizes["y"]
    part = jnp.sum(lax.all_to_all(out.reshape(n_y, -1, 128), "y", 0, 0), axis=0)
    part = jnp.sum(lax.all_to_all(part.reshape(n_z, -1, 128), z_axes, 0, 0), axis=0)
    part = lax.all_to_all(
        jnp.broadcast_to(part, (n_z,) + part.shape), z_axes, 0, 0
    ).reshape(-1, 128)
    part = lax.all_gather(part, "y", axis=0)
    total = (
        part.reshape(6, lanes, 8, 128)
        .transpose(0, 2, 1, 3)
        .reshape(3, RANK, lanes * 128)
    )
    count = sequences * n_z * sizes["y"]
    bound = clipping_limit[0]
    wide = total[:, :, :local_width]
    inner = total[:, :, local_width : local_width + hidden]
    return (
        (wide + bound * width_noise_draw) / count,
        (inner + bound * hidden_noise_draw) / count,
    )


def solution(mesh):
    names = ("z", "y", "x", "c")
    extents = (16, 4, 4, 2)
    fine = Mesh(mesh.devices.reshape(extents), names)
    dp, tensor = ("z", "y"), ("x", "c")
    placed = (
        P(dp, tensor),
        P(dp, tensor),
        P(dp, tensor),
        P(dp, tensor),
        P(tensor, dp),
        P(),
        P(None, None, tensor),
        P(),
        P(None, None, tensor),
        P(None, None, tensor),
    )
    return jax.shard_map(
        functools.partial(per_device, dict(zip(names, extents, strict=True))),
        mesh=fine,
        in_specs=placed,
        out_specs=(P(None, None, tensor), P(None, None, tensor)),
        check_vma=False,
    )
```

```python
import functools

import jax
import jax.numpy as jnp
from jax import lax
from jax.experimental import pallas as pl
from jax.experimental.pallas import tpu as pltpu
from jax.sharding import Mesh
from jax.sharding import PartitionSpec as P

SEQUENCE_TOKENS = 128
RANK = 16
SCALE = 2.0
F32 = jnp.float32
BF16 = jnp.bfloat16


def contract(left, right, left_dim, right_dim):
    return lax.dot_general(
        left, right, (((left_dim,), (right_dim,)), ((), ())), preferred_element_type=F32
    )


def column_tiles(hidden, step, tile):
    whole = hidden // step

    def body(i, carry):
        tile(pl.multiple_of(i * step, step), step)
        return carry

    lax.fori_loop(0, whole, body, 0)
    if hidden > whole * step:
        tile(whole * step, hidden - whole * step)


def gram_of(rows_ref, out_ref):
    for e in range(out_ref.shape[0]):
        rows = rows_ref[e * SEQUENCE_TOKENS : (e + 1) * SEQUENCE_TOKENS, :]
        out_ref[e] = contract(rows, rows, 1, 1)


def gather_kernel(rows_ref, factors_ref, projected_ref, gram_ref):
    projected_ref[...] = contract(factors_ref[...], rows_ref[...], 1, 1).astype(BF16)
    gram_of(rows_ref, gram_ref)


def hidden_kernel(plan, n_blocks, spot_ref, gradient_ref, *refs):
    block_refs = refs[:n_blocks]
    (gate_ref, up_ref, factors_ref, in_ref, lora_ref, lora_t_ref) = refs[
        n_blocks : n_blocks + 6
    ]
    sums_ref, mids_ref, weight, gradient, total, sems = refs[n_blocks + 6 :]
    tokens, hidden = gate_ref.shape
    sequences = tokens // SEQUENCE_TOKENS
    z, y, core = spot_ref[0], spot_ref[1], spot_ref[2]
    n_z, n_y, piece = plan["n_z"], plan["n_y"], plan["piece"]
    mids_ref[...] = jnp.zeros_like(mids_ref)

    def fetch(pieces):
        copies = [pltpu.make_async_copy(gradient_ref, gradient, sems.at[0])]
        for i, (block, row, off_z, off_y) in enumerate(pieces):
            to = lax.rem(z + (off_z + n_z), n_z) * n_y + lax.rem(y + (off_y + n_y), n_y)
            to = pl.multiple_of(to * piece, piece)
            copies.append(
                pltpu.make_async_copy(
                    block_refs[block].at[pl.ds(row, piece), :],
                    weight.at[pl.ds(to, piece), :],
                    sems.at[i + 1],
                )
            )
        for copy in copies:
            copy.start()
        for copy in copies:
            copy.wait()

    for c in range(2):
        pl.when(core == c)(functools.partial(fetch, plan["pieces"][c]))

    def tile(start, width):
        cols = pl.ds(start, width)
        factors = factors_ref[:, cols]
        total[:, :width] = jnp.dot(
            gradient[...], weight[:, cols], preferred_element_type=F32
        ) + SCALE * jnp.dot(lora_ref[...], factors[2 * RANK :], preferred_element_type=F32)
        for e in range(sequences):
            rows = slice(e * SEQUENCE_TOKENS, (e + 1) * SEQUENCE_TOKENS)
            hidden_grad = total[rows, :width]
            gate = gate_ref[rows, cols].astype(F32)
            up = up_ref[rows, cols].astype(F32)
            sigmoid = jax.nn.sigmoid(gate)
            silu = gate * sigmoid
            slope = sigmoid * (1.0 + gate * (1.0 - sigmoid))
            activation = (silu * up).astype(BF16)
            gate_grad = (hidden_grad * up * slope).astype(BF16)
            up_grad = (hidden_grad * silu).astype(BF16)
            left = (in_ref[:RANK, rows], in_ref[RANK:, rows], lora_t_ref[:, rows])
            for j, right in enumerate((gate_grad, up_grad, activation)):
                part = slice(j * RANK, (j + 1) * RANK)
                sums_ref[e, part, cols] = SCALE * jnp.dot(
                    left[j], right, preferred_element_type=F32
                )
                mids_ref[part, rows] += contract(factors[part], right, 1, 1)

    column_tiles(hidden, 256, tile)
    for e in range(sequences):
        square = sums_ref[e] * sums_ref[e]
        line = jnp.sum(jnp.sum(square, axis=0, keepdims=True), axis=1, keepdims=True)
        mids_ref[3 * RANK + e : 3 * RANK + e + 1, :] = jnp.broadcast_to(line, (1, tokens))


def quadratic(left, gram):
    product = jnp.zeros((left.shape[0], gram.shape[1]), F32)
    rest = gram
    for _ in range(3):
        part = rest.astype(BF16)
        product = product + jnp.dot(left, part, preferred_element_type=F32)
        rest = rest - part.astype(F32)
    return product * left.astype(F32)


def total_of(values):
    return jnp.sum(jnp.sum(values, axis=0, keepdims=True), axis=1, keepdims=True)


def clip_kernel(
    clip_ref,
    mids_ref,
    sums_ref,
    normed_ref,
    gradient_ref,
    normed_gram_ref,
    gradient_gram_ref,
    out_ref,
    wide,
):
    sequences, _, hidden = sums_ref.shape
    local = wide.shape[1]
    bound = clip_ref[0]
    weights = []
    for e in range(sequences):
        rows = slice(e * SEQUENCE_TOKENS, (e + 1) * SEQUENCE_TOKENS)
        mids = mids_ref[: 3 * RANK, rows].astype(BF16)
        square = total_of(quadratic(mids[: 2 * RANK], normed_gram_ref[e])) + total_of(
            quadratic(mids[2 * RANK :], gradient_gram_ref[e])
        )
        square = SCALE * SCALE * jnp.maximum(square, 0.0)
        square = square + mids_ref[3 * RANK + e : 3 * RANK + e + 1, 0:1]
        weight = bound / jnp.maximum(jnp.sqrt(square), bound)
        weights.append(weight)
        first = weight * (
            SCALE * jnp.dot(mids[: 2 * RANK], normed_ref[rows, :], preferred_element_type=F32)
        )
        second = weight * (
            SCALE * jnp.dot(mids[2 * RANK :], gradient_ref[rows, :], preferred_element_type=F32)
        )
        if e == 0:
            wide[: 2 * RANK] = first
            wide[2 * RANK :] = second
        else:
            wide[: 2 * RANK] += first
            wide[2 * RANK :] += second
    lanes = out_ref.shape[0] // 6
    for t in range(out_ref.shape[0]):
        r, c = divmod(t, lanes)
        rows = slice(8 * r, 8 * r + 8)
        at = c * 128
        if at < local:
            value = wide[rows, at : at + 128]
        elif at < local + hidden:
            at = at - local
            value = weights[0] * sums_ref[0, rows, at : at + 128]
            for e in range(1, sequences):
                value = value + weights[e] * sums_ref[e, rows, at : at + 128]
        else:
            value = jnp.zeros((8, 128), F32)
        out_ref[t] = value


def core_ring(size, by, core):
    return [(2 * i + core, 2 * ((i + by) % size) + core) for i in range(size)]


def gather_weight(shard, n_z, n_y):
    piece = shard.shape[0]

    def along_z(block, by, core):
        return lax.ppermute(block, ("z", "c"), core_ring(n_z, by, core))

    def along_y(block, by, core):
        return lax.ppermute(block, ("y", "c"), core_ring(n_y, by, core))

    last = n_z // 2
    blocks, pieces = [], ([], [])

    def keep(block, core, places):
        for row, (off_z, off_y) in enumerate(places):
            pieces[core].append((len(blocks), row * piece, off_z, off_y))
        blocks.append(block)

    around = [0, -1, 1, 2]
    column = jnp.concatenate(
        [shard, along_y(shard, 1, 0), along_y(shard, -1, 0), along_y(shard, 2, 0)], axis=0
    )
    keep(column, 0, [(0, off) for off in around])
    low0 = high0 = column
    low1 = high1 = shard
    singles, places = [shard], [0]
    half = 2 * piece

    def exchange(group, offs):
        batch = jnp.concatenate(group, axis=0)
        before, after = along_y(batch, 1, 1), along_y(batch, -1, 1)
        return batch, before, after, offs

    def forward(batch, before, after, offs):
        middle = len(offs) // 2
        opposite = (
            along_y(before[: middle * piece], 1, 1),
            along_y(after[middle * piece :], -1, 1),
        )
        keep(batch, 1, [(off, 0) for off in offs])
        keep(before, 1, [(off, -1) for off in offs])
        keep(after, 1, [(off, 1) for off in offs])
        keep(opposite[0], 1, [(off, 2) for off in offs[:middle]])
        keep(opposite[1], 1, [(off, 2) for off in offs[middle:]])

    open_batches = []
    for k in range(1, last + 1):
        if k == last - 1:
            batch, before, after, offs = open_batches.pop()
            before, after, low1, high1 = lax.optimization_barrier((before, after, low1, high1))
            forward(batch, before, after, offs)
        low1 = along_z(low1, 1, 1)
        singles, places = singles + [low1], places + [-k]
        if k < last:
            high1 = along_z(high1, -1, 1)
            singles, places = singles + [high1], places + [k]
        if len(singles) >= last:
            open_batches.append(exchange(singles[:last], places[:last]))
            singles, places = singles[last:], places[last:]
        if k < last:
            low0, high0 = along_z(low0, 1, 0), along_z(high0, -1, 0)
            keep(low0, 0, [(-k, off) for off in around])
            keep(high0, 0, [(k, off) for off in around])
        else:
            keep(along_z(low0[:half], 1, 0), 0, [(last, off) for off in around[:2]])
            keep(along_z(high0[half:], -1, 0), 0, [(last, off) for off in around[2:]])
    assert not singles
    forward(*open_batches.pop())
    return blocks, pieces


def per_device(
    sizes,
    normed,
    output_gradient,
    gate_preactivation,
    upward_preactivation,
    frozen_down_weight,
    adapter_width_factors,
    adapter_hidden_factors,
    clipping_limit,
    width_noise_draw,
    hidden_noise_draw,
):
    tokens, local_width = normed.shape
    hidden = gate_preactivation.shape[1]
    sequences = tokens // SEQUENCE_TOKENS
    n_z = sizes["z"]
    n_tensor = sizes["x"] * sizes["c"]
    z_axes, tensor_axes = "z", ("x", "c")
    z = lax.axis_index(z_axes)

    gradient = lax.all_gather(output_gradient, tensor_axes, axis=1, tiled=True)
    normed_all = lax.all_gather(normed, tensor_axes, axis=1, tiled=True)
    shard = frozen_down_weight.T
    blocks, pieces = gather_weight(shard, n_z, sizes["y"])

    vmem = pl.BlockSpec(memory_space=pltpu.VMEM)
    smem = pl.BlockSpec(memory_space=pltpu.SMEM)
    hbm = pl.BlockSpec(memory_space=pltpu.HBM)
    params = pltpu.CompilerParams(vmem_limit_bytes=32 * 2**20)

    def project(rows, factors, name):
        return pl.pallas_call(
            gather_kernel,
            out_shape=(
                jax.ShapeDtypeStruct((factors.shape[0], tokens), BF16),
                jax.ShapeDtypeStruct((sequences, SEQUENCE_TOKENS, SEQUENCE_TOKENS), F32),
            ),
            in_specs=[vmem, vmem],
            out_specs=(vmem, vmem),
            compiler_params=params,
            cost_estimate=pl.CostEstimate(
                flops=2 * tokens * rows.shape[1] * (128 + factors.shape[0]),
                bytes_accessed=5 * 2**20,
                transcendentals=0,
            ),
            name=name,
        )(rows, factors)

    late = [i for i, _, off_z, _ in pieces[0] if off_z == n_z // 2 - 2][0]
    gradient, blocks[late] = lax.optimization_barrier((gradient, blocks[late]))
    lora_t, gradient_gram = project(gradient, adapter_width_factors[2], "gradient_side")
    in_t, normed_gram = project(
        normed_all, adapter_width_factors[:2].reshape(2 * RANK, -1), "normed_side"
    )

    n_copies = 1 + max(len(p) for p in pieces)
    plan = dict(n_z=n_z, n_y=sizes["y"], piece=shard.shape[0], pieces=pieces)
    sums, mids = pl.pallas_call(
        functools.partial(hidden_kernel, plan, len(blocks)),
        out_shape=(
            jax.ShapeDtypeStruct((sequences, 3 * RANK, hidden), F32),
            jax.ShapeDtypeStruct((8 * n_tensor, tokens), F32),
        ),
        in_specs=[smem, hbm] + [hbm] * len(blocks) + [vmem] * 6,
        out_specs=(vmem, vmem),
        scratch_shapes=[
            pltpu.VMEM((gradient.shape[1], hidden), BF16),
            pltpu.VMEM(gradient.shape, BF16),
            pltpu.VMEM((tokens, 256), F32),
            pltpu.SemaphoreType.DMA((n_copies,)),
        ],
        compiler_params=params,
        name="hidden_side",
    )(
        jnp.stack([z, lax.axis_index("y"), lax.axis_index("c")]).astype(jnp.int32),
        gradient,
        *blocks,
        gate_preactivation,
        upward_preactivation,
        adapter_hidden_factors.reshape(3 * RANK, hidden),
        in_t,
        lora_t.T,
        lora_t,
    )

    shares = lax.all_to_all(mids.reshape(n_tensor, 8, tokens), tensor_axes, 0, 0)
    share = jnp.sum(shares, axis=0)
    mids = lax.all_to_all(
        jnp.broadcast_to(share, (n_tensor,) + share.shape), tensor_axes, 0, 0
    ).reshape(8 * n_tensor, tokens)

    lanes = 12
    out = pl.pallas_call(
        clip_kernel,
        out_shape=jax.ShapeDtypeStruct((6 * lanes, 8, 128), F32),
        in_specs=[smem] + [vmem] * 6,
        out_specs=vmem,
        scratch_shapes=[pltpu.VMEM((3 * RANK, local_width), F32)],
        compiler_params=params,
        name="clip_side",
    )(
        clipping_limit,
        mids,
        sums,
        normed,
        output_gradient,
        normed_gram,
        gradient_gram,
    )

    n_y = sizes["y"]
    part = jnp.sum(lax.all_to_all(out.reshape(n_y, -1, 128), "y", 0, 0), axis=0)
    part = jnp.sum(lax.all_to_all(part.reshape(n_z, -1, 128), z_axes, 0, 0), axis=0)
    part = lax.all_to_all(
        jnp.broadcast_to(part, (n_z,) + part.shape), z_axes, 0, 0
    ).reshape(-1, 128)
    part = lax.all_gather(part, "y", axis=0)
    total = (
        part.reshape(6, lanes, 8, 128)
        .transpose(0, 2, 1, 3)
        .reshape(3, RANK, lanes * 128)
    )
    count = sequences * n_z * sizes["y"]
    bound = clipping_limit[0]
    wide = total[:, :, :local_width]
    inner = total[:, :, local_width : local_width + hidden]
    return (
        (wide + bound * width_noise_draw) / count,
        (inner + bound * hidden_noise_draw) / count,
    )


def solution(mesh):
    names = ("z", "y", "x", "c")
    extents = (16, 4, 4, 2)
    fine = Mesh(mesh.devices.reshape(extents), names)
    dp, tensor = ("z", "y"), ("x", "c")
    placed = (
        P(dp, tensor),
        P(dp, tensor),
        P(dp, tensor),
        P(dp, tensor),
        P(tensor, dp),
        P(),
        P(None, None, tensor),
        P(),
        P(None, None, tensor),
        P(None, None, tensor),
    )
    return jax.shard_map(
        functools.partial(per_device, dict(zip(names, extents, strict=True))),
        mesh=fine,
        in_specs=placed,
        out_specs=(P(None, None, tensor), P(None, None, tensor)),
        check_vma=False,
    )
```

```python
import functools

import jax
import jax.numpy as jnp
from jax import lax
from jax.experimental import pallas as pl
from jax.experimental.pallas import tpu as pltpu
from jax.sharding import Mesh
from jax.sharding import PartitionSpec as P

SEQUENCE_TOKENS = 128
RANK = 16
SCALE = 2.0
F32 = jnp.float32
BF16 = jnp.bfloat16


def contract(left, right, left_dim, right_dim):
    return lax.dot_general(
        left, right, (((left_dim,), (right_dim,)), ((), ())), preferred_element_type=F32
    )


def column_tiles(hidden, step, tile):
    whole = hidden // step

    def body(i, carry):
        tile(pl.multiple_of(i * step, step), step)
        return carry

    lax.fori_loop(0, whole, body, 0)
    if hidden > whole * step:
        tile(whole * step, hidden - whole * step)


def fetch_blocks(place_ref, gradient_ref, block_refs, left, right, sems):
    copies, row = [], 0
    for i, block in enumerate(block_refs):
        rows = block.shape[0]
        at = pl.ds(pl.multiple_of(place_ref[i] * 128, 128), rows)
        copies.append(
            pltpu.make_async_copy(
                gradient_ref.at[:, at], left.at[:, pl.ds(row, rows)], sems.at[2 * i]
            )
        )
        copies.append(
            pltpu.make_async_copy(block, right.at[pl.ds(row, rows), :], sems.at[2 * i + 1])
        )
        row += rows
    for copy in copies:
        copy.start()
    return copies


def side_kernel(rows_ref, factors_ref, projected_ref, gram_ref, total):
    step = pl.program_id(0)

    @pl.when(step == 0)
    def _():
        total[...] = jnp.zeros_like(total)
        gram_ref[...] = jnp.zeros_like(gram_ref)

    total[...] += contract(factors_ref[...], rows_ref[...], 1, 1)
    for e in range(gram_ref.shape[0]):
        rows = rows_ref[e * SEQUENCE_TOKENS : (e + 1) * SEQUENCE_TOKENS, :]
        gram_ref[e] += contract(rows, rows, 1, 1)

    @pl.when(step == pl.num_programs(0) - 1)
    def _():
        projected_ref[...] = total[...].astype(BF16)


def part_kernel(n_blocks, first, place_ref, gradient_ref, *refs):
    block_refs = refs[:n_blocks]
    if first:
        total_ref, left, right, sems = refs[n_blocks:]
    else:
        before_ref, total_ref, left, right, sems = refs[n_blocks:]
    for copy in fetch_blocks(place_ref, gradient_ref, block_refs, left, right, sems):
        copy.wait()

    def tile(start, width):
        cols = pl.ds(start, width)
        product = jnp.dot(left[...], right[:, cols], preferred_element_type=F32)
        if first:
            total_ref[:, cols] = product
        else:
            total_ref[:, cols] = before_ref[:, cols] + product

    column_tiles(total_ref.shape[1], 256, tile)


def hidden_kernel(n_blocks, place_ref, gradient_ref, *refs):
    block_refs = refs[:n_blocks]
    (before_ref, gate_ref, up_ref, factors_ref, in_ref, lora_ref, lora_t_ref) = refs[
        n_blocks : n_blocks + 7
    ]
    sums_ref, mids_ref, total, left_rows, right_rows, sems = refs[n_blocks + 7 :]
    tokens, hidden = gate_ref.shape
    sequences = tokens // SEQUENCE_TOKENS
    copies = fetch_blocks(place_ref, gradient_ref, block_refs, left_rows, right_rows, sems)
    mids_ref[...] = jnp.zeros_like(mids_ref)
    for copy in copies:
        copy.wait()

    def tile(start, width):
        cols = pl.ds(start, width)
        factors = factors_ref[:, cols]
        total[:, :width] = (
            before_ref[:, cols]
            + jnp.dot(left_rows[...], right_rows[:, cols], preferred_element_type=F32)
            + SCALE * jnp.dot(lora_ref[...], factors[2 * RANK :], preferred_element_type=F32)
        )
        for e in range(sequences):
            rows = slice(e * SEQUENCE_TOKENS, (e + 1) * SEQUENCE_TOKENS)
            hidden_grad = total[rows, :width]
            gate = gate_ref[rows, cols].astype(F32)
            up = up_ref[rows, cols].astype(F32)
            sigmoid = jax.nn.sigmoid(gate)
            silu = gate * sigmoid
            slope = sigmoid * (1.0 + gate * (1.0 - sigmoid))
            activation = (silu * up).astype(BF16)
            gate_grad = (hidden_grad * up * slope).astype(BF16)
            up_grad = (hidden_grad * silu).astype(BF16)
            left = (in_ref[:RANK, rows], in_ref[RANK:, rows], lora_t_ref[:, rows])
            for j, right in enumerate((gate_grad, up_grad, activation)):
                part = slice(j * RANK, (j + 1) * RANK)
                sums_ref[e, part, cols] = SCALE * jnp.dot(
                    left[j], right, preferred_element_type=F32
                )
                mids_ref[part, rows] += contract(factors[part], right, 1, 1)

    column_tiles(hidden, 256, tile)
    for e in range(sequences):
        square = sums_ref[e] * sums_ref[e]
        line = jnp.sum(jnp.sum(square, axis=0, keepdims=True), axis=1, keepdims=True)
        mids_ref[3 * RANK + e : 3 * RANK + e + 1, :] = jnp.broadcast_to(line, (1, tokens))


def quadratic(left, gram):
    product = jnp.zeros((left.shape[0], gram.shape[1]), F32)
    rest = gram
    for _ in range(3):
        part = rest.astype(BF16)
        product = product + jnp.dot(left, part, preferred_element_type=F32)
        rest = rest - part.astype(F32)
    return product * left.astype(F32)


def total_of(values):
    return jnp.sum(jnp.sum(values, axis=0, keepdims=True), axis=1, keepdims=True)


def clip_kernel(
    clip_ref,
    mids_ref,
    sums_ref,
    normed_ref,
    gradient_ref,
    normed_gram_ref,
    gradient_gram_ref,
    out_ref,
    wide,
):
    sequences, _, hidden = sums_ref.shape
    local = wide.shape[1]
    bound = clip_ref[0]
    weights = []
    for e in range(sequences):
        rows = slice(e * SEQUENCE_TOKENS, (e + 1) * SEQUENCE_TOKENS)
        mids = mids_ref[: 3 * RANK, rows].astype(BF16)
        square = total_of(quadratic(mids[: 2 * RANK], normed_gram_ref[e])) + total_of(
            quadratic(mids[2 * RANK :], gradient_gram_ref[e])
        )
        square = SCALE * SCALE * jnp.maximum(square, 0.0)
        square = square + mids_ref[3 * RANK + e : 3 * RANK + e + 1, 0:1]
        weight = bound / jnp.maximum(jnp.sqrt(square), bound)
        weights.append(weight)
        first = weight * (
            SCALE * jnp.dot(mids[: 2 * RANK], normed_ref[rows, :], preferred_element_type=F32)
        )
        second = weight * (
            SCALE * jnp.dot(mids[2 * RANK :], gradient_ref[rows, :], preferred_element_type=F32)
        )
        if e == 0:
            wide[: 2 * RANK] = first
            wide[2 * RANK :] = second
        else:
            wide[: 2 * RANK] += first
            wide[2 * RANK :] += second
    lanes = (local + hidden) // 128
    for t in range(out_ref.shape[0]):
        r, c = divmod(t, lanes)
        rows = slice(8 * r, 8 * r + 8)
        at = c * 128
        if r >= 3 * RANK // 8:
            value = jnp.zeros((8, 128), F32)
        elif at < local:
            value = wide[rows, at : at + 128]
        else:
            at = at - local
            value = weights[0] * sums_ref[0, rows, at : at + 128]
            for e in range(1, sequences):
                value = value + weights[e] * sums_ref[e, rows, at : at + 128]
        out_ref[t] = value


def ring(size, by):
    return [(i, (i + by) % size) for i in range(size)]


def per_device(
    sizes,
    normed,
    output_gradient,
    gate_preactivation,
    upward_preactivation,
    frozen_down_weight,
    adapter_width_factors,
    adapter_hidden_factors,
    clipping_limit,
    width_noise_draw,
    hidden_noise_draw,
):
    tokens, local_width = normed.shape
    hidden = gate_preactivation.shape[1]
    sequences = tokens // SEQUENCE_TOKENS
    n_z = sizes["z"]
    n_tensor = sizes["x"] * sizes["c"]
    z_axes, tensor_axes = "z", ("x", "c")
    z = lax.axis_index(z_axes)

    gradient = lax.all_gather(output_gradient, tensor_axes, axis=1, tiled=True)
    block = lax.all_gather(frozen_down_weight.T, "y", axis=0, tiled=True)
    normed_all = lax.all_gather(normed, tensor_axes, axis=1, tiled=True)

    rows = block.shape[0]
    half = rows // 2
    units = rows // 128
    vmem = pl.BlockSpec(memory_space=pltpu.VMEM)
    smem = pl.BlockSpec(memory_space=pltpu.SMEM)
    hbm = pl.BlockSpec(memory_space=pl.ANY)
    params = pltpu.CompilerParams(vmem_limit_bytes=60 * 2**20)

    def place(offsets):
        at = [((z + offset) % n_z) * units for offset in offsets]
        return jnp.stack(at).astype(jnp.int32)

    low, high = {0: block}, {0: block}

    def step(k, low_from, high_from):
        low[k] = lax.ppermute(low_from, z_axes, ring(n_z, 1))
        high[k] = lax.ppermute(high_from, z_axes, ring(n_z, -1))

    def side(values, factors, name):
        width = values.shape[1]
        chunk = 1024
        return pl.pallas_call(
            side_kernel,
            out_shape=(
                jax.ShapeDtypeStruct((factors.shape[0], tokens), BF16),
                jax.ShapeDtypeStruct((sequences, SEQUENCE_TOKENS, SEQUENCE_TOKENS), F32),
            ),
            grid=(width // chunk,),
            in_specs=[
                pl.BlockSpec((tokens, chunk), lambda i: (0, i)),
                pl.BlockSpec((factors.shape[0], chunk), lambda i: (0, i)),
            ],
            out_specs=(
                pl.BlockSpec((factors.shape[0], tokens), lambda i: (0, 0)),
                pl.BlockSpec((sequences, SEQUENCE_TOKENS, SEQUENCE_TOKENS), lambda i: (0, 0, 0)),
            ),
            scratch_shapes=[pltpu.VMEM((factors.shape[0], tokens), F32)],
            compiler_params=params,
            cost_estimate=pl.CostEstimate(
                flops=2 * tokens * width * (128 + factors.shape[0]),
                bytes_accessed=5 * 2**20,
                transcendentals=0,
            ),
            name=name,
        )(values, factors)

    def scratch(n_rows, n_blocks):
        return [
            pltpu.VMEM((tokens, n_rows), BF16),
            pltpu.VMEM((n_rows, hidden), BF16),
            pltpu.SemaphoreType.DMA((2 * n_blocks,)),
        ]

    def part(offsets, before=None):
        blocks = [(low if offset < 0 else high)[abs(offset)] for offset in offsets]
        n = len(blocks)
        given = [] if before is None else [before]
        return pl.pallas_call(
            functools.partial(part_kernel, n, before is None),
            out_shape=jax.ShapeDtypeStruct((tokens, hidden), F32),
            in_specs=[smem] + [hbm] * (n + 1) + [vmem] * len(given),
            out_specs=vmem,
            scratch_shapes=scratch(n * rows, n),
            compiler_params=params,
            cost_estimate=pl.CostEstimate(
                flops=2 * tokens * n * rows * hidden,
                bytes_accessed=6 * 2**20,
                transcendentals=0,
            ),
            name="part_product",
        )(place(offsets), gradient, *blocks, *given)

    def pairs(first, end):
        return [sign * k for k in range(first, end) for sign in (-1, 1)]

    last = n_z // 2
    for k in range(1, last - 2):
        step(k, low[k - 1], high[k - 1])
    total = part([0] + pairs(1, last - 5))
    at = last - 3
    low_in, high_in, total = lax.optimization_barrier((low[at], high[at], total))
    step(last - 2, low_in, high_in)
    total = part(pairs(last - 5, last - 3), total)
    lora_t, gradient_gram = side(gradient, adapter_width_factors[2], "gradient_side")
    at = last - 2
    low_in, high_in, total, lora_t = lax.optimization_barrier(
        (low[at], high[at], total, lora_t)
    )
    step(last - 1, low_in, high_in)
    total = part(pairs(last - 3, last - 1), total)
    at = last - 1
    low_in, high_in, total = lax.optimization_barrier((low[at], high[at], total))
    step(last, low_in[:half], high_in[half:])
    in_t, normed_gram = side(
        normed_all, adapter_width_factors[:2].reshape(2 * RANK, -1), "normed_side"
    )
    far = ((z + last) % n_z) * units
    blocks = [low[last - 1], high[last - 1], low[last], high[last]]
    places = jnp.concatenate(
        [place(pairs(last - 1, last)), jnp.stack([far, far + units // 2]).astype(jnp.int32)]
    )
    sums, mids = pl.pallas_call(
        functools.partial(hidden_kernel, len(blocks)),
        out_shape=(
            jax.ShapeDtypeStruct((sequences, 3 * RANK, hidden), F32),
            jax.ShapeDtypeStruct((8 * n_tensor, tokens), F32),
        ),
        in_specs=[smem] + [hbm] * (len(blocks) + 1) + [vmem] * 7,
        out_specs=(vmem, vmem),
        scratch_shapes=[pltpu.VMEM((tokens, 256), F32)] + scratch(3 * rows, len(blocks)),
        compiler_params=params,
        name="hidden_side",
    )(
        places,
        gradient,
        *blocks,
        total,
        gate_preactivation,
        upward_preactivation,
        adapter_hidden_factors.reshape(3 * RANK, hidden),
        in_t,
        lora_t.T,
        lora_t,
    )

    pieces = lax.all_to_all(mids.reshape(n_tensor, 8, tokens), tensor_axes, 0, 0)
    piece = jnp.sum(pieces, axis=0)
    mids = lax.all_to_all(
        jnp.broadcast_to(piece, (n_tensor,) + piece.shape), tensor_axes, 0, 0
    ).reshape(8 * n_tensor, tokens)

    lanes = (local_width + hidden) // 128
    tiles = 6 * lanes
    padded = -(-tiles // n_z) * n_z
    out = pl.pallas_call(
        clip_kernel,
        out_shape=jax.ShapeDtypeStruct((padded, 8, 128), F32),
        in_specs=[smem] + [vmem] * 6,
        out_specs=vmem,
        scratch_shapes=[pltpu.VMEM((3 * RANK, local_width), F32)],
        compiler_params=params,
        name="clip_side",
    )(
        clipping_limit,
        mids,
        sums,
        normed,
        output_gradient,
        normed_gram,
        gradient_gram,
    )

    part_sum = jnp.sum(lax.all_to_all(out.reshape(n_z, -1, 128), z_axes, 0, 0), axis=0)
    part_sum = jnp.sum(lax.all_gather(part_sum, "y", axis=0), axis=0)
    whole = lax.all_to_all(
        jnp.broadcast_to(part_sum, (n_z,) + part_sum.shape), z_axes, 0, 0
    )
    total = (
        whole.reshape(padded, 8, 128)[:tiles]
        .reshape(6, lanes, 8, 128)
        .transpose(0, 2, 1, 3)
        .reshape(3, RANK, lanes * 128)
    )
    count = sequences * n_z * sizes["y"]
    bound = clipping_limit[0]
    wide = total[:, :, :local_width]
    inner = total[:, :, local_width : local_width + hidden]
    return (
        (wide + bound * width_noise_draw) / count,
        (inner + bound * hidden_noise_draw) / count,
    )


def solution(mesh):
    names = ("z", "y", "x", "c")
    extents = (16, 4, 4, 2)
    fine = Mesh(mesh.devices.reshape(extents), names)
    dp, tensor = ("z", "y"), ("x", "c")
    placed = (
        P(dp, tensor),
        P(dp, tensor),
        P(dp, tensor),
        P(dp, tensor),
        P(tensor, dp),
        P(),
        P(None, None, tensor),
        P(),
        P(None, None, tensor),
        P(None, None, tensor),
    )
    return jax.shard_map(
        functools.partial(per_device, dict(zip(names, extents, strict=True))),
        mesh=fine,
        in_specs=placed,
        out_specs=(P(None, None, tensor), P(None, None, tensor)),
        check_vma=False,
    )
```

```python
import functools

import jax
import jax.numpy as jnp
from jax import lax
from jax.experimental import pallas as pl
from jax.experimental.pallas import tpu as pltpu
from jax.sharding import Mesh
from jax.sharding import PartitionSpec as P

SEQUENCE_TOKENS = 128
RANK = 16
SCALE = 2.0
F32 = jnp.float32
BF16 = jnp.bfloat16


def contract(left, right, left_dim, right_dim):
    return lax.dot_general(
        left, right, (((left_dim,), (right_dim,)), ((), ())), preferred_element_type=F32
    )


def column_tiles(hidden, step, tile):
    whole = hidden // step

    def body(i, carry):
        tile(i, pl.multiple_of(i * step, step), step)
        return carry

    lax.fori_loop(0, whole, body, 0)
    spans = [(i * step, step) for i in range(whole)]
    if hidden > whole * step:
        spans.append((whole * step, hidden - whole * step))
        tile(whole, *spans[-1])
    return spans


def copy_rows(source, target, sems, at, parts):
    rows = source.shape[0] // parts
    copies = []
    for i in range(parts):
        span = pl.ds(i * rows, rows)
        copies.append(
            pltpu.make_async_copy(source.at[span, :], target.at[span, :], sems.at[at + i])
        )
    return copies


def fetch_blocks(place_ref, gradient_ref, block_refs, left, right, sems):
    copies, row = [], 0
    for i, block in enumerate(block_refs):
        rows = block.shape[0]
        at = pl.ds(pl.multiple_of(place_ref[i] * 128, 128), rows)
        span = pl.ds(row, rows)
        copies += copy_rows(gradient_ref.at[:, at], left.at[:, span], sems, 4 * i, 2)
        copies += copy_rows(block, right.at[span, :], sems, 4 * i + 2, 2)
        row += rows
    return copies


def side_kernel(n_rows, *refs):
    row_refs = refs[:n_rows]
    factors_ref, projected_ref, gram_ref, total = refs[n_rows:]
    step = pl.program_id(0)

    @pl.when(step == 0)
    def _():
        total[...] = jnp.zeros_like(total)
        gram_ref[...] = jnp.zeros_like(gram_ref)

    for e, rows_ref in enumerate(row_refs):
        rows = rows_ref[...]
        span = slice(e * SEQUENCE_TOKENS, (e + 1) * SEQUENCE_TOKENS)
        total[:, span] += contract(factors_ref[...], rows, 1, 1)
        gram_ref[e] += contract(rows, rows, 1, 1)

    @pl.when(step == pl.num_programs(0) - 1)
    def _():
        projected_ref[...] = total[...].astype(BF16)


def part_kernel(n_blocks, first, place_ref, gradient_ref, *refs):
    block_refs = refs[:n_blocks]
    refs = refs[n_blocks:]
    if not first:
        before_ref, refs = refs[0], refs[1:]
    out_ref, total, left, right, sems, out_sems = refs
    copies = fetch_blocks(place_ref, gradient_ref, block_refs, left, right, sems)
    if not first:
        copies += copy_rows(before_ref, total, sems, 4 * n_blocks, 4)
    for copy in copies:
        copy.start()
    for copy in copies:
        copy.wait()

    def write(i, cols):
        return pltpu.make_async_copy(total.at[:, cols], out_ref.at[:, cols], out_sems.at[i])

    def tile(i, start, width):
        cols = pl.ds(start, width)
        product = jnp.dot(left[...], right[:, cols], preferred_element_type=F32)
        total[:, cols] = product if first else total[:, cols] + product
        write(i, cols).start()

    for i, (start, width) in enumerate(column_tiles(total.shape[1], 256, tile)):
        write(i, pl.ds(start, width)).wait()


def hidden_kernel(n_blocks, place_ref, gradient_ref, *refs):
    block_refs = refs[:n_blocks]
    (before_hbm, gate_hbm, up_hbm, factors_ref, in_ref, lora_ref, lora_t_ref) = refs[
        n_blocks : n_blocks + 7
    ]
    (sums_hbm, mids_ref, total, before_ref, gate_ref, up_ref, sums_ref, left_rows, right_rows) = (
        refs[n_blocks + 7 : -2]
    )
    sems, out_sems = refs[-2:]
    tokens, hidden = gate_ref.shape
    sequences = tokens // SEQUENCE_TOKENS
    copies = fetch_blocks(place_ref, gradient_ref, block_refs, left_rows, right_rows, sems)
    at = 4 * n_blocks
    for source, target in ((before_hbm, before_ref), (gate_hbm, gate_ref), (up_hbm, up_ref)):
        copies += copy_rows(source, target, sems, at, 4)
        at += 4
    for copy in copies:
        copy.start()
    mids_ref[...] = jnp.zeros_like(mids_ref)
    for copy in copies:
        copy.wait()

    def write(i, cols):
        return pltpu.make_async_copy(
            sums_ref.at[:, :, cols], sums_hbm.at[:, :, cols], out_sems.at[i]
        )

    def tile(i, start, width):
        cols = pl.ds(start, width)
        factors = factors_ref[:, cols]
        total[:, :width] = (
            before_ref[:, cols]
            + jnp.dot(left_rows[...], right_rows[:, cols], preferred_element_type=F32)
            + SCALE * jnp.dot(lora_ref[...], factors[2 * RANK :], preferred_element_type=F32)
        )
        for e in range(sequences):
            rows = slice(e * SEQUENCE_TOKENS, (e + 1) * SEQUENCE_TOKENS)
            hidden_grad = total[rows, :width]
            gate = gate_ref[rows, cols].astype(F32)
            up = up_ref[rows, cols].astype(F32)
            sigmoid = jax.nn.sigmoid(gate)
            silu = gate * sigmoid
            slope = sigmoid * (1.0 + gate * (1.0 - sigmoid))
            activation = (silu * up).astype(BF16)
            gate_grad = (hidden_grad * up * slope).astype(BF16)
            up_grad = (hidden_grad * silu).astype(BF16)
            left = (in_ref[:RANK, rows], in_ref[RANK:, rows], lora_t_ref[:, rows])
            for j, right in enumerate((gate_grad, up_grad, activation)):
                part = slice(j * RANK, (j + 1) * RANK)
                sums_ref[e, part, cols] = SCALE * jnp.dot(
                    left[j], right, preferred_element_type=F32
                )
                mids_ref[part, rows] += contract(factors[part], right, 1, 1)
        write(i, cols).start()

    spans = column_tiles(hidden, 256, tile)
    for e in range(sequences):
        square = sums_ref[e] * sums_ref[e]
        line = jnp.sum(jnp.sum(square, axis=0, keepdims=True), axis=1, keepdims=True)
        mids_ref[3 * RANK + e : 3 * RANK + e + 1, :] = jnp.broadcast_to(line, (1, tokens))
    for i, (start, width) in enumerate(spans):
        write(i, pl.ds(start, width)).wait()


def quadratic(left, gram):
    product = jnp.zeros((left.shape[0], gram.shape[1]), F32)
    rest = gram
    for _ in range(3):
        part = rest.astype(BF16)
        product = product + jnp.dot(left, part, preferred_element_type=F32)
        rest = rest - part.astype(F32)
    return product * left.astype(F32)


def total_of(values):
    return jnp.sum(jnp.sum(values, axis=0, keepdims=True), axis=1, keepdims=True)


def clip_kernel(
    clip_ref,
    mids_ref,
    sums_ref,
    normed_ref,
    gradient_ref,
    normed_gram_ref,
    gradient_gram_ref,
    out_ref,
    wide,
):
    sequences, _, hidden = sums_ref.shape
    local = wide.shape[1]
    bound = clip_ref[0]
    weights = []
    for e in range(sequences):
        rows = slice(e * SEQUENCE_TOKENS, (e + 1) * SEQUENCE_TOKENS)
        mids = mids_ref[: 3 * RANK, rows].astype(BF16)
        square = total_of(quadratic(mids[: 2 * RANK], normed_gram_ref[e])) + total_of(
            quadratic(mids[2 * RANK :], gradient_gram_ref[e])
        )
        square = SCALE * SCALE * jnp.maximum(square, 0.0)
        square = square + mids_ref[3 * RANK + e : 3 * RANK + e + 1, 0:1]
        weight = bound / jnp.maximum(jnp.sqrt(square), bound)
        weights.append(weight)
        first = weight * (
            SCALE * jnp.dot(mids[: 2 * RANK], normed_ref[rows, :], preferred_element_type=F32)
        )
        second = weight * (
            SCALE * jnp.dot(mids[2 * RANK :], gradient_ref[rows, :], preferred_element_type=F32)
        )
        if e == 0:
            wide[: 2 * RANK] = first
            wide[2 * RANK :] = second
        else:
            wide[: 2 * RANK] += first
            wide[2 * RANK :] += second
    lanes = (local + hidden) // 128
    for t in range(out_ref.shape[0]):
        r, c = divmod(t, lanes)
        rows = slice(8 * r, 8 * r + 8)
        at = c * 128
        if r >= 3 * RANK // 8:
            value = jnp.zeros((8, 128), F32)
        elif at < local:
            value = wide[rows, at : at + 128]
        else:
            at = at - local
            value = weights[0] * sums_ref[0, rows, at : at + 128]
            for e in range(1, sequences):
                value = value + weights[e] * sums_ref[e, rows, at : at + 128]
        out_ref[t] = value


def ring(size, by):
    return [(i, (i + by) % size) for i in range(size)]


def per_device(
    sizes,
    normed,
    output_gradient,
    gate_preactivation,
    upward_preactivation,
    frozen_down_weight,
    adapter_width_factors,
    adapter_hidden_factors,
    clipping_limit,
    width_noise_draw,
    hidden_noise_draw,
):
    tokens, local_width = normed.shape
    hidden = gate_preactivation.shape[1]
    sequences = tokens // SEQUENCE_TOKENS
    n_z = sizes["z"]
    n_tensor = sizes["x"] * sizes["c"]
    z_axes, tensor_axes = "z", ("x", "c")
    z = lax.axis_index(z_axes)

    gradient = lax.all_gather(output_gradient, tensor_axes, axis=1, tiled=True)
    block = lax.all_gather(frozen_down_weight.T, "y", axis=0, tiled=True)
    normed_all = lax.all_gather(normed, tensor_axes, axis=1, tiled=True)

    rows = block.shape[0]
    half = rows // 2
    units = rows // 128
    vmem = pl.BlockSpec(memory_space=pltpu.VMEM)
    smem = pl.BlockSpec(memory_space=pltpu.SMEM)
    hbm = pl.BlockSpec(memory_space=pl.ANY)
    params = pltpu.CompilerParams(vmem_limit_bytes=60 * 2**20)

    def place(offsets):
        at = [((z + offset) % n_z) * units for offset in offsets]
        return jnp.stack(at).astype(jnp.int32)

    low, high = {0: block}, {0: block}

    def step(k, low_from, high_from):
        low[k] = lax.ppermute(low_from, z_axes, ring(n_z, 1))
        high[k] = lax.ppermute(high_from, z_axes, ring(n_z, -1))

    def side(values, factors, name):
        width = values.shape[1]
        chunk = 1024
        return pl.pallas_call(
            functools.partial(side_kernel, sequences),
            out_shape=(
                jax.ShapeDtypeStruct((factors.shape[0], tokens), BF16),
                jax.ShapeDtypeStruct((sequences, SEQUENCE_TOKENS, SEQUENCE_TOKENS), F32),
            ),
            grid=(width // chunk,),
            in_specs=[
                pl.BlockSpec((SEQUENCE_TOKENS, chunk), functools.partial(lambda e, i: (e, i), e))
                for e in range(sequences)
            ]
            + [pl.BlockSpec((factors.shape[0], chunk), lambda i: (0, i))],
            out_specs=(
                pl.BlockSpec((factors.shape[0], tokens), lambda i: (0, 0)),
                pl.BlockSpec((sequences, SEQUENCE_TOKENS, SEQUENCE_TOKENS), lambda i: (0, 0, 0)),
            ),
            scratch_shapes=[pltpu.VMEM((factors.shape[0], tokens), F32)],
            compiler_params=params,
            cost_estimate=pl.CostEstimate(
                flops=2 * tokens * width * (128 + factors.shape[0]),
                bytes_accessed=5 * 2**20,
                transcendentals=0,
            ),
            name=name,
        )(*[values] * sequences, factors)

    def scratch(n_rows, n_sems):
        return [
            pltpu.VMEM((tokens, n_rows), BF16),
            pltpu.VMEM((n_rows, hidden), BF16),
            pltpu.SemaphoreType.DMA((n_sems,)),
            pltpu.SemaphoreType.DMA((-(-hidden // 256),)),
        ]

    def part(offsets, before=None):
        blocks = [(low if offset < 0 else high)[abs(offset)] for offset in offsets]
        n = len(blocks)
        given = [] if before is None else [before]
        return pl.pallas_call(
            functools.partial(part_kernel, n, before is None),
            out_shape=jax.ShapeDtypeStruct((tokens, hidden), F32),
            in_specs=[smem] + [hbm] * (n + 1 + len(given)),
            out_specs=hbm,
            scratch_shapes=[pltpu.VMEM((tokens, hidden), F32)] + scratch(n * rows, 4 * n + 4),
            compiler_params=params,
            cost_estimate=pl.CostEstimate(
                flops=2 * tokens * n * rows * hidden,
                bytes_accessed=6 * 2**20,
                transcendentals=0,
            ),
            name="part_product",
        )(place(offsets), gradient, *blocks, *given)

    def pairs(first, end):
        return [sign * k for k in range(first, end) for sign in (-1, 1)]

    last = n_z // 2
    for k in range(1, last - 2):
        step(k, low[k - 1], high[k - 1])
    total = part([0] + pairs(1, last - 5))
    at = last - 3
    high_in, total = lax.optimization_barrier((high[at], total))
    step(last - 2, low[at], high_in)
    total = part(pairs(last - 5, last - 3), total)
    lora_t, gradient_gram = side(gradient, adapter_width_factors[2], "gradient_side")
    at = last - 2
    high_in, total, lora_t = lax.optimization_barrier((high[at], total, lora_t))
    step(last - 1, low[at], high_in)
    total = part(pairs(last - 3, last - 1), total)
    at = last - 1
    high_in, total = lax.optimization_barrier((high[at], total))
    step(last, low[at][:half], high_in[half:])
    in_t, normed_gram = side(
        normed_all, adapter_width_factors[:2].reshape(2 * RANK, -1), "normed_side"
    )
    far = ((z + last) % n_z) * units
    blocks = [low[last - 1], high[last - 1], low[last], high[last]]
    places = jnp.concatenate(
        [place(pairs(last - 1, last)), jnp.stack([far, far + units // 2]).astype(jnp.int32)]
    )
    sums, mids = pl.pallas_call(
        functools.partial(hidden_kernel, len(blocks)),
        out_shape=(
            jax.ShapeDtypeStruct((sequences, 3 * RANK, hidden), F32),
            jax.ShapeDtypeStruct((8 * n_tensor, tokens), F32),
        ),
        in_specs=[smem] + [hbm] * (len(blocks) + 4) + [vmem] * 4,
        out_specs=(hbm, vmem),
        scratch_shapes=[
            pltpu.VMEM((tokens, 256), F32),
            pltpu.VMEM((tokens, hidden), F32),
            pltpu.VMEM((tokens, hidden), BF16),
            pltpu.VMEM((tokens, hidden), BF16),
            pltpu.VMEM((sequences, 3 * RANK, hidden), F32),
        ]
        + scratch(3 * rows, 4 * len(blocks) + 12),
        compiler_params=params,
        name="hidden_side",
    )(
        places,
        gradient,
        *blocks,
        total,
        gate_preactivation,
        upward_preactivation,
        adapter_hidden_factors.reshape(3 * RANK, hidden),
        in_t,
        lora_t.T,
        lora_t,
    )

    pieces = lax.all_to_all(mids.reshape(n_tensor, 8, tokens), tensor_axes, 0, 0)
    piece = jnp.sum(pieces, axis=0)
    mids = lax.all_to_all(
        jnp.broadcast_to(piece, (n_tensor,) + piece.shape), tensor_axes, 0, 0
    ).reshape(8 * n_tensor, tokens)

    lanes = (local_width + hidden) // 128
    tiles = 6 * lanes
    padded = -(-tiles // 8) * 8
    out = pl.pallas_call(
        clip_kernel,
        out_shape=jax.ShapeDtypeStruct((padded, 8, 128), F32),
        in_specs=[smem] + [vmem] * 6,
        out_specs=vmem,
        scratch_shapes=[pltpu.VMEM((3 * RANK, local_width), F32)],
        compiler_params=params,
        name="clip_side",
    )(
        clipping_limit,
        mids,
        sums,
        normed,
        output_gradient,
        normed_gram,
        gradient_gram,
    )

    n_y = sizes["y"]
    share = jnp.sum(lax.all_to_all(out.reshape(n_y, -1, 128), "y", 0, 0), axis=0)
    share = jnp.sum(lax.all_to_all(share.reshape(n_z, -1, 128), z_axes, 0, 0), axis=0)
    share = lax.all_to_all(
        jnp.broadcast_to(share, (n_z,) + share.shape), z_axes, 0, 0
    ).reshape(-1, 128)
    whole = lax.all_to_all(jnp.broadcast_to(share, (n_y,) + share.shape), "y", 0, 0)
    total = (
        whole.reshape(padded, 8, 128)[:tiles]
        .reshape(6, lanes, 8, 128)
        .transpose(0, 2, 1, 3)
        .reshape(3, RANK, lanes * 128)
    )
    count = sequences * n_z * sizes["y"]
    bound = clipping_limit[0]
    wide = total[:, :, :local_width]
    inner = total[:, :, local_width : local_width + hidden]
    return (
        (wide + bound * width_noise_draw) / count,
        (inner + bound * hidden_noise_draw) / count,
    )


def solution(mesh):
    names = ("z", "y", "x", "c")
    extents = (16, 4, 4, 2)
    fine = Mesh(mesh.devices.reshape(extents), names)
    dp, tensor = ("z", "y"), ("x", "c")
    placed = (
        P(dp, tensor),
        P(dp, tensor),
        P(dp, tensor),
        P(dp, tensor),
        P(tensor, dp),
        P(),
        P(None, None, tensor),
        P(),
        P(None, None, tensor),
        P(None, None, tensor),
    )
    return jax.shard_map(
        functools.partial(per_device, dict(zip(names, extents, strict=True))),
        mesh=fine,
        in_specs=placed,
        out_specs=(P(None, None, tensor), P(None, None, tensor)),
        check_vma=False,
    )
```

```python
import functools

import jax
import jax.numpy as jnp
from jax import lax
from jax.experimental import pallas as pl
from jax.experimental.pallas import tpu as pltpu
from jax.sharding import Mesh
from jax.sharding import PartitionSpec as P

SEQUENCE_TOKENS = 128
RANK = 16
SCALE = 2.0
F32 = jnp.float32
BF16 = jnp.bfloat16


def contract(left, right, left_dim, right_dim):
    return lax.dot_general(
        left, right, (((left_dim,), (right_dim,)), ((), ())), preferred_element_type=F32
    )


def column_tiles(hidden, step, tile):
    whole = hidden // step

    def body(i, carry):
        tile(i, pl.multiple_of(i * step, step), step)
        return carry

    lax.fori_loop(0, whole, body, 0)
    spans = [(i * step, step) for i in range(whole)]
    if hidden > whole * step:
        spans.append((whole * step, hidden - whole * step))
        tile(whole, *spans[-1])
    return spans


def copy_rows(source, target, sems, at, parts):
    rows = source.shape[0] // parts
    copies = []
    for i in range(parts):
        span = pl.ds(i * rows, rows)
        copies.append(
            pltpu.make_async_copy(source.at[span, :], target.at[span, :], sems.at[at + i])
        )
    return copies


def fetch_blocks(place_ref, gradient_ref, block_refs, left, right, sems):
    copies, row = [], 0
    for i, block in enumerate(block_refs):
        rows = block.shape[0]
        at = pl.ds(pl.multiple_of(place_ref[i] * 128, 128), rows)
        span = pl.ds(row, rows)
        copies += copy_rows(gradient_ref.at[:, at], left.at[:, span], sems, 4 * i, 2)
        copies += copy_rows(block, right.at[span, :], sems, 4 * i + 2, 2)
        row += rows
    return copies


def side_kernel(n_pairs, *refs):
    row_refs = refs[:n_pairs]
    factors_ref, projected_ref, gram_ref, total = refs[n_pairs:]
    step = pl.program_id(0)
    size = SEQUENCE_TOKENS

    @pl.when(step == 0)
    def _():
        total[...] = jnp.zeros_like(total)

    for p, rows_ref in enumerate(row_refs):
        rows = rows_ref[...]
        stacked = jnp.concatenate([rows, factors_ref[...]], axis=0)
        total[p] += contract(stacked, rows, 1, 1)

    @pl.when(step == pl.num_programs(0) - 1)
    def _():
        for p in range(n_pairs):
            gram_ref[2 * p] = total[p, :size, :size]
            gram_ref[2 * p + 1] = total[p, size : 2 * size, size:]
            projected_ref[:, 2 * size * p : 2 * size * (p + 1)] = total[p, 2 * size :].astype(BF16)


def part_kernel(n_blocks, first, place_ref, gradient_ref, *refs):
    block_refs = refs[:n_blocks]
    refs = refs[n_blocks:]
    if not first:
        before_ref, refs = refs[0], refs[1:]
    out_ref, total, left, right, sems, out_sems = refs
    copies = fetch_blocks(place_ref, gradient_ref, block_refs, left, right, sems)
    if not first:
        copies += copy_rows(before_ref, total, sems, 4 * n_blocks, 4)
    for copy in copies:
        copy.start()
    for copy in copies:
        copy.wait()

    writes = []
    hidden = total.shape[1]
    for i, start in enumerate(range(0, hidden, 512)):
        cols = slice(start, min(start + 512, hidden))
        product = jnp.dot(left[...], right[:, cols], preferred_element_type=F32)
        total[:, cols] = product if first else total[:, cols] + product
        write = pltpu.make_async_copy(total.at[:, cols], out_ref.at[:, cols], out_sems.at[i])
        write.start()
        writes.append(write)
    for write in writes:
        write.wait()


def hidden_kernel(n_blocks, place_ref, gradient_ref, *refs):
    block_refs = refs[:n_blocks]
    (before_hbm, gate_hbm, up_hbm, factors_ref, in_ref, lora_ref, lora_t_ref) = refs[
        n_blocks : n_blocks + 7
    ]
    (sums_hbm, mids_ref, total, before_ref, gate_ref, up_ref, sums_ref, left_rows, right_rows) = (
        refs[n_blocks + 7 : -2]
    )
    sems, out_sems = refs[-2:]
    tokens, hidden = gate_ref.shape
    sequences = tokens // SEQUENCE_TOKENS
    blocks = fetch_blocks(place_ref, gradient_ref, block_refs, left_rows, right_rows, sems)
    copies, at = [], 4 * n_blocks
    for source, target in ((before_hbm, before_ref), (gate_hbm, gate_ref), (up_hbm, up_ref)):
        copies += copy_rows(source, target, sems, at, 4)
        at += 4
    for copy in blocks + copies:
        copy.start()
    mids_ref[...] = jnp.zeros_like(mids_ref)
    for copy in blocks:
        copy.wait()
    total[...] = jnp.dot(left_rows[...], right_rows[...], preferred_element_type=F32)
    for copy in copies:
        copy.wait()

    def write(i, cols):
        return pltpu.make_async_copy(
            sums_ref.at[:, :, cols], sums_hbm.at[:, :, cols], out_sems.at[i]
        )

    def tile(i, start, width):
        cols = pl.ds(start, width)
        factors = factors_ref[:, cols]
        for e in range(sequences):
            rows = slice(e * SEQUENCE_TOKENS, (e + 1) * SEQUENCE_TOKENS)
            hidden_grad = (
                total[rows, cols]
                + before_ref[rows, cols]
                + SCALE
                * jnp.dot(lora_ref[rows, :], factors[2 * RANK :], preferred_element_type=F32)
            )
            gate = gate_ref[rows, cols].astype(F32)
            up = up_ref[rows, cols].astype(F32)
            sigmoid = jax.nn.sigmoid(gate)
            silu = gate * sigmoid
            slope = sigmoid * (1.0 + gate * (1.0 - sigmoid))
            activation = (silu * up).astype(BF16)
            gate_grad = (hidden_grad * up * slope).astype(BF16)
            up_grad = (hidden_grad * silu).astype(BF16)
            left = (in_ref[:RANK, rows], in_ref[RANK:, rows], lora_t_ref[:, rows])
            for j, right in enumerate((gate_grad, up_grad, activation)):
                part = slice(j * RANK, (j + 1) * RANK)
                sums_ref[e, part, cols] = SCALE * jnp.dot(
                    left[j], right, preferred_element_type=F32
                )
                mids_ref[part, rows] += contract(factors[part], right, 1, 1)
        write(i, cols).start()

    spans = column_tiles(hidden, 256, tile)
    for e in range(sequences):
        square = sums_ref[e] * sums_ref[e]
        line = jnp.sum(jnp.sum(square, axis=0, keepdims=True), axis=1, keepdims=True)
        mids_ref[3 * RANK + e : 3 * RANK + e + 1, :] = jnp.broadcast_to(line, (1, tokens))
    for i, (start, width) in enumerate(spans):
        write(i, pl.ds(start, width)).wait()


def quadratic(left, gram):
    product = jnp.zeros((left.shape[0], gram.shape[1]), F32)
    rest = gram
    for _ in range(3):
        part = rest.astype(BF16)
        product = product + jnp.dot(left, part, preferred_element_type=F32)
        rest = rest - part.astype(F32)
    return product * left.astype(F32)


def total_of(values):
    return jnp.sum(jnp.sum(values, axis=0, keepdims=True), axis=1, keepdims=True)


def clip_kernel(
    clip_ref,
    mids_ref,
    sums_ref,
    normed_ref,
    gradient_ref,
    normed_gram_ref,
    gradient_gram_ref,
    out_ref,
    wide,
):
    sequences, _, hidden = sums_ref.shape
    local = wide.shape[1]
    bound = clip_ref[0]
    weights = []
    for e in range(sequences):
        rows = slice(e * SEQUENCE_TOKENS, (e + 1) * SEQUENCE_TOKENS)
        mids = mids_ref[: 3 * RANK, rows].astype(BF16)
        square = total_of(quadratic(mids[: 2 * RANK], normed_gram_ref[e])) + total_of(
            quadratic(mids[2 * RANK :], gradient_gram_ref[e])
        )
        square = SCALE * SCALE * jnp.maximum(square, 0.0)
        square = square + mids_ref[3 * RANK + e : 3 * RANK + e + 1, 0:1]
        weight = bound / jnp.maximum(jnp.sqrt(square), bound)
        weights.append(weight)
        first = weight * (
            SCALE * jnp.dot(mids[: 2 * RANK], normed_ref[rows, :], preferred_element_type=F32)
        )
        second = weight * (
            SCALE * jnp.dot(mids[2 * RANK :], gradient_ref[rows, :], preferred_element_type=F32)
        )
        if e == 0:
            wide[: 2 * RANK] = first
            wide[2 * RANK :] = second
        else:
            wide[: 2 * RANK] += first
            wide[2 * RANK :] += second
    lanes = (local + hidden) // 128
    for t in range(out_ref.shape[0]):
        r, c = divmod(t, lanes)
        rows = slice(8 * r, 8 * r + 8)
        at = c * 128
        if r >= 3 * RANK // 8:
            value = jnp.zeros((8, 128), F32)
        elif at < local:
            value = wide[rows, at : at + 128]
        else:
            at = at - local
            value = weights[0] * sums_ref[0, rows, at : at + 128]
            for e in range(1, sequences):
                value = value + weights[e] * sums_ref[e, rows, at : at + 128]
        out_ref[t] = value


def ring(size, by):
    return [(i, (i + by) % size) for i in range(size)]


def per_device(
    sizes,
    normed,
    output_gradient,
    gate_preactivation,
    upward_preactivation,
    frozen_down_weight,
    adapter_width_factors,
    adapter_hidden_factors,
    clipping_limit,
    width_noise_draw,
    hidden_noise_draw,
):
    tokens, local_width = normed.shape
    hidden = gate_preactivation.shape[1]
    sequences = tokens // SEQUENCE_TOKENS
    n_z = sizes["z"]
    n_tensor = sizes["x"] * sizes["c"]
    z_axes, tensor_axes = "z", ("x", "c")
    z = lax.axis_index(z_axes)

    gradient = lax.all_gather(output_gradient, tensor_axes, axis=1, tiled=True)
    block = lax.all_gather(frozen_down_weight.T, "y", axis=0, tiled=True)
    normed_all = lax.all_gather(normed, tensor_axes, axis=1, tiled=True)

    rows = block.shape[0]
    half = rows // 2
    units = rows // 128
    vmem = pl.BlockSpec(memory_space=pltpu.VMEM)
    smem = pl.BlockSpec(memory_space=pltpu.SMEM)
    hbm = pl.BlockSpec(memory_space=pl.ANY)
    params = pltpu.CompilerParams(vmem_limit_bytes=60 * 2**20)

    def place(offsets):
        at = [((z + offset) % n_z) * units for offset in offsets]
        return jnp.stack(at).astype(jnp.int32)

    low, high = {0: block}, {0: block}

    def step(k, low_from, high_from):
        low[k] = lax.ppermute(low_from, z_axes, ring(n_z, 1))
        high[k] = lax.ppermute(high_from, z_axes, ring(n_z, -1))

    def side(values, factors, name):
        width = values.shape[1]
        chunk = 1024
        return pl.pallas_call(
            functools.partial(side_kernel, sequences // 2),
            out_shape=(
                jax.ShapeDtypeStruct((factors.shape[0], tokens), BF16),
                jax.ShapeDtypeStruct((sequences, SEQUENCE_TOKENS, SEQUENCE_TOKENS), F32),
            ),
            grid=(width // chunk,),
            in_specs=[
                pl.BlockSpec((2 * SEQUENCE_TOKENS, chunk), functools.partial(lambda p, i: (p, i), p))
                for p in range(sequences // 2)
            ]
            + [pl.BlockSpec((factors.shape[0], chunk), lambda i: (0, i))],
            out_specs=(
                pl.BlockSpec((factors.shape[0], tokens), lambda i: (0, 0)),
                pl.BlockSpec((sequences, SEQUENCE_TOKENS, SEQUENCE_TOKENS), lambda i: (0, 0, 0)),
            ),
            scratch_shapes=[
                pltpu.VMEM(
                    (sequences // 2, 2 * SEQUENCE_TOKENS + factors.shape[0], 2 * SEQUENCE_TOKENS), F32
                )
            ],
            compiler_params=params,
            cost_estimate=pl.CostEstimate(
                flops=2 * tokens * width * (128 + factors.shape[0]),
                bytes_accessed=5 * 2**20,
                transcendentals=0,
            ),
            name=name,
        )(*[values] * (sequences // 2), factors)

    def scratch(n_rows, n_sems):
        return [
            pltpu.VMEM((tokens, n_rows), BF16),
            pltpu.VMEM((n_rows, hidden), BF16),
            pltpu.SemaphoreType.DMA((n_sems,)),
            pltpu.SemaphoreType.DMA((-(-hidden // 256),)),
        ]

    def part(offsets, before=None):
        blocks = [(low if offset < 0 else high)[abs(offset)] for offset in offsets]
        n = len(blocks)
        given = [] if before is None else [before]
        return pl.pallas_call(
            functools.partial(part_kernel, n, before is None),
            out_shape=jax.ShapeDtypeStruct((tokens, hidden), F32),
            in_specs=[smem] + [hbm] * (n + 1 + len(given)),
            out_specs=hbm,
            scratch_shapes=[pltpu.VMEM((tokens, hidden), F32)] + scratch(n * rows, 4 * n + 4),
            compiler_params=params,
            cost_estimate=pl.CostEstimate(
                flops=2 * tokens * n * rows * hidden,
                bytes_accessed=6 * 2**20,
                transcendentals=0,
            ),
            name="part_product",
        )(place(offsets), gradient, *blocks, *given)

    def after(value, other):
        return lax.optimization_barrier((value, other))[0]

    def pairs(first, end):
        return [sign * k for k in range(first, end) for sign in (-1, 1)]

    last = n_z // 2
    for k in range(1, last - 3):
        step(k, low[k - 1], high[k - 1])
    total = part([0] + pairs(1, last - 5))
    at = last - 4
    step(at + 1, after(low[at], total), after(high[at], total))
    lora_t, gradient_gram = side(gradient, adapter_width_factors[2], "gradient_side")
    at = last - 3
    step(at + 1, after(low[at], lora_t), after(high[at], lora_t))
    total = part(pairs(last - 5, last - 2), total)
    at = last - 2
    step(at + 1, after(low[at], total), after(high[at], total))
    at = last - 1
    step(last, low[at][:half], high[at][half:])
    in_t, normed_gram = side(
        normed_all, adapter_width_factors[:2].reshape(2 * RANK, -1), "normed_side"
    )
    far = ((z + last) % n_z) * units
    blocks = [side_of[k] for k in range(last - 2, last + 1) for side_of in (low, high)]
    places = jnp.concatenate(
        [place(pairs(last - 2, last)), jnp.stack([far, far + units // 2]).astype(jnp.int32)]
    )
    sums, mids = pl.pallas_call(
        functools.partial(hidden_kernel, len(blocks)),
        out_shape=(
            jax.ShapeDtypeStruct((sequences, 3 * RANK, hidden), F32),
            jax.ShapeDtypeStruct((8 * n_tensor, tokens), F32),
        ),
        in_specs=[smem] + [hbm] * (len(blocks) + 4) + [vmem] * 4,
        out_specs=(hbm, vmem),
        scratch_shapes=[
            pltpu.VMEM((tokens, hidden), F32),
            pltpu.VMEM((tokens, hidden), F32),
            pltpu.VMEM((tokens, hidden), BF16),
            pltpu.VMEM((tokens, hidden), BF16),
            pltpu.VMEM((sequences, 3 * RANK, hidden), F32),
        ]
        + scratch(5 * rows, 4 * len(blocks) + 12),
        compiler_params=params,
        name="hidden_side",
    )(
        places,
        gradient,
        *blocks,
        total,
        gate_preactivation,
        upward_preactivation,
        adapter_hidden_factors.reshape(3 * RANK, hidden),
        in_t,
        lora_t.T,
        lora_t,
    )

    pieces = lax.all_to_all(mids.reshape(n_tensor, 8, tokens), tensor_axes, 0, 0)
    piece = jnp.sum(pieces, axis=0)
    mids = lax.all_to_all(
        jnp.broadcast_to(piece, (n_tensor,) + piece.shape), tensor_axes, 0, 0
    ).reshape(8 * n_tensor, tokens)

    lanes = (local_width + hidden) // 128
    tiles = 6 * lanes
    padded = -(-tiles // 8) * 8
    out = pl.pallas_call(
        clip_kernel,
        out_shape=jax.ShapeDtypeStruct((padded, 8, 128), F32),
        in_specs=[smem] + [vmem] * 6,
        out_specs=vmem,
        scratch_shapes=[pltpu.VMEM((3 * RANK, local_width), F32)],
        compiler_params=params,
        name="clip_side",
    )(
        clipping_limit,
        mids,
        sums,
        normed,
        output_gradient,
        normed_gram,
        gradient_gram,
    )

    n_y = sizes["y"]
    share = jnp.sum(lax.all_to_all(out.reshape(n_y, -1, 128), "y", 0, 0), axis=0)
    share = jnp.sum(lax.all_to_all(share.reshape(n_z, -1, 128), z_axes, 0, 0), axis=0)
    share = lax.all_to_all(
        jnp.broadcast_to(share, (n_z,) + share.shape), z_axes, 0, 0
    ).reshape(-1, 128)
    whole = lax.all_to_all(jnp.broadcast_to(share, (n_y,) + share.shape), "y", 0, 0)
    total = (
        whole.reshape(padded, 8, 128)[:tiles]
        .reshape(6, lanes, 8, 128)
        .transpose(0, 2, 1, 3)
        .reshape(3, RANK, lanes * 128)
    )
    count = sequences * n_z * sizes["y"]
    bound = clipping_limit[0]
    wide = total[:, :, :local_width]
    inner = total[:, :, local_width : local_width + hidden]
    return (
        (wide + bound * width_noise_draw) / count,
        (inner + bound * hidden_noise_draw) / count,
    )


def solution(mesh):
    names = ("z", "y", "x", "c")
    extents = (16, 4, 4, 2)
    fine = Mesh(mesh.devices.reshape(extents), names)
    dp, tensor = ("z", "y"), ("x", "c")
    placed = (
        P(dp, tensor),
        P(dp, tensor),
        P(dp, tensor),
        P(dp, tensor),
        P(tensor, dp),
        P(),
        P(None, None, tensor),
        P(),
        P(None, None, tensor),
        P(None, None, tensor),
    )
    return jax.shard_map(
        functools.partial(per_device, dict(zip(names, extents, strict=True))),
        mesh=fine,
        in_specs=placed,
        out_specs=(P(None, None, tensor), P(None, None, tensor)),
        check_vma=False,
    )
```

```python
import functools

import jax
import jax.numpy as jnp
from jax import lax
from jax.experimental import pallas as pl
from jax.experimental.pallas import tpu as pltpu
from jax.sharding import Mesh
from jax.sharding import PartitionSpec as P

SEQUENCE_TOKENS = 128
RANK = 16
SCALE = 2.0
F32 = jnp.float32
BF16 = jnp.bfloat16


def contract(left, right, left_dim, right_dim):
    return lax.dot_general(
        left, right, (((left_dim,), (right_dim,)), ((), ())), preferred_element_type=F32
    )


def column_tiles(hidden, step, tile):
    whole = hidden // step

    def body(i, carry):
        tile(i, pl.multiple_of(i * step, step), step)
        return carry

    lax.fori_loop(0, whole, body, 0)
    spans = [(i * step, step) for i in range(whole)]
    if hidden > whole * step:
        spans.append((whole * step, hidden - whole * step))
        tile(whole, *spans[-1])
    return spans


def copy_rows(source, target, sems, at, parts):
    rows = source.shape[0] // parts
    copies = []
    for i in range(parts):
        span = pl.ds(i * rows, rows)
        copies.append(
            pltpu.make_async_copy(source.at[span, :], target.at[span, :], sems.at[at + i])
        )
    return copies


def fetch_blocks(plan, place_ref, gradient_ref, block_refs, left, right, sems):
    copies, at = [], 0
    for i, sources in enumerate(plan):
        n = len(sources)
        rows = right.shape[0] // len(plan)
        piece = rows // n
        span = pl.ds(i * rows, rows)
        columns = pl.ds(pl.multiple_of(place_ref[i] * rows, rows), rows)
        copies += copy_rows(gradient_ref.at[:, columns], left.at[:, span], sems, at, 2)
        at += 2
        for j, (block, row) in enumerate(sources):
            to = i * rows + lax.rem(place_ref[len(plan)] + j, n) * piece
            copies.append(
                pltpu.make_async_copy(
                    block_refs[block].at[pl.ds(row, piece), :],
                    right.at[pl.ds(pl.multiple_of(to, piece), piece), :],
                    sems.at[at],
                )
            )
            at += 1
    return copies


def side_kernel(n_pairs, *refs):
    row_refs = refs[:n_pairs]
    factors_ref, projected_ref, gram_ref, total = refs[n_pairs:]
    step = pl.program_id(0)
    size = SEQUENCE_TOKENS

    @pl.when(step == 0)
    def _():
        total[...] = jnp.zeros_like(total)

    for p, rows_ref in enumerate(row_refs):
        rows = rows_ref[...]
        stacked = jnp.concatenate([rows, factors_ref[...]], axis=0)
        total[p] += contract(stacked, rows, 1, 1)

    @pl.when(step == pl.num_programs(0) - 1)
    def _():
        for p in range(n_pairs):
            gram_ref[2 * p] = total[p, :size, :size]
            gram_ref[2 * p + 1] = total[p, size : 2 * size, size:]
            projected_ref[:, 2 * size * p : 2 * size * (p + 1)] = total[p, 2 * size :].astype(BF16)


def part_kernel(plan, n_blocks, first, place_ref, gradient_ref, *refs):
    block_refs = refs[:n_blocks]
    refs = refs[n_blocks:]
    if not first:
        before_ref, refs = refs[0], refs[1:]
    out_ref, total, left, right, sems, out_sems = refs
    copies = fetch_blocks(plan, place_ref, gradient_ref, block_refs, left, right, sems)
    if not first:
        copies += copy_rows(before_ref, total, sems, len(copies), 4)
    for copy in copies:
        copy.start()
    for copy in copies:
        copy.wait()

    writes = []
    hidden = total.shape[1]
    for i, start in enumerate(range(0, hidden, 512)):
        cols = slice(start, min(start + 512, hidden))
        product = jnp.dot(left[...], right[:, cols], preferred_element_type=F32)
        total[:, cols] = product if first else total[:, cols] + product
        write = pltpu.make_async_copy(total.at[:, cols], out_ref.at[:, cols], out_sems.at[i])
        write.start()
        writes.append(write)
    for write in writes:
        write.wait()


def hidden_kernel(plan, n_blocks, place_ref, gradient_ref, *refs):
    block_refs = refs[:n_blocks]
    (before_hbm, gate_hbm, up_hbm, factors_ref, in_ref, lora_ref, lora_t_ref) = refs[
        n_blocks : n_blocks + 7
    ]
    (sums_hbm, mids_ref, total, before_ref, gate_ref, up_ref, sums_ref, left_rows, right_rows) = (
        refs[n_blocks + 7 : -2]
    )
    sems, out_sems = refs[-2:]
    tokens, hidden = gate_ref.shape
    sequences = tokens // SEQUENCE_TOKENS
    blocks = fetch_blocks(plan, place_ref, gradient_ref, block_refs, left_rows, right_rows, sems)
    copies, at = [], len(blocks)
    for source, target in ((before_hbm, before_ref), (gate_hbm, gate_ref), (up_hbm, up_ref)):
        copies += copy_rows(source, target, sems, at, 4)
        at += 4
    for copy in blocks + copies:
        copy.start()
    mids_ref[...] = jnp.zeros_like(mids_ref)
    for copy in blocks:
        copy.wait()
    total[...] = jnp.dot(left_rows[...], right_rows[...], preferred_element_type=F32)
    for copy in copies:
        copy.wait()

    def write(i, cols):
        return pltpu.make_async_copy(
            sums_ref.at[:, :, cols], sums_hbm.at[:, :, cols], out_sems.at[i]
        )

    def tile(i, start, width):
        cols = pl.ds(start, width)
        factors = factors_ref[:, cols]
        for e in range(sequences):
            rows = slice(e * SEQUENCE_TOKENS, (e + 1) * SEQUENCE_TOKENS)
            hidden_grad = (
                total[rows, cols]
                + before_ref[rows, cols]
                + SCALE
                * jnp.dot(lora_ref[rows, :], factors[2 * RANK :], preferred_element_type=F32)
            )
            gate = gate_ref[rows, cols].astype(F32)
            up = up_ref[rows, cols].astype(F32)
            sigmoid = jax.nn.sigmoid(gate)
            silu = gate * sigmoid
            slope = sigmoid * (1.0 + gate * (1.0 - sigmoid))
            activation = (silu * up).astype(BF16)
            gate_grad = (hidden_grad * up * slope).astype(BF16)
            up_grad = (hidden_grad * silu).astype(BF16)
            left = (in_ref[:RANK, rows], in_ref[RANK:, rows], lora_t_ref[:, rows])
            for j, right in enumerate((gate_grad, up_grad, activation)):
                part = slice(j * RANK, (j + 1) * RANK)
                sums_ref[e, part, cols] = SCALE * jnp.dot(
                    left[j], right, preferred_element_type=F32
                )
                mids_ref[part, rows] += contract(factors[part], right, 1, 1)
        write(i, cols).start()

    spans = column_tiles(hidden, 256, tile)
    for e in range(sequences):
        square = sums_ref[e] * sums_ref[e]
        line = jnp.sum(jnp.sum(square, axis=0, keepdims=True), axis=1, keepdims=True)
        mids_ref[3 * RANK + e : 3 * RANK + e + 1, :] = jnp.broadcast_to(line, (1, tokens))
    for i, (start, width) in enumerate(spans):
        write(i, pl.ds(start, width)).wait()


def quadratic(left, gram):
    product = jnp.zeros((left.shape[0], gram.shape[1]), F32)
    rest = gram
    for _ in range(3):
        part = rest.astype(BF16)
        product = product + jnp.dot(left, part, preferred_element_type=F32)
        rest = rest - part.astype(F32)
    return product * left.astype(F32)


def total_of(values):
    return jnp.sum(jnp.sum(values, axis=0, keepdims=True), axis=1, keepdims=True)


def clip_kernel(
    clip_ref,
    mids_ref,
    sums_ref,
    normed_ref,
    gradient_ref,
    normed_gram_ref,
    gradient_gram_ref,
    out_ref,
    wide,
):
    sequences, _, hidden = sums_ref.shape
    local = wide.shape[1]
    bound = clip_ref[0]
    weights = []
    for e in range(sequences):
        rows = slice(e * SEQUENCE_TOKENS, (e + 1) * SEQUENCE_TOKENS)
        mids = mids_ref[: 3 * RANK, rows].astype(BF16)
        square = total_of(quadratic(mids[: 2 * RANK], normed_gram_ref[e])) + total_of(
            quadratic(mids[2 * RANK :], gradient_gram_ref[e])
        )
        square = SCALE * SCALE * jnp.maximum(square, 0.0)
        square = square + mids_ref[3 * RANK + e : 3 * RANK + e + 1, 0:1]
        weight = bound / jnp.maximum(jnp.sqrt(square), bound)
        weights.append(weight)
        first = weight * (
            SCALE * jnp.dot(mids[: 2 * RANK], normed_ref[rows, :], preferred_element_type=F32)
        )
        second = weight * (
            SCALE * jnp.dot(mids[2 * RANK :], gradient_ref[rows, :], preferred_element_type=F32)
        )
        if e == 0:
            wide[: 2 * RANK] = first
            wide[2 * RANK :] = second
        else:
            wide[: 2 * RANK] += first
            wide[2 * RANK :] += second
    lanes = (local + hidden) // 128
    for t in range(out_ref.shape[0]):
        r, c = divmod(t, lanes)
        rows = slice(8 * r, 8 * r + 8)
        at = c * 128
        if r >= 3 * RANK // 8:
            value = jnp.zeros((8, 128), F32)
        elif at < local:
            value = wide[rows, at : at + 128]
        else:
            at = at - local
            value = weights[0] * sums_ref[0, rows, at : at + 128]
            for e in range(1, sequences):
                value = value + weights[e] * sums_ref[e, rows, at : at + 128]
        out_ref[t] = value


def ring(size, by):
    return [(i, (i + by) % size) for i in range(size)]


def per_device(
    sizes,
    normed,
    output_gradient,
    gate_preactivation,
    upward_preactivation,
    frozen_down_weight,
    adapter_width_factors,
    adapter_hidden_factors,
    clipping_limit,
    width_noise_draw,
    hidden_noise_draw,
):
    tokens, local_width = normed.shape
    hidden = gate_preactivation.shape[1]
    sequences = tokens // SEQUENCE_TOKENS
    n_z = sizes["z"]
    n_tensor = sizes["x"] * sizes["c"]
    z_axes, tensor_axes = "z", ("x", "c")
    z = lax.axis_index(z_axes)

    gradient = lax.all_gather(output_gradient, tensor_axes, axis=1, tiled=True)
    shard = frozen_down_weight.T
    normed_all = lax.all_gather(normed, tensor_axes, axis=1, tiled=True)

    n_y = sizes["y"]
    piece = shard.shape[0]
    rows = n_y * piece
    y = lax.axis_index("y")
    vmem = pl.BlockSpec(memory_space=pltpu.VMEM)
    smem = pl.BlockSpec(memory_space=pltpu.SMEM)
    hbm = pl.BlockSpec(memory_space=pl.ANY)
    params = pltpu.CompilerParams(vmem_limit_bytes=60 * 2**20)

    def place(offsets):
        at = [(z + offset + n_z) % n_z for offset in offsets]
        return jnp.stack(at + [y]).astype(jnp.int32)

    block = jnp.concatenate([shard, lax.ppermute(shard, "y", ring(n_y, -1))], axis=0)
    low, high = {0: block}, {0: block}
    last = n_z // 2

    def step(k, low_from, high_from):
        low[k] = lax.ppermute(low_from, z_axes, ring(n_z, 1))
        high[k] = lax.ppermute(high_from, z_axes, ring(n_z, -1))

    def pair_of(offset):
        if offset == last:
            return low[last], high[last]
        whole = (low if offset < 0 else high)[abs(offset)]
        return whole[:piece], whole[piece:]

    def exchange(offsets):
        own, following = zip(*(pair_of(offset) for offset in offsets), strict=True)
        return (
            lax.ppermute(jnp.concatenate(following, axis=0), "y", ring(n_y, -1)),
            lax.ppermute(jnp.concatenate(own, axis=0), "y", ring(n_y, 1)),
        )

    def blocks_of(offsets, others):
        blocks, plan = list(others), []
        for i, offset in enumerate(offsets):
            if offset == last:
                here = [(len(blocks), 0), (len(blocks) + 1, 0)]
                blocks += [low[last], high[last]]
            else:
                here = [(len(blocks), 0), (len(blocks), piece)]
                blocks.append((low if offset < 0 else high)[abs(offset)])
            plan.append(here + [(0, i * piece), (1, i * piece)])
        return blocks, plan

    def side(values, factors, name):
        width = values.shape[1]
        chunk = 1024
        return pl.pallas_call(
            functools.partial(side_kernel, sequences // 2),
            out_shape=(
                jax.ShapeDtypeStruct((factors.shape[0], tokens), BF16),
                jax.ShapeDtypeStruct((sequences, SEQUENCE_TOKENS, SEQUENCE_TOKENS), F32),
            ),
            grid=(width // chunk,),
            in_specs=[
                pl.BlockSpec((2 * SEQUENCE_TOKENS, chunk), functools.partial(lambda p, i: (p, i), p))
                for p in range(sequences // 2)
            ]
            + [pl.BlockSpec((factors.shape[0], chunk), lambda i: (0, i))],
            out_specs=(
                pl.BlockSpec((factors.shape[0], tokens), lambda i: (0, 0)),
                pl.BlockSpec((sequences, SEQUENCE_TOKENS, SEQUENCE_TOKENS), lambda i: (0, 0, 0)),
            ),
            scratch_shapes=[
                pltpu.VMEM(
                    (sequences // 2, 2 * SEQUENCE_TOKENS + factors.shape[0], 2 * SEQUENCE_TOKENS), F32
                )
            ],
            compiler_params=params,
            cost_estimate=pl.CostEstimate(
                flops=2 * tokens * width * (128 + factors.shape[0]),
                bytes_accessed=5 * 2**20,
                transcendentals=0,
            ),
            name=name,
        )(*[values] * (sequences // 2), factors)

    def scratch(n_rows, n_sems):
        return [
            pltpu.VMEM((tokens, n_rows), BF16),
            pltpu.VMEM((n_rows, hidden), BF16),
            pltpu.SemaphoreType.DMA((n_sems,)),
            pltpu.SemaphoreType.DMA((-(-hidden // 256),)),
        ]

    def part(offsets, others, before=None):
        blocks, plan = blocks_of(offsets, others)
        n = len(offsets)
        given = [] if before is None else [before]
        return pl.pallas_call(
            functools.partial(part_kernel, plan, len(blocks), before is None),
            out_shape=jax.ShapeDtypeStruct((tokens, hidden), F32),
            in_specs=[smem] + [hbm] * (len(blocks) + 1 + len(given)),
            out_specs=hbm,
            scratch_shapes=[pltpu.VMEM((tokens, hidden), F32)]
            + scratch(n * rows, (2 + n_y) * n + 4),
            compiler_params=params,
            cost_estimate=pl.CostEstimate(
                flops=2 * tokens * n * rows * hidden,
                bytes_accessed=6 * 2**20,
                transcendentals=0,
            ),
            name="part_product",
        )(place(offsets), gradient, *blocks, *given)

    def after(value, other):
        return lax.optimization_barrier((value, other))[0]

    def pairs(first, end):
        return [sign * k for k in range(first, end) for sign in (-1, 1)]

    last = n_z // 2
    for k in range(1, last - 4):
        step(k, low[k - 1], high[k - 1])
    groups = [[0] + pairs(1, last - 4), pairs(last - 4, last - 1), pairs(last - 1, last) + [last]]
    others = [exchange(groups[0])]
    for k in range(last - 4, last - 2):
        step(k, low[k - 1], high[k - 1])
    lora_t, gradient_gram = side(gradient, adapter_width_factors[2], "gradient_side")
    at = last - 3
    step(at + 1, after(low[at], lora_t), after(high[at], lora_t))
    others.append(exchange(groups[1]))
    total = part(groups[0], others[0])
    at = last - 2
    step(at + 1, after(low[at], total), after(high[at], total))
    at = last - 1
    step(last, low[at][:piece], high[at][piece:])
    others.append(exchange(groups[2]))
    total = part(groups[1], others[1], after(total, low[last]))
    in_t, normed_gram = side(
        normed_all, adapter_width_factors[:2].reshape(2 * RANK, -1), "normed_side"
    )
    blocks, plan = blocks_of(groups[2], others[2])
    sums, mids = pl.pallas_call(
        functools.partial(hidden_kernel, plan, len(blocks)),
        out_shape=(
            jax.ShapeDtypeStruct((sequences, 3 * RANK, hidden), F32),
            jax.ShapeDtypeStruct((8 * n_tensor, tokens), F32),
        ),
        in_specs=[smem] + [hbm] * (len(blocks) + 4) + [vmem] * 4,
        out_specs=(hbm, vmem),
        scratch_shapes=[
            pltpu.VMEM((tokens, hidden), F32),
            pltpu.VMEM((tokens, hidden), F32),
            pltpu.VMEM((tokens, hidden), BF16),
            pltpu.VMEM((tokens, hidden), BF16),
            pltpu.VMEM((sequences, 3 * RANK, hidden), F32),
        ]
        + scratch(len(plan) * rows, (2 + n_y) * len(plan) + 12),
        compiler_params=params,
        name="hidden_side",
    )(
        place(groups[2]),
        gradient,
        *blocks,
        total,
        gate_preactivation,
        upward_preactivation,
        adapter_hidden_factors.reshape(3 * RANK, hidden),
        in_t,
        lora_t.T,
        lora_t,
    )

    pieces = lax.all_to_all(mids.reshape(n_tensor, 8, tokens), tensor_axes, 0, 0)
    piece = jnp.sum(pieces, axis=0)
    mids = lax.all_to_all(
        jnp.broadcast_to(piece, (n_tensor,) + piece.shape), tensor_axes, 0, 0
    ).reshape(8 * n_tensor, tokens)

    lanes = (local_width + hidden) // 128
    tiles = 6 * lanes
    padded = -(-tiles // 8) * 8
    out = pl.pallas_call(
        clip_kernel,
        out_shape=jax.ShapeDtypeStruct((padded, 8, 128), F32),
        in_specs=[smem] + [vmem] * 6,
        out_specs=vmem,
        scratch_shapes=[pltpu.VMEM((3 * RANK, local_width), F32)],
        compiler_params=params,
        name="clip_side",
    )(
        clipping_limit,
        mids,
        sums,
        normed,
        output_gradient,
        normed_gram,
        gradient_gram,
    )

    share = jnp.sum(lax.all_to_all(out.reshape(n_y, -1, 128), "y", 0, 0), axis=0)
    share = jnp.sum(lax.all_to_all(share.reshape(n_z, -1, 128), z_axes, 0, 0), axis=0)
    share = lax.all_to_all(
        jnp.broadcast_to(share, (n_z,) + share.shape), z_axes, 0, 0
    ).reshape(-1, 128)
    whole = lax.all_to_all(jnp.broadcast_to(share, (n_y,) + share.shape), "y", 0, 0)
    total = (
        whole.reshape(padded, 8, 128)[:tiles]
        .reshape(6, lanes, 8, 128)
        .transpose(0, 2, 1, 3)
        .reshape(3, RANK, lanes * 128)
    )
    count = sequences * n_z * sizes["y"]
    bound = clipping_limit[0]
    wide = total[:, :, :local_width]
    inner = total[:, :, local_width : local_width + hidden]
    return (
        (wide + bound * width_noise_draw) / count,
        (inner + bound * hidden_noise_draw) / count,
    )


def solution(mesh):
    names = ("z", "y", "x", "c")
    extents = (16, 4, 4, 2)
    fine = Mesh(mesh.devices.reshape(extents), names)
    dp, tensor = ("z", "y"), ("x", "c")
    placed = (
        P(dp, tensor),
        P(dp, tensor),
        P(dp, tensor),
        P(dp, tensor),
        P(tensor, dp),
        P(),
        P(None, None, tensor),
        P(),
        P(None, None, tensor),
        P(None, None, tensor),
    )
    return jax.shard_map(
        functools.partial(per_device, dict(zip(names, extents, strict=True))),
        mesh=fine,
        in_specs=placed,
        out_specs=(P(None, None, tensor), P(None, None, tensor)),
        check_vma=False,
    )
```

```python
import functools

import jax
import jax.numpy as jnp
from jax import lax
from jax.experimental import pallas as pl
from jax.experimental.pallas import tpu as pltpu
from jax.sharding import Mesh
from jax.sharding import PartitionSpec as P

SEQUENCE_TOKENS = 128
RANK = 16
SCALE = 2.0
F32 = jnp.float32
BF16 = jnp.bfloat16


def contract(left, right, left_dim, right_dim):
    return lax.dot_general(
        left, right, (((left_dim,), (right_dim,)), ((), ())), preferred_element_type=F32
    )


def column_tiles(hidden, step, tile):
    whole = hidden // step

    def body(i, carry):
        tile(i, pl.multiple_of(i * step, step), step)
        return carry

    lax.fori_loop(0, whole, body, 0)
    spans = [(i * step, step) for i in range(whole)]
    if hidden > whole * step:
        spans.append((whole * step, hidden - whole * step))
        tile(whole, *spans[-1])
    return spans


def copy_rows(source, target, sems, at, parts):
    rows = source.shape[0] // parts
    copies = []
    for i in range(parts):
        span = pl.ds(i * rows, rows)
        copies.append(
            pltpu.make_async_copy(source.at[span, :], target.at[span, :], sems.at[at + i])
        )
    return copies


def fetch_blocks(plan, z_ref, gradient_ref, block_refs, left, right, sems):
    n_z, rows_z = plan["n_z"], plan["rows"]
    fetched, row, at = [], 0, 0
    for (offset, first), block in zip(plan["blocks"], block_refs, strict=True):
        rows = block.shape[0]
        start = lax.rem(z_ref[0] + (offset + n_z), n_z) * rows_z + first
        columns = pl.ds(pl.multiple_of(start, 128), rows)
        span = pl.ds(row, rows)
        fetched.append(
            copy_rows(gradient_ref.at[:, columns], left.at[:, span], sems, at, 2)
            + copy_rows(block, right.at[span, :], sems, at + 2, 2)
        )
        row += rows
        at += 4
    return fetched


def side_kernel(n_pairs, *refs):
    row_refs = refs[:n_pairs]
    factors_ref, projected_ref, turned_ref, gram_ref, total = refs[n_pairs:]
    step = pl.program_id(0)
    size = SEQUENCE_TOKENS

    @pl.when(step == 0)
    def _():
        total[...] = jnp.zeros_like(total)

    for p, rows_ref in enumerate(row_refs):
        rows = rows_ref[...]
        stacked = jnp.concatenate([rows, factors_ref[...]], axis=0)
        total[p] += contract(stacked, rows, 1, 1)

    @pl.when(step == pl.num_programs(0) - 1)
    def _():
        for p in range(n_pairs):
            gram_ref[2 * p] = total[p, :size, :size]
            gram_ref[2 * p + 1] = total[p, size : 2 * size, size:]
            span = slice(2 * size * p, 2 * size * (p + 1))
            projected = total[p, 2 * size :]
            projected_ref[:, span] = projected.astype(BF16)
            turned_ref[span, :] = projected.T.astype(BF16)


def part_kernel(plan, z_ref, gradient_ref, *refs):
    n_blocks = len(plan["blocks"])
    block_refs = refs[:n_blocks]
    out_ref, total, left, right, sems, out_sems = refs[n_blocks:]
    copies = sum(fetch_blocks(plan, z_ref, gradient_ref, block_refs, left, right, sems), [])
    for copy in copies:
        copy.start()
    for copy in copies:
        copy.wait()

    writes = []
    hidden = total.shape[1]
    for i, start in enumerate(range(0, hidden, 512)):
        cols = slice(start, min(start + 512, hidden))
        total[:, cols] = jnp.dot(left[...], right[:, cols], preferred_element_type=F32)
        write = pltpu.make_async_copy(total.at[:, cols], out_ref.at[:, cols], out_sems.at[i])
        write.start()
        writes.append(write)
    for write in writes:
        write.wait()


def hidden_kernel(plan, z_ref, gradient_ref, *refs):
    n_blocks = len(plan["blocks"])
    block_refs = refs[:n_blocks]
    (before_hbm, gate_hbm, up_hbm, factors_ref, in_ref, lora_ref, lora_t_ref) = refs[
        n_blocks : n_blocks + 7
    ]
    sums_hbm, mids_ref, total, before_ref, gate_ref, up_ref, silu_ref, scaled_ref, sums_ref = refs[
        n_blocks + 7 : -4
    ]
    left_rows, right_rows, sems, out_sems = refs[-4:]
    tokens, hidden = gate_ref.shape
    sequences = tokens // SEQUENCE_TOKENS
    fetched = fetch_blocks(plan, z_ref, gradient_ref, block_refs, left_rows, right_rows, sems)
    at = 4 * n_blocks
    activations = copy_rows(gate_hbm, gate_ref, sems, at, 4)
    activations += copy_rows(up_hbm, up_ref, sems, at + 4, 4)
    running = copy_rows(before_hbm, before_ref, sems, at + 8, 4)
    for copy in activations + sum(fetched, []) + running:
        copy.start()
    mids_ref[...] = jnp.zeros_like(mids_ref)

    def adapters(j, e, rows, cols, left, right):
        part = slice(j * RANK, (j + 1) * RANK)
        sums_ref[e, part, cols] = SCALE * jnp.dot(left, right, preferred_element_type=F32)
        mids_ref[part, rows] += contract(factors_ref[part, cols], right, 1, 1)

    def each(i, start, width, body):
        for e in range(sequences):
            body(e, slice(e * SEQUENCE_TOKENS, (e + 1) * SEQUENCE_TOKENS), pl.ds(start, width))

    def forward(e, rows, cols):
        gate = gate_ref[rows, cols].astype(F32)
        up = up_ref[rows, cols].astype(F32)
        sigmoid = jax.nn.sigmoid(gate)
        silu = gate * sigmoid
        slope = sigmoid * (1.0 + gate * (1.0 - sigmoid))
        silu_ref[rows, cols] = silu
        scaled_ref[rows, cols] = up * slope
        adapters(2, e, rows, cols, lora_t_ref[:, rows], (silu * up).astype(BF16))

    def backward(e, rows, cols):
        hidden_grad = (
            total[rows, cols]
            + before_ref[rows, cols]
            + SCALE
            * jnp.dot(lora_ref[rows, :], factors_ref[2 * RANK :, cols], preferred_element_type=F32)
        )
        gate_grad = (hidden_grad * scaled_ref[rows, cols]).astype(BF16)
        adapters(0, e, rows, cols, in_ref[:RANK, rows], gate_grad)
        up_grad = (hidden_grad * silu_ref[rows, cols]).astype(BF16)
        adapters(1, e, rows, cols, in_ref[RANK:, rows], up_grad)

    def write(i, cols):
        return pltpu.make_async_copy(
            sums_ref.at[:, :, cols], sums_hbm.at[:, :, cols], out_sems.at[i]
        )

    def last_tile(i, start, width):
        each(i, start, width, backward)
        write(i, pl.ds(start, width)).start()

    for copy in activations:
        copy.wait()
    column_tiles(hidden, hidden, functools.partial(each, body=forward))
    row = 0
    for some in plan["chunks"]:
        for copy in sum(fetched[some], []):
            copy.wait()
        rows = sum(block.shape[0] for block in block_refs[some])
        span = slice(row, row + rows)
        product = jnp.dot(left_rows[:, span], right_rows[span, :], preferred_element_type=F32)
        total[...] = product if row == 0 else total[...] + product
        row += rows
    for copy in running:
        copy.wait()
    spans = column_tiles(hidden, hidden, last_tile)
    for e in range(sequences):
        square = sums_ref[e] * sums_ref[e]
        line = jnp.sum(jnp.sum(square, axis=0, keepdims=True), axis=1, keepdims=True)
        mids_ref[3 * RANK + e : 3 * RANK + e + 1, :] = jnp.broadcast_to(line, (1, tokens))
    for i, (start, width) in enumerate(spans):
        write(i, pl.ds(start, width)).wait()


def quadratic(left, gram):
    product = jnp.zeros((left.shape[0], gram.shape[1]), F32)
    rest = gram
    for _ in range(3):
        part = rest.astype(BF16)
        product = product + jnp.dot(left, part, preferred_element_type=F32)
        rest = rest - part.astype(F32)
    return product * left.astype(F32)


def total_of(values):
    return jnp.sum(jnp.sum(values, axis=0, keepdims=True), axis=1, keepdims=True)


def clip_kernel(
    clip_ref,
    mids_ref,
    sums_ref,
    normed_ref,
    gradient_ref,
    normed_gram_ref,
    gradient_gram_ref,
    out_ref,
    wide,
):
    sequences, _, hidden = sums_ref.shape
    local = wide.shape[1]
    bound = clip_ref[0]
    weights = []
    for e in range(sequences):
        rows = slice(e * SEQUENCE_TOKENS, (e + 1) * SEQUENCE_TOKENS)
        mids = mids_ref[: 3 * RANK, rows].astype(BF16)
        square = total_of(quadratic(mids[: 2 * RANK], normed_gram_ref[e])) + total_of(
            quadratic(mids[2 * RANK :], gradient_gram_ref[e])
        )
        square = SCALE * SCALE * jnp.maximum(square, 0.0)
        square = square + mids_ref[3 * RANK + e : 3 * RANK + e + 1, 0:1]
        weight = bound / jnp.maximum(jnp.sqrt(square), bound)
        weights.append(weight)
        first = weight * (
            SCALE * jnp.dot(mids[: 2 * RANK], normed_ref[rows, :], preferred_element_type=F32)
        )
        second = weight * (
            SCALE * jnp.dot(mids[2 * RANK :], gradient_ref[rows, :], preferred_element_type=F32)
        )
        if e == 0:
            wide[: 2 * RANK] = first
            wide[2 * RANK :] = second
        else:
            wide[: 2 * RANK] += first
            wide[2 * RANK :] += second
    lanes = (local + hidden) // 128
    for t in range(out_ref.shape[0]):
        r, c = divmod(t, lanes)
        rows = slice(8 * r, 8 * r + 8)
        at = c * 128
        if r >= 3 * RANK // 8:
            value = jnp.zeros((8, 128), F32)
        elif at < local:
            value = wide[rows, at : at + 128]
        else:
            at = at - local
            value = weights[0] * sums_ref[0, rows, at : at + 128]
            for e in range(1, sequences):
                value = value + weights[e] * sums_ref[e, rows, at : at + 128]
        out_ref[t] = value


def ring(size, by):
    return [(i, (i + by) % size) for i in range(size)]


def per_device(
    sizes,
    normed,
    output_gradient,
    gate_preactivation,
    upward_preactivation,
    frozen_down_weight,
    adapter_width_factors,
    adapter_hidden_factors,
    clipping_limit,
    width_noise_draw,
    hidden_noise_draw,
):
    tokens, local_width = normed.shape
    hidden = gate_preactivation.shape[1]
    sequences = tokens // SEQUENCE_TOKENS
    n_z = sizes["z"]
    n_tensor = sizes["x"] * sizes["c"]
    z_axes, tensor_axes = "z", ("x", "c")
    spot = lax.axis_index(z_axes).reshape(1).astype(jnp.int32)

    gradient = lax.all_gather(output_gradient, tensor_axes, axis=1, tiled=True)
    block = lax.all_gather(frozen_down_weight.T, "y", axis=0, tiled=True)
    normed_all = lax.all_gather(normed, tensor_axes, axis=1, tiled=True)

    rows = block.shape[0]
    half = rows // 2
    vmem = pl.BlockSpec(memory_space=pltpu.VMEM)
    smem = pl.BlockSpec(memory_space=pltpu.SMEM)
    hbm = pl.BlockSpec(memory_space=pl.ANY)
    params = pltpu.CompilerParams(vmem_limit_bytes=60 * 2**20)

    low, high = {0: block}, {0: block}

    def step(k, low_from, high_from):
        low[k] = lax.ppermute(low_from, z_axes, ring(n_z, 1))
        high[k] = lax.ppermute(high_from, z_axes, ring(n_z, -1))

    def side(values, first, count, name):
        width = values.shape[1]
        chunk = 1024
        return pl.pallas_call(
            functools.partial(side_kernel, sequences // 2),
            out_shape=(
                jax.ShapeDtypeStruct((count, tokens), BF16),
                jax.ShapeDtypeStruct((tokens, count), BF16),
                jax.ShapeDtypeStruct((sequences, SEQUENCE_TOKENS, SEQUENCE_TOKENS), F32),
            ),
            grid=(width // chunk,),
            in_specs=[
                pl.BlockSpec((2 * SEQUENCE_TOKENS, chunk), functools.partial(lambda p, i: (p, i), p))
                for p in range(sequences // 2)
            ]
            + [pl.BlockSpec((count, chunk), lambda i: (first // count, i))],
            out_specs=(
                pl.BlockSpec((count, tokens), lambda i: (0, 0)),
                pl.BlockSpec((tokens, count), lambda i: (0, 0)),
                pl.BlockSpec((sequences, SEQUENCE_TOKENS, SEQUENCE_TOKENS), lambda i: (0, 0, 0)),
            ),
            scratch_shapes=[
                pltpu.VMEM(
                    (sequences // 2, 2 * SEQUENCE_TOKENS + count, 2 * SEQUENCE_TOKENS), F32
                )
            ],
            compiler_params=params,
            cost_estimate=pl.CostEstimate(
                flops=2 * tokens * width * (128 + count),
                bytes_accessed=5 * 2**20,
                transcendentals=0,
            ),
            name=name,
        )(*[values] * (sequences // 2), adapter_width_factors.reshape(3 * RANK, width))

    def scratch(n_rows, n_sems):
        return [
            pltpu.VMEM((tokens, n_rows), BF16),
            pltpu.VMEM((n_rows, hidden), BF16),
            pltpu.SemaphoreType.DMA((n_sems,)),
            pltpu.SemaphoreType.DMA((-(-hidden // 256),)),
        ]

    def at_z(offset):
        return (low if offset < 0 else high)[abs(offset)]

    def part(offsets):
        blocks = [at_z(offset) for offset in offsets]
        plan = dict(n_z=n_z, rows=rows, blocks=[(offset, 0) for offset in offsets])
        n = len(blocks)
        return pl.pallas_call(
            functools.partial(part_kernel, plan),
            out_shape=jax.ShapeDtypeStruct((tokens, hidden), F32),
            in_specs=[smem] + [hbm] * (n + 1),
            out_specs=hbm,
            scratch_shapes=[pltpu.VMEM((tokens, hidden), F32)] + scratch(n * rows, 4 * n),
            compiler_params=params,
            cost_estimate=pl.CostEstimate(
                flops=2 * tokens * n * rows * hidden,
                bytes_accessed=6 * 2**20,
                transcendentals=0,
            ),
            name="part_product",
        )(spot, gradient, *blocks)

    def after(value, other):
        return lax.optimization_barrier((value, other))[0]

    def pairs(first, end):
        return [sign * k for k in range(first, end) for sign in (-1, 1)]

    last = n_z // 2
    for k in range(1, last - 3):
        step(k, low[k - 1], high[k - 1])
    total = part([0] + pairs(1, last - 4))
    at = last - 4
    step(at + 1, after(low[at], total), after(high[at], total))
    lora_t, lora, gradient_gram = side(gradient, 2 * RANK, RANK, "gradient_side")
    at = last - 3
    step(at + 1, after(low[at], lora_t), after(high[at], lora_t))
    step(last - 1, low[last - 2], high[last - 2])
    step(last, low[last - 1][:half], high[last - 1][half:])
    in_t, _, normed_gram = side(normed_all, 0, 2 * RANK, "normed_side")
    offsets = pairs(last - 4, last)
    blocks = [at_z(offset) for offset in offsets] + [low[last], high[last]]
    plan = dict(
        n_z=n_z,
        rows=rows,
        blocks=[(offset, 0) for offset in offsets] + [(last, 0), (last, half)],
        chunks=[slice(0, 4), slice(4, 8), slice(8, 10)],
    )
    sums, mids = pl.pallas_call(
        functools.partial(hidden_kernel, plan),
        out_shape=(
            jax.ShapeDtypeStruct((sequences, 3 * RANK, hidden), F32),
            jax.ShapeDtypeStruct((8 * n_tensor, tokens), F32),
        ),
        in_specs=[smem] + [hbm] * (len(blocks) + 4) + [vmem] * 4,
        out_specs=(hbm, vmem),
        scratch_shapes=[
            pltpu.VMEM((tokens, hidden), F32),
            pltpu.VMEM((tokens, hidden), F32),
            pltpu.VMEM((tokens, hidden), BF16),
            pltpu.VMEM((tokens, hidden), BF16),
            pltpu.VMEM((tokens, hidden), F32),
            pltpu.VMEM((tokens, hidden), F32),
            pltpu.VMEM((sequences, 3 * RANK, hidden), F32),
        ]
        + scratch((len(offsets) + 1) * rows, 4 * len(blocks) + 12),
        compiler_params=params,
        name="hidden_side",
    )(
        spot,
        gradient,
        *blocks,
        total,
        gate_preactivation,
        upward_preactivation,
        adapter_hidden_factors.reshape(3 * RANK, hidden),
        in_t,
        lora,
        lora_t,
    )

    pieces = lax.all_to_all(mids.reshape(n_tensor, 8, tokens), tensor_axes, 0, 0)
    piece = jnp.sum(pieces, axis=0)
    mids = lax.all_to_all(
        jnp.broadcast_to(piece, (n_tensor,) + piece.shape), tensor_axes, 0, 0
    ).reshape(8 * n_tensor, tokens)

    lanes = (local_width + hidden) // 128
    tiles = 6 * lanes
    padded = -(-tiles // 8) * 8
    out = pl.pallas_call(
        clip_kernel,
        out_shape=jax.ShapeDtypeStruct((padded, 8, 128), F32),
        in_specs=[smem] + [vmem] * 6,
        out_specs=vmem,
        scratch_shapes=[pltpu.VMEM((3 * RANK, local_width), F32)],
        compiler_params=params,
        name="clip_side",
    )(
        clipping_limit,
        mids,
        sums,
        normed,
        output_gradient,
        normed_gram,
        gradient_gram,
    )

    n_y = sizes["y"]
    share = jnp.sum(lax.all_to_all(out.reshape(n_y, -1, 128), "y", 0, 0), axis=0)
    share = jnp.sum(lax.all_to_all(share.reshape(n_z, -1, 128), z_axes, 0, 0), axis=0)
    share = lax.all_to_all(
        jnp.broadcast_to(share, (n_z,) + share.shape), z_axes, 0, 0
    ).reshape(-1, 128)
    whole = lax.all_to_all(jnp.broadcast_to(share, (n_y,) + share.shape), "y", 0, 0)
    total = (
        whole.reshape(padded, 8, 128)[:tiles]
        .reshape(6, lanes, 8, 128)
        .transpose(0, 2, 1, 3)
        .reshape(3, RANK, lanes * 128)
    )
    count = sequences * n_z * sizes["y"]
    bound = clipping_limit[0]
    wide = total[:, :, :local_width]
    inner = total[:, :, local_width : local_width + hidden]
    return (
        (wide + bound * width_noise_draw) / count,
        (inner + bound * hidden_noise_draw) / count,
    )


def solution(mesh):
    names = ("z", "y", "x", "c")
    extents = (16, 4, 4, 2)
    fine = Mesh(mesh.devices.reshape(extents), names)
    dp, tensor = ("z", "y"), ("x", "c")
    placed = (
        P(dp, tensor),
        P(dp, tensor),
        P(dp, tensor),
        P(dp, tensor),
        P(tensor, dp),
        P(),
        P(None, None, tensor),
        P(),
        P(None, None, tensor),
        P(None, None, tensor),
    )
    return jax.shard_map(
        functools.partial(per_device, dict(zip(names, extents, strict=True))),
        mesh=fine,
        in_specs=placed,
        out_specs=(P(None, None, tensor), P(None, None, tensor)),
        check_vma=False,
    )
```

```python
import functools

import jax
import jax.numpy as jnp
from jax import lax
from jax.experimental import pallas as pl
from jax.experimental.pallas import tpu as pltpu
from jax.sharding import Mesh
from jax.sharding import PartitionSpec as P

SEQUENCE_TOKENS = 128
RANK = 16
SCALE = 2.0
F32 = jnp.float32
BF16 = jnp.bfloat16


def contract(left, right, left_dim, right_dim):
    return lax.dot_general(
        left, right, (((left_dim,), (right_dim,)), ((), ())), preferred_element_type=F32
    )


def column_tiles(hidden, step, tile):
    whole = hidden // step

    def body(i, carry):
        tile(i, pl.multiple_of(i * step, step), step)
        return carry

    lax.fori_loop(0, whole, body, 0)
    spans = [(i * step, step) for i in range(whole)]
    if hidden > whole * step:
        spans.append((whole * step, hidden - whole * step))
        tile(whole, *spans[-1])
    return spans


def copy_rows(source, target, sems, at, parts):
    rows = source.shape[0] // parts
    copies = []
    for i in range(parts):
        span = pl.ds(i * rows, rows)
        copies.append(
            pltpu.make_async_copy(source.at[span, :], target.at[span, :], sems.at[at + i])
        )
    return copies


def locate(spot_ref, n_x):
    x, core = spot_ref[1], spot_ref[2]
    other = 1 - core
    near = lax.rem(x + jnp.where(core == 0, n_x - 1, 1), n_x) * 2
    beyond = lax.rem(x + jnp.where(core == 0, 1, n_x - 1), n_x) * 2
    across = lax.rem(x + 2, n_x) * 2
    return [
        (0, 0, 2 * x + core),
        (1, 0, 2 * x + other),
        (2, 0, near + core),
        (2, 1, near + other),
        (3, 0, across + core),
        (4, 0, beyond + other),
        (4, 1, beyond + core),
        (5, 0, across + other),
    ]


def fetch_blocks(plan, spot_ref, piece_refs, block_refs, left, right, sems):
    n_z, rows, tokens = plan["n_z"], plan["rows"], left.shape[0]
    count = left.shape[1] // rows

    def columns(array, piece, half, i):
        return pltpu.make_async_copy(
            piece_refs[array].at[pl.ds(2 * tokens * piece, tokens), pl.ds(half * rows, rows)],
            left.at[:, pl.ds(pl.multiple_of(i * rows, rows), rows)],
            sems.at[i],
        )

    halves = piece_refs[0].shape[1] // rows
    for array, piece, rank in locate(spot_ref, plan["n_x"]):
        for half in range(halves):
            at = rank * halves + half
            i = lax.rem(at - spot_ref[0] - plan["first"] + 2 * n_z, n_z)

            @pl.when(i < count)
            def _(array=array, piece=piece, half=half, i=i):
                columns(array, piece, half, i).start()

    waits = [[columns(0, 0, 0, i)] for i in range(count)]
    sem = count
    for (offset, first), block in zip(plan["blocks"], block_refs, strict=True):
        i = offset - plan["first"]
        span = pl.ds(i * rows + first, block.shape[0])
        copies = copy_rows(block, right.at[span, :], sems, sem, 2)
        sem += 2
        for copy in copies:
            copy.start()
        waits[i] += copies
    return waits


def side_kernel(n_x, first, count, which, spot_ref, *refs):
    piece_refs = refs[:6]
    factors_ref, projected_ref, turned_ref, gram_ref, total, rows_ref, sems = refs[6:]
    size = SEQUENCE_TOKENS
    tokens, width = rows_ref.shape[1:]
    places = locate(spot_ref, n_x)
    copies = []
    for i, (array, piece, _) in enumerate(places):
        span = pl.ds((2 * piece + which) * tokens, tokens)
        copies.append(
            pltpu.make_async_copy(piece_refs[array].at[span, :], rows_ref.at[i], sems.at[i])
        )
    for copy in copies:
        copy.start()
    total[...] = jnp.zeros_like(total)
    for i, (_, _, rank) in enumerate(places):
        copies[i].wait()
        columns = pl.ds(pl.multiple_of(rank * width, width), width)
        factors = factors_ref[first : first + count, columns]
        for p in range(total.shape[0]):
            rows = rows_ref[i, 2 * size * p : 2 * size * (p + 1), :]
            total[p] += contract(jnp.concatenate([rows, factors], axis=0), rows, 1, 1)
    for p in range(total.shape[0]):
        gram_ref[2 * p] = total[p, :size, :size]
        gram_ref[2 * p + 1] = total[p, size : 2 * size, size:]
        span = slice(2 * size * p, 2 * size * (p + 1))
        projected = total[p, 2 * size :]
        projected_ref[:, span] = projected.astype(BF16)
        turned_ref[span, :] = projected.T.astype(BF16)


def part_kernel(plan, spot_ref, *refs):
    n_blocks = len(plan["blocks"])
    piece_refs, refs = refs[:6], refs[6:]
    block_refs = refs[:n_blocks]
    out_ref, total, left, right, sems, out_sems = refs[n_blocks:]
    waits = fetch_blocks(plan, spot_ref, piece_refs, block_refs, left, right, sems)
    for copy in sum(waits, []):
        copy.wait()

    writes = []
    hidden = total.shape[1]
    for i, start in enumerate(range(0, hidden, 512)):
        cols = slice(start, min(start + 512, hidden))
        total[:, cols] = jnp.dot(left[...], right[:, cols], preferred_element_type=F32)
        write = pltpu.make_async_copy(total.at[:, cols], out_ref.at[:, cols], out_sems.at[i])
        write.start()
        writes.append(write)
    for write in writes:
        write.wait()


def hidden_kernel(plan, spot_ref, *refs):
    n_blocks = len(plan["blocks"])
    piece_refs, refs = refs[:6], refs[6:]
    block_refs = refs[:n_blocks]
    (before_hbm, gate_hbm, up_hbm, factors_ref, in_ref, lora_ref, lora_t_ref) = refs[
        n_blocks : n_blocks + 7
    ]
    sums_hbm, mids_ref, total, before_ref, gate_ref, up_ref, silu_ref, scaled_ref, sums_ref = refs[
        n_blocks + 7 : -4
    ]
    left_rows, right_rows, sems, out_sems = refs[-4:]
    tokens, hidden = gate_ref.shape
    sequences = tokens // SEQUENCE_TOKENS
    at = sems.shape[0] - 12
    activations = copy_rows(gate_hbm, gate_ref, sems, at, 4)
    activations += copy_rows(up_hbm, up_ref, sems, at + 4, 4)
    running = copy_rows(before_hbm, before_ref, sems, at + 8, 4)
    for copy in activations:
        copy.start()
    waits = fetch_blocks(plan, spot_ref, piece_refs, block_refs, left_rows, right_rows, sems)
    for copy in running:
        copy.start()
    mids_ref[...] = jnp.zeros_like(mids_ref)

    def adapters(j, e, rows, cols, left, right):
        part = slice(j * RANK, (j + 1) * RANK)
        sums_ref[e, part, cols] = SCALE * jnp.dot(left, right, preferred_element_type=F32)
        mids_ref[part, rows] += contract(factors_ref[part, cols], right, 1, 1)

    def each(i, start, width, body):
        for e in range(sequences):
            body(e, slice(e * SEQUENCE_TOKENS, (e + 1) * SEQUENCE_TOKENS), pl.ds(start, width))

    def forward(e, rows, cols):
        gate = gate_ref[rows, cols].astype(F32)
        up = up_ref[rows, cols].astype(F32)
        sigmoid = jax.nn.sigmoid(gate)
        silu = gate * sigmoid
        slope = sigmoid * (1.0 + gate * (1.0 - sigmoid))
        silu_ref[rows, cols] = silu
        scaled_ref[rows, cols] = up * slope
        adapters(2, e, rows, cols, lora_t_ref[:, rows], (silu * up).astype(BF16))

    def backward(e, rows, cols):
        hidden_grad = (
            total[rows, cols]
            + before_ref[rows, cols]
            + SCALE
            * jnp.dot(lora_ref[rows, :], factors_ref[2 * RANK :, cols], preferred_element_type=F32)
        )
        gate_grad = (hidden_grad * scaled_ref[rows, cols]).astype(BF16)
        adapters(0, e, rows, cols, in_ref[:RANK, rows], gate_grad)
        up_grad = (hidden_grad * silu_ref[rows, cols]).astype(BF16)
        adapters(1, e, rows, cols, in_ref[RANK:, rows], up_grad)

    def write(i, cols):
        return pltpu.make_async_copy(
            sums_ref.at[:, :, cols], sums_hbm.at[:, :, cols], out_sems.at[i]
        )

    def last_tile(i, start, width):
        each(i, start, width, backward)
        write(i, pl.ds(start, width)).start()

    for copy in activations:
        copy.wait()
    column_tiles(hidden, hidden, functools.partial(each, body=forward))
    for start, end in plan["chunks"]:
        for copy in sum(waits[start:end], []):
            copy.wait()
        span = slice(start * plan["rows"], end * plan["rows"])
        product = jnp.dot(left_rows[:, span], right_rows[span, :], preferred_element_type=F32)
        total[...] = product if start == 0 else total[...] + product
    for copy in running:
        copy.wait()
    spans = column_tiles(hidden, hidden, last_tile)
    for e in range(sequences):
        square = sums_ref[e] * sums_ref[e]
        line = jnp.sum(jnp.sum(square, axis=0, keepdims=True), axis=1, keepdims=True)
        mids_ref[3 * RANK + e : 3 * RANK + e + 1, :] = jnp.broadcast_to(line, (1, tokens))
    for i, (start, width) in enumerate(spans):
        write(i, pl.ds(start, width)).wait()


def quadratic(left, gram):
    product = jnp.zeros((left.shape[0], gram.shape[1]), F32)
    rest = gram
    for _ in range(3):
        part = rest.astype(BF16)
        product = product + jnp.dot(left, part, preferred_element_type=F32)
        rest = rest - part.astype(F32)
    return product * left.astype(F32)


def total_of(values):
    return jnp.sum(jnp.sum(values, axis=0, keepdims=True), axis=1, keepdims=True)


def clip_kernel(
    clip_ref,
    mids_ref,
    sums_ref,
    normed_ref,
    gradient_ref,
    normed_gram_ref,
    gradient_gram_ref,
    out_ref,
    wide,
):
    sequences, _, hidden = sums_ref.shape
    local = wide.shape[1]
    bound = clip_ref[0]
    weights = []
    for e in range(sequences):
        rows = slice(e * SEQUENCE_TOKENS, (e + 1) * SEQUENCE_TOKENS)
        mids = mids_ref[: 3 * RANK, rows].astype(BF16)
        square = total_of(quadratic(mids[: 2 * RANK], normed_gram_ref[e])) + total_of(
            quadratic(mids[2 * RANK :], gradient_gram_ref[e])
        )
        square = SCALE * SCALE * jnp.maximum(square, 0.0)
        square = square + mids_ref[3 * RANK + e : 3 * RANK + e + 1, 0:1]
        weight = bound / jnp.maximum(jnp.sqrt(square), bound)
        weights.append(weight)
        first = weight * (
            SCALE * jnp.dot(mids[: 2 * RANK], normed_ref[rows, :], preferred_element_type=F32)
        )
        second = weight * (
            SCALE * jnp.dot(mids[2 * RANK :], gradient_ref[rows, :], preferred_element_type=F32)
        )
        if e == 0:
            wide[: 2 * RANK] = first
            wide[2 * RANK :] = second
        else:
            wide[: 2 * RANK] += first
            wide[2 * RANK :] += second
    lanes = (local + hidden) // 128
    for t in range(out_ref.shape[0]):
        r, c = divmod(t, lanes)
        rows = slice(8 * r, 8 * r + 8)
        at = c * 128
        if r >= 3 * RANK // 8:
            value = jnp.zeros((8, 128), F32)
        elif at < local:
            value = wide[rows, at : at + 128]
        else:
            at = at - local
            value = weights[0] * sums_ref[0, rows, at : at + 128]
            for e in range(1, sequences):
                value = value + weights[e] * sums_ref[e, rows, at : at + 128]
        out_ref[t] = value


def ring(size, by):
    return [(i, (i + by) % size) for i in range(size)]


def per_device(
    sizes,
    normed,
    output_gradient,
    gate_preactivation,
    upward_preactivation,
    frozen_down_weight,
    adapter_width_factors,
    adapter_hidden_factors,
    clipping_limit,
    width_noise_draw,
    hidden_noise_draw,
):
    tokens, local_width = normed.shape
    hidden = gate_preactivation.shape[1]
    sequences = tokens // SEQUENCE_TOKENS
    n_z = sizes["z"]
    n_tensor = sizes["x"] * sizes["c"]
    z_axes, tensor_axes = "z", ("x", "c")
    spot = jnp.stack([lax.axis_index(axis) for axis in ("z", "x", "c")]).astype(jnp.int32)

    n_x = sizes["x"]
    swap = [(0, 1), (1, 0)]
    around = [(2 * i, 2 * ((i + 1) % n_x)) for i in range(n_x)]
    around += [(2 * i + 1, 2 * ((i - 1) % n_x) + 1) for i in range(n_x)]
    own = jnp.concatenate([output_gradient, normed], axis=0)
    partner = lax.ppermute(own, "c", swap)
    near = lax.ppermute(jnp.concatenate([own, partner], axis=0), tensor_axes, around)
    across = lax.ppermute(near[: 2 * tokens], tensor_axes, around)
    beyond = lax.ppermute(near, "c", swap)
    across_partner = lax.ppermute(across, "c", swap)
    pieces = (own, partner, near, across, beyond, across_partner)
    block = lax.all_gather(frozen_down_weight.T, "y", axis=0, tiled=True)

    rows = block.shape[0]
    half = rows // 2
    vmem = pl.BlockSpec(memory_space=pltpu.VMEM)
    smem = pl.BlockSpec(memory_space=pltpu.SMEM)
    hbm = pl.BlockSpec(memory_space=pl.ANY)
    params = pltpu.CompilerParams(vmem_limit_bytes=60 * 2**20)

    low, high = {0: block}, {0: block}

    def step(k, low_from, high_from):
        low[k] = lax.ppermute(low_from, z_axes, ring(n_z, 1))
        high[k] = lax.ppermute(high_from, z_axes, ring(n_z, -1))

    def side(which, first, count, name):
        width = n_tensor * local_width
        return pl.pallas_call(
            functools.partial(side_kernel, n_x, first, count, which),
            out_shape=(
                jax.ShapeDtypeStruct((count, tokens), BF16),
                jax.ShapeDtypeStruct((tokens, count), BF16),
                jax.ShapeDtypeStruct((sequences, SEQUENCE_TOKENS, SEQUENCE_TOKENS), F32),
            ),
            in_specs=[smem] + [hbm] * len(pieces) + [vmem],
            out_specs=(vmem, vmem, vmem),
            scratch_shapes=[
                pltpu.VMEM(
                    (sequences // 2, 2 * SEQUENCE_TOKENS + count, 2 * SEQUENCE_TOKENS), F32
                ),
                pltpu.VMEM((n_tensor, tokens, local_width), BF16),
                pltpu.SemaphoreType.DMA((n_tensor,)),
            ],
            compiler_params=params,
            cost_estimate=pl.CostEstimate(
                flops=2 * tokens * width * (128 + count),
                bytes_accessed=5 * 2**20,
                transcendentals=0,
            ),
            name=name,
        )(spot, *pieces, adapter_width_factors.reshape(3 * RANK, width))

    def scratch(n_rows, n_sems):
        return [
            pltpu.VMEM((tokens, n_rows), BF16),
            pltpu.VMEM((n_rows, hidden), BF16),
            pltpu.SemaphoreType.DMA((n_sems,)),
            pltpu.SemaphoreType.DMA((-(-hidden // 256),)),
        ]

    def at_z(offset):
        return (low if offset < 0 else high)[abs(offset)]

    def part(offsets):
        blocks = [at_z(offset) for offset in offsets]
        plan = dict(
            n_z=n_z,
            n_x=n_x,
            rows=rows,
            first=offsets[0],
            blocks=[(offset, 0) for offset in offsets],
        )
        n = len(blocks)
        return pl.pallas_call(
            functools.partial(part_kernel, plan),
            out_shape=jax.ShapeDtypeStruct((tokens, hidden), F32),
            in_specs=[smem] + [hbm] * (len(pieces) + n),
            out_specs=hbm,
            scratch_shapes=[pltpu.VMEM((tokens, hidden), F32)] + scratch(n * rows, 3 * n),
            compiler_params=params,
            cost_estimate=pl.CostEstimate(
                flops=2 * tokens * n * rows * hidden,
                bytes_accessed=6 * 2**20,
                transcendentals=0,
            ),
            name="part_product",
        )(spot, *pieces, *blocks)

    def after(value, other):
        return lax.optimization_barrier((value, other))[0]

    last = n_z // 2
    for k in range(1, last - 1):
        step(k, low[k - 1], high[k - 1])
    split = last - 4
    total = part(list(range(1 - split, split)))
    at = last - 2
    step(at + 1, after(low[at], total), after(high[at], total))
    lora_t, lora, gradient_gram = side(0, 2 * RANK, RANK, "gradient_side")
    at = last - 1
    low_in, high_in = after(low[at], lora_t), after(high[at], lora_t)
    step(last, low_in[:half], high_in[half:])
    in_t, _, normed_gram = side(1, 0, 2 * RANK, "normed_side")
    ahead, behind = list(range(split, last)), list(range(last + 1, n_z - split + 1))
    blocks = [high[k] for k in ahead] + [low[last], high[last]] + [low[n_z - k] for k in behind]
    plan = dict(
        n_z=n_z,
        n_x=n_x,
        rows=rows,
        first=split,
        blocks=[(k, 0) for k in ahead] + [(last, 0), (last, half)] + [(k, 0) for k in behind],
        chunks=[(0, last - split), (last - split, n_z - 2 * split + 1)],
    )
    n_offsets = n_z - 2 * split + 1
    sums, mids = pl.pallas_call(
        functools.partial(hidden_kernel, plan),
        out_shape=(
            jax.ShapeDtypeStruct((sequences, 3 * RANK, hidden), F32),
            jax.ShapeDtypeStruct((8 * n_tensor, tokens), F32),
        ),
        in_specs=[smem] + [hbm] * (len(pieces) + len(blocks) + 3) + [vmem] * 4,
        out_specs=(hbm, vmem),
        scratch_shapes=[
            pltpu.VMEM((tokens, hidden), F32),
            pltpu.VMEM((tokens, hidden), F32),
            pltpu.VMEM((tokens, hidden), BF16),
            pltpu.VMEM((tokens, hidden), BF16),
            pltpu.VMEM((tokens, hidden), F32),
            pltpu.VMEM((tokens, hidden), F32),
            pltpu.VMEM((sequences, 3 * RANK, hidden), F32),
        ]
        + scratch(n_offsets * rows, n_offsets + 2 * len(blocks) + 12),
        compiler_params=params,
        name="hidden_side",
    )(
        spot,
        *pieces,
        *blocks,
        total,
        gate_preactivation,
        upward_preactivation,
        adapter_hidden_factors.reshape(3 * RANK, hidden),
        in_t,
        lora,
        lora_t,
    )

    pieces = lax.all_to_all(mids.reshape(n_tensor, 8, tokens), tensor_axes, 0, 0)
    piece = jnp.sum(pieces, axis=0)
    mids = lax.all_to_all(
        jnp.broadcast_to(piece, (n_tensor,) + piece.shape), tensor_axes, 0, 0
    ).reshape(8 * n_tensor, tokens)

    lanes = (local_width + hidden) // 128
    tiles = 6 * lanes
    padded = -(-tiles // 8) * 8
    out = pl.pallas_call(
        clip_kernel,
        out_shape=jax.ShapeDtypeStruct((padded, 8, 128), F32),
        in_specs=[smem] + [vmem] * 6,
        out_specs=vmem,
        scratch_shapes=[pltpu.VMEM((3 * RANK, local_width), F32)],
        compiler_params=params,
        name="clip_side",
    )(
        clipping_limit,
        mids,
        sums,
        normed,
        output_gradient,
        normed_gram,
        gradient_gram,
    )

    n_y = sizes["y"]
    share = jnp.sum(lax.all_to_all(out.reshape(n_y, -1, 128), "y", 0, 0), axis=0)
    share = jnp.sum(lax.all_to_all(share.reshape(n_z, -1, 128), z_axes, 0, 0), axis=0)
    share = lax.all_to_all(
        jnp.broadcast_to(share, (n_z,) + share.shape), z_axes, 0, 0
    ).reshape(-1, 128)
    whole = lax.all_to_all(jnp.broadcast_to(share, (n_y,) + share.shape), "y", 0, 0)
    total = (
        whole.reshape(padded, 8, 128)[:tiles]
        .reshape(6, lanes, 8, 128)
        .transpose(0, 2, 1, 3)
        .reshape(3, RANK, lanes * 128)
    )
    count = sequences * n_z * sizes["y"]
    bound = clipping_limit[0]
    wide = total[:, :, :local_width]
    inner = total[:, :, local_width : local_width + hidden]
    return (
        (wide + bound * width_noise_draw) / count,
        (inner + bound * hidden_noise_draw) / count,
    )


def solution(mesh):
    names = ("z", "y", "x", "c")
    extents = (16, 4, 4, 2)
    fine = Mesh(mesh.devices.reshape(extents), names)
    dp, tensor = ("z", "y"), ("x", "c")
    placed = (
        P(dp, tensor),
        P(dp, tensor),
        P(dp, tensor),
        P(dp, tensor),
        P(tensor, dp),
        P(),
        P(None, None, tensor),
        P(),
        P(None, None, tensor),
        P(None, None, tensor),
    )
    return jax.shard_map(
        functools.partial(per_device, dict(zip(names, extents, strict=True))),
        mesh=fine,
        in_specs=placed,
        out_specs=(P(None, None, tensor), P(None, None, tensor)),
        check_vma=False,
    )
```

```python
import functools

import jax
import jax.numpy as jnp
from jax import lax
from jax.experimental import pallas as pl
from jax.experimental.pallas import tpu as pltpu
from jax.sharding import Mesh
from jax.sharding import PartitionSpec as P

SEQUENCE_TOKENS = 128
RANK = 16
SCALE = 2.0
F32 = jnp.float32
BF16 = jnp.bfloat16


def contract(left, right, left_dim, right_dim):
    return lax.dot_general(
        left, right, (((left_dim,), (right_dim,)), ((), ())), preferred_element_type=F32
    )


def column_tiles(hidden, step, tile):
    whole = hidden // step

    def body(i, carry):
        tile(i, pl.multiple_of(i * step, step), step)
        return carry

    lax.fori_loop(0, whole, body, 0)
    spans = [(i * step, step) for i in range(whole)]
    if hidden > whole * step:
        spans.append((whole * step, hidden - whole * step))
        tile(whole, *spans[-1])
    return spans


def copy_rows(source, target, sems, at, parts):
    rows = source.shape[0] // parts
    copies = []
    for i in range(parts):
        span = pl.ds(i * rows, rows)
        copies.append(
            pltpu.make_async_copy(source.at[span, :], target.at[span, :], sems.at[at + i])
        )
    return copies


def locate(spot_ref, n_x):
    x, core = spot_ref[1], spot_ref[2]
    other = 1 - core
    near = lax.rem(x + jnp.where(core == 0, n_x - 1, 1), n_x) * 2
    beyond = lax.rem(x + jnp.where(core == 0, 1, n_x - 1), n_x) * 2
    across = lax.rem(x + 2, n_x) * 2
    return [
        (0, 0, 2 * x + core),
        (1, 0, 2 * x + other),
        (2, 0, near + core),
        (2, 1, near + other),
        (3, 0, across + core),
        (4, 0, beyond + other),
        (4, 1, beyond + core),
        (5, 0, across + other),
    ]


def fetch_blocks(plan, spot_ref, piece_refs, block_refs, left, right, sems):
    n_z, rows, tokens = plan["n_z"], plan["rows"], left.shape[0]
    count = left.shape[1] // rows

    def columns(array, piece, half, i):
        return pltpu.make_async_copy(
            piece_refs[array].at[pl.ds(2 * tokens * piece, tokens), pl.ds(half * rows, rows)],
            left.at[:, pl.ds(pl.multiple_of(i * rows, rows), rows)],
            sems.at[i],
        )

    halves = piece_refs[0].shape[1] // rows
    for array, piece, rank in locate(spot_ref, plan["n_x"]):
        for half in range(halves):
            at = rank * halves + half
            i = lax.rem(at - spot_ref[0] - plan["first"] + 2 * n_z, n_z)

            @pl.when(i < count)
            def _(array=array, piece=piece, half=half, i=i):
                columns(array, piece, half, i).start()

    waits = [[columns(0, 0, 0, i)] for i in range(count)]
    sem = count
    column = plan["column"]
    piece = rows // len(column)
    for (offset, first), block in zip(plan["blocks"], block_refs, strict=True):
        i = offset - plan["first"]
        for row in range(0, block.shape[0], piece):
            turn = spot_ref[3] + column[(first + row) // piece] + len(column)
            to = i * rows + lax.rem(turn, len(column)) * piece
            copy = pltpu.make_async_copy(
                block.at[pl.ds(row, piece), :],
                right.at[pl.ds(pl.multiple_of(to, piece), piece), :],
                sems.at[sem],
            )
            sem += 1
            copy.start()
            waits[i].append(copy)
    return waits


def side_kernel(n_x, first, count, which, spot_ref, *refs):
    piece_refs = refs[:6]
    factors_ref, projected_ref, turned_ref, gram_ref, total, rows_ref, sems = refs[6:]
    size = SEQUENCE_TOKENS
    tokens, width = rows_ref.shape[1:]
    places = locate(spot_ref, n_x)
    copies = []
    for i, (array, piece, _) in enumerate(places):
        span = pl.ds((2 * piece + which) * tokens, tokens)
        copies.append(
            pltpu.make_async_copy(piece_refs[array].at[span, :], rows_ref.at[i], sems.at[i])
        )
    for copy in copies:
        copy.start()
    total[...] = jnp.zeros_like(total)
    for i, (_, _, rank) in enumerate(places):
        copies[i].wait()
        columns = pl.ds(pl.multiple_of(rank * width, width), width)
        factors = factors_ref[first : first + count, columns]
        for p in range(total.shape[0]):
            rows = rows_ref[i, 2 * size * p : 2 * size * (p + 1), :]
            total[p] += contract(jnp.concatenate([rows, factors], axis=0), rows, 1, 1)
    for p in range(total.shape[0]):
        gram_ref[2 * p] = total[p, :size, :size]
        gram_ref[2 * p + 1] = total[p, size : 2 * size, size:]
        span = slice(2 * size * p, 2 * size * (p + 1))
        projected = total[p, 2 * size :]
        projected_ref[:, span] = projected.astype(BF16)
        turned_ref[span, :] = projected.T.astype(BF16)


def part_kernel(plan, spot_ref, *refs):
    n_blocks = len(plan["blocks"])
    piece_refs, refs = refs[:6], refs[6:]
    block_refs = refs[:n_blocks]
    out_ref, total, left, right, sems, out_sems = refs[n_blocks:]
    waits = fetch_blocks(plan, spot_ref, piece_refs, block_refs, left, right, sems)
    for copy in sum(waits, []):
        copy.wait()

    writes = []
    hidden = total.shape[1]
    for i, start in enumerate(range(0, hidden, 512)):
        cols = slice(start, min(start + 512, hidden))
        total[:, cols] = jnp.dot(left[...], right[:, cols], preferred_element_type=F32)
        write = pltpu.make_async_copy(total.at[:, cols], out_ref.at[:, cols], out_sems.at[i])
        write.start()
        writes.append(write)
    for write in writes:
        write.wait()


def hidden_kernel(plan, spot_ref, *refs):
    n_blocks = len(plan["blocks"])
    piece_refs, refs = refs[:6], refs[6:]
    block_refs = refs[:n_blocks]
    (before_hbm, gate_hbm, up_hbm, factors_ref, in_ref, lora_ref, lora_t_ref) = refs[
        n_blocks : n_blocks + 7
    ]
    sums_hbm, mids_ref, total, before_ref, gate_ref, up_ref, silu_ref, scaled_ref, sums_ref = refs[
        n_blocks + 7 : -4
    ]
    left_rows, right_rows, sems, out_sems = refs[-4:]
    tokens, hidden = gate_ref.shape
    sequences = tokens // SEQUENCE_TOKENS
    at = sems.shape[0] - 12
    activations = copy_rows(gate_hbm, gate_ref, sems, at, 4)
    activations += copy_rows(up_hbm, up_ref, sems, at + 4, 4)
    running = copy_rows(before_hbm, before_ref, sems, at + 8, 4)
    for copy in activations:
        copy.start()
    waits = fetch_blocks(plan, spot_ref, piece_refs, block_refs, left_rows, right_rows, sems)
    for copy in running:
        copy.start()
    mids_ref[...] = jnp.zeros_like(mids_ref)

    def adapters(j, e, rows, cols, left, right):
        part = slice(j * RANK, (j + 1) * RANK)
        sums_ref[e, part, cols] = SCALE * jnp.dot(left, right, preferred_element_type=F32)
        mids_ref[part, rows] += contract(factors_ref[part, cols], right, 1, 1)

    def each(i, start, width, body):
        for e in range(sequences):
            body(e, slice(e * SEQUENCE_TOKENS, (e + 1) * SEQUENCE_TOKENS), pl.ds(start, width))

    def forward(e, rows, cols):
        gate = gate_ref[rows, cols].astype(F32)
        up = up_ref[rows, cols].astype(F32)
        sigmoid = jax.nn.sigmoid(gate)
        silu = gate * sigmoid
        slope = sigmoid * (1.0 + gate * (1.0 - sigmoid))
        silu_ref[rows, cols] = silu
        scaled_ref[rows, cols] = up * slope
        adapters(2, e, rows, cols, lora_t_ref[:, rows], (silu * up).astype(BF16))

    def backward(e, rows, cols):
        hidden_grad = (
            total[rows, cols]
            + before_ref[rows, cols]
            + SCALE
            * jnp.dot(lora_ref[rows, :], factors_ref[2 * RANK :, cols], preferred_element_type=F32)
        )
        gate_grad = (hidden_grad * scaled_ref[rows, cols]).astype(BF16)
        adapters(0, e, rows, cols, in_ref[:RANK, rows], gate_grad)
        up_grad = (hidden_grad * silu_ref[rows, cols]).astype(BF16)
        adapters(1, e, rows, cols, in_ref[RANK:, rows], up_grad)

    def write(i, cols):
        return pltpu.make_async_copy(
            sums_ref.at[:, :, cols], sums_hbm.at[:, :, cols], out_sems.at[i]
        )

    def last_tile(i, start, width):
        each(i, start, width, backward)
        write(i, pl.ds(start, width)).start()

    for copy in activations:
        copy.wait()
    column_tiles(hidden, hidden, functools.partial(each, body=forward))
    for start, end in plan["chunks"]:
        for copy in sum(waits[start:end], []):
            copy.wait()
        span = slice(start * plan["rows"], end * plan["rows"])
        product = jnp.dot(left_rows[:, span], right_rows[span, :], preferred_element_type=F32)
        total[...] = product if start == 0 else total[...] + product
    for copy in running:
        copy.wait()
    spans = column_tiles(hidden, hidden, last_tile)
    for e in range(sequences):
        square = sums_ref[e] * sums_ref[e]
        line = jnp.sum(jnp.sum(square, axis=0, keepdims=True), axis=1, keepdims=True)
        mids_ref[3 * RANK + e : 3 * RANK + e + 1, :] = jnp.broadcast_to(line, (1, tokens))
    for i, (start, width) in enumerate(spans):
        write(i, pl.ds(start, width)).wait()


def quadratic(left, gram):
    product = jnp.zeros((left.shape[0], gram.shape[1]), F32)
    rest = gram
    for _ in range(3):
        part = rest.astype(BF16)
        product = product + jnp.dot(left, part, preferred_element_type=F32)
        rest = rest - part.astype(F32)
    return product * left.astype(F32)


def total_of(values):
    return jnp.sum(jnp.sum(values, axis=0, keepdims=True), axis=1, keepdims=True)


def clip_kernel(
    clip_ref,
    mids_ref,
    sums_ref,
    normed_ref,
    gradient_ref,
    normed_gram_ref,
    gradient_gram_ref,
    out_ref,
    wide,
):
    sequences, _, hidden = sums_ref.shape
    local = wide.shape[1]
    bound = clip_ref[0]
    weights = []
    for e in range(sequences):
        rows = slice(e * SEQUENCE_TOKENS, (e + 1) * SEQUENCE_TOKENS)
        mids = mids_ref[: 3 * RANK, rows].astype(BF16)
        square = total_of(quadratic(mids[: 2 * RANK], normed_gram_ref[e])) + total_of(
            quadratic(mids[2 * RANK :], gradient_gram_ref[e])
        )
        square = SCALE * SCALE * jnp.maximum(square, 0.0)
        square = square + mids_ref[3 * RANK + e : 3 * RANK + e + 1, 0:1]
        weight = bound / jnp.maximum(jnp.sqrt(square), bound)
        weights.append(weight)
        first = weight * (
            SCALE * jnp.dot(mids[: 2 * RANK], normed_ref[rows, :], preferred_element_type=F32)
        )
        second = weight * (
            SCALE * jnp.dot(mids[2 * RANK :], gradient_ref[rows, :], preferred_element_type=F32)
        )
        if e == 0:
            wide[: 2 * RANK] = first
            wide[2 * RANK :] = second
        else:
            wide[: 2 * RANK] += first
            wide[2 * RANK :] += second
    lanes = (local + hidden) // 128
    for t in range(out_ref.shape[0]):
        r, c = divmod(t, lanes)
        rows = slice(8 * r, 8 * r + 8)
        at = c * 128
        if r >= 3 * RANK // 8:
            value = jnp.zeros((8, 128), F32)
        elif at < local:
            value = wide[rows, at : at + 128]
        else:
            at = at - local
            value = weights[0] * sums_ref[0, rows, at : at + 128]
            for e in range(1, sequences):
                value = value + weights[e] * sums_ref[e, rows, at : at + 128]
        out_ref[t] = value


def after(value, *others):
    return lax.optimization_barrier((value, *others))[0]


def ring(size, by):
    return [(i, (i + by) % size) for i in range(size)]


def per_device(
    sizes,
    normed,
    output_gradient,
    gate_preactivation,
    upward_preactivation,
    frozen_down_weight,
    adapter_width_factors,
    adapter_hidden_factors,
    clipping_limit,
    width_noise_draw,
    hidden_noise_draw,
):
    tokens, local_width = normed.shape
    hidden = gate_preactivation.shape[1]
    sequences = tokens // SEQUENCE_TOKENS
    n_z = sizes["z"]
    n_tensor = sizes["x"] * sizes["c"]
    z_axes, tensor_axes = "z", ("x", "c")
    spot = jnp.stack([lax.axis_index(axis) for axis in ("z", "x", "c", "y")]).astype(jnp.int32)

    shard = frozen_down_weight.T
    n_y = sizes["y"]
    column = [0, -1, 1, 2]
    others = [lax.ppermute(shard, "y", ring(n_y, -by)) for by in column[1:]]
    block = jnp.concatenate([shard, *others], axis=0)
    n_x = sizes["x"]
    swap = [(0, 1), (1, 0)]
    around = [(2 * i, 2 * ((i + 1) % n_x)) for i in range(n_x)]
    around += [(2 * i + 1, 2 * ((i - 1) % n_x) + 1) for i in range(n_x)]
    own = jnp.concatenate([after(output_gradient, *others), normed], axis=0)
    partner = lax.ppermute(own, "c", swap)

    rows = block.shape[0]
    half = rows // 2
    vmem = pl.BlockSpec(memory_space=pltpu.VMEM)
    smem = pl.BlockSpec(memory_space=pltpu.SMEM)
    hbm = pl.BlockSpec(memory_space=pl.ANY)
    params = pltpu.CompilerParams(vmem_limit_bytes=60 * 2**20)

    low, high = {0: block}, {0: block}

    def step(k, low_from, high_from):
        low[k] = lax.ppermute(low_from, z_axes, ring(n_z, 1))
        high[k] = lax.ppermute(high_from, z_axes, ring(n_z, -1))

    def side(which, first, count, name):
        width = n_tensor * local_width
        return pl.pallas_call(
            functools.partial(side_kernel, n_x, first, count, which),
            out_shape=(
                jax.ShapeDtypeStruct((count, tokens), BF16),
                jax.ShapeDtypeStruct((tokens, count), BF16),
                jax.ShapeDtypeStruct((sequences, SEQUENCE_TOKENS, SEQUENCE_TOKENS), F32),
            ),
            in_specs=[smem] + [hbm] * len(pieces) + [vmem],
            out_specs=(vmem, vmem, vmem),
            scratch_shapes=[
                pltpu.VMEM(
                    (sequences // 2, 2 * SEQUENCE_TOKENS + count, 2 * SEQUENCE_TOKENS), F32
                ),
                pltpu.VMEM((n_tensor, tokens, local_width), BF16),
                pltpu.SemaphoreType.DMA((n_tensor,)),
            ],
            compiler_params=params,
            cost_estimate=pl.CostEstimate(
                flops=2 * tokens * width * (128 + count),
                bytes_accessed=5 * 2**20,
                transcendentals=0,
            ),
            name=name,
        )(spot, *pieces, adapter_width_factors.reshape(3 * RANK, width))

    def scratch(n_rows, n_sems):
        return [
            pltpu.VMEM((tokens, n_rows), BF16),
            pltpu.VMEM((n_rows, hidden), BF16),
            pltpu.SemaphoreType.DMA((n_sems,)),
            pltpu.SemaphoreType.DMA((-(-hidden // 256),)),
        ]

    def at_z(offset):
        return (low if offset < 0 else high)[abs(offset)]

    def part(offsets):
        blocks = [at_z(offset) for offset in offsets]
        plan = dict(
            n_z=n_z,
            n_x=n_x,
            column=column,
            rows=rows,
            first=offsets[0],
            blocks=[(offset, 0) for offset in offsets],
        )
        n = len(blocks)
        return pl.pallas_call(
            functools.partial(part_kernel, plan),
            out_shape=jax.ShapeDtypeStruct((tokens, hidden), F32),
            in_specs=[smem] + [hbm] * (len(pieces) + n),
            out_specs=hbm,
            scratch_shapes=[pltpu.VMEM((tokens, hidden), F32)] + scratch(n * rows, (1 + n_y) * n),
            compiler_params=params,
            cost_estimate=pl.CostEstimate(
                flops=2 * tokens * n * rows * hidden,
                bytes_accessed=6 * 2**20,
                transcendentals=0,
            ),
            name="part_product",
        )(spot, *pieces, *blocks)

    last = n_z // 2
    step(1, block, block)
    pair = jnp.concatenate([own, partner], axis=0)
    near = lax.ppermute(after(pair, low[1], high[1]), tensor_axes, around)
    across = lax.ppermute(near[: 2 * tokens], tensor_axes, around)
    beyond = lax.ppermute(near, "c", swap)
    across_partner = lax.ppermute(across, "c", swap)
    pieces = (own, partner, near, across, beyond, across_partner)
    for k in range(2, last - 1):
        step(k, low[k - 1], high[k - 1])
    split = last - 4
    total = part(list(range(1 - split, split)))
    at = last - 2
    step(at + 1, after(low[at], total), after(high[at], total))
    lora_t, lora, gradient_gram = side(0, 2 * RANK, RANK, "gradient_side")
    at = last - 1
    low_in, high_in = after(low[at], lora_t), after(high[at], lora_t)
    step(last, low_in[:half], high_in[half:])
    in_t, _, normed_gram = side(1, 0, 2 * RANK, "normed_side")
    ahead, behind = list(range(split, last)), list(range(last + 1, n_z - split + 1))
    blocks = [high[k] for k in ahead] + [low[last], high[last]] + [low[n_z - k] for k in behind]
    plan = dict(
        n_z=n_z,
        n_x=n_x,
        column=column,
        rows=rows,
        first=split,
        blocks=[(k, 0) for k in ahead] + [(last, 0), (last, half)] + [(k, 0) for k in behind],
        chunks=[(0, last - split), (last - split, n_z - 2 * split + 1)],
    )
    n_offsets = n_z - 2 * split + 1
    sums, mids = pl.pallas_call(
        functools.partial(hidden_kernel, plan),
        out_shape=(
            jax.ShapeDtypeStruct((sequences, 3 * RANK, hidden), F32),
            jax.ShapeDtypeStruct((8 * n_tensor, tokens), F32),
        ),
        in_specs=[smem] + [hbm] * (len(pieces) + len(blocks) + 3) + [vmem] * 4,
        out_specs=(hbm, vmem),
        scratch_shapes=[
            pltpu.VMEM((tokens, hidden), F32),
            pltpu.VMEM((tokens, hidden), F32),
            pltpu.VMEM((tokens, hidden), BF16),
            pltpu.VMEM((tokens, hidden), BF16),
            pltpu.VMEM((tokens, hidden), F32),
            pltpu.VMEM((tokens, hidden), F32),
            pltpu.VMEM((sequences, 3 * RANK, hidden), F32),
        ]
        + scratch(n_offsets * rows, (1 + n_y) * n_offsets + 12),
        compiler_params=params,
        name="hidden_side",
    )(
        spot,
        *pieces,
        *blocks,
        total,
        gate_preactivation,
        upward_preactivation,
        adapter_hidden_factors.reshape(3 * RANK, hidden),
        in_t,
        lora,
        lora_t,
    )

    pieces = lax.all_to_all(mids.reshape(n_tensor, 8, tokens), tensor_axes, 0, 0)
    piece = jnp.sum(pieces, axis=0)
    mids = lax.all_to_all(
        jnp.broadcast_to(piece, (n_tensor,) + piece.shape), tensor_axes, 0, 0
    ).reshape(8 * n_tensor, tokens)

    lanes = (local_width + hidden) // 128
    tiles = 6 * lanes
    padded = -(-tiles // 8) * 8
    out = pl.pallas_call(
        clip_kernel,
        out_shape=jax.ShapeDtypeStruct((padded, 8, 128), F32),
        in_specs=[smem] + [vmem] * 6,
        out_specs=vmem,
        scratch_shapes=[pltpu.VMEM((3 * RANK, local_width), F32)],
        compiler_params=params,
        name="clip_side",
    )(
        clipping_limit,
        mids,
        sums,
        normed,
        output_gradient,
        normed_gram,
        gradient_gram,
    )

    share = jnp.sum(lax.all_to_all(out.reshape(n_y, -1, 128), "y", 0, 0), axis=0)
    share = jnp.sum(lax.all_to_all(share.reshape(n_z, -1, 128), z_axes, 0, 0), axis=0)
    share = lax.all_to_all(
        jnp.broadcast_to(share, (n_z,) + share.shape), z_axes, 0, 0
    ).reshape(-1, 128)
    whole = lax.all_to_all(jnp.broadcast_to(share, (n_y,) + share.shape), "y", 0, 0)
    total = (
        whole.reshape(padded, 8, 128)[:tiles]
        .reshape(6, lanes, 8, 128)
        .transpose(0, 2, 1, 3)
        .reshape(3, RANK, lanes * 128)
    )
    count = sequences * n_z * sizes["y"]
    bound = clipping_limit[0]
    wide = total[:, :, :local_width]
    inner = total[:, :, local_width : local_width + hidden]
    return (
        (wide + bound * width_noise_draw) / count,
        (inner + bound * hidden_noise_draw) / count,
    )


def solution(mesh):
    names = ("z", "y", "x", "c")
    extents = (16, 4, 4, 2)
    fine = Mesh(mesh.devices.reshape(extents), names)
    dp, tensor = ("z", "y"), ("x", "c")
    placed = (
        P(dp, tensor),
        P(dp, tensor),
        P(dp, tensor),
        P(dp, tensor),
        P(tensor, dp),
        P(),
        P(None, None, tensor),
        P(),
        P(None, None, tensor),
        P(None, None, tensor),
    )
    return jax.shard_map(
        functools.partial(per_device, dict(zip(names, extents, strict=True))),
        mesh=fine,
        in_specs=placed,
        out_specs=(P(None, None, tensor), P(None, None, tensor)),
        check_vma=False,
    )
```

```python
import functools

import jax
import jax.numpy as jnp
from jax import lax
from jax.experimental import pallas as pl
from jax.experimental.pallas import tpu as pltpu
from jax.sharding import Mesh
from jax.sharding import PartitionSpec as P

SEQUENCE_TOKENS = 128
RANK = 16
SCALE = 2.0
F32 = jnp.float32
BF16 = jnp.bfloat16


def contract(left, right, left_dim, right_dim):
    return lax.dot_general(
        left, right, (((left_dim,), (right_dim,)), ((), ())), preferred_element_type=F32
    )


def column_tiles(hidden, step, tile):
    whole = hidden // step

    def body(i, carry):
        tile(i, pl.multiple_of(i * step, step), step)
        return carry

    lax.fori_loop(0, whole, body, 0)
    spans = [(i * step, step) for i in range(whole)]
    if hidden > whole * step:
        spans.append((whole * step, hidden - whole * step))
        tile(whole, *spans[-1])
    return spans


def copy_rows(source, target, sems, at, parts):
    rows = source.shape[0] // parts
    copies = []
    for i in range(parts):
        span = pl.ds(i * rows, rows)
        copies.append(
            pltpu.make_async_copy(source.at[span, :], target.at[span, :], sems.at[at + i])
        )
    return copies


def fetch_blocks(plan, z_ref, gradient_ref, block_refs, left, right, sems):
    n_z, rows_z = plan["n_z"], plan["rows"]
    fetched, row, at = [], 0, 0
    for (offset, first), block in zip(plan["blocks"], block_refs, strict=True):
        rows = block.shape[0]
        start = lax.rem(z_ref[0] + (offset + n_z), n_z) * rows_z + first
        columns = pl.ds(pl.multiple_of(start, 128), rows)
        span = pl.ds(row, rows)
        fetched.append(
            copy_rows(gradient_ref.at[:, columns], left.at[:, span], sems, at, 2)
            + copy_rows(block, right.at[span, :], sems, at + 2, 2)
        )
        row += rows
        at += 4
    return fetched


def side_kernel(n_pairs, *refs):
    row_refs = refs[:n_pairs]
    factors_ref, projected_ref, turned_ref, gram_ref, total = refs[n_pairs:]
    step = pl.program_id(0)
    size = SEQUENCE_TOKENS

    @pl.when(step == 0)
    def _():
        total[...] = jnp.zeros_like(total)

    for p, rows_ref in enumerate(row_refs):
        rows = rows_ref[...]
        stacked = jnp.concatenate([rows, factors_ref[...]], axis=0)
        total[p] += contract(stacked, rows, 1, 1)

    @pl.when(step == pl.num_programs(0) - 1)
    def _():
        for p in range(n_pairs):
            gram_ref[2 * p] = total[p, :size, :size]
            gram_ref[2 * p + 1] = total[p, size : 2 * size, size:]
            span = slice(2 * size * p, 2 * size * (p + 1))
            projected = total[p, 2 * size :]
            projected_ref[:, span] = projected.astype(BF16)
            turned_ref[span, :] = projected.T.astype(BF16)


def part_kernel(plan, first, z_ref, gradient_ref, *refs):
    n_blocks = len(plan["blocks"])
    block_refs, refs = refs[:n_blocks], refs[n_blocks:]
    if not first:
        before_ref, refs = refs[0], refs[1:]
    out_ref, total, left, right, sems, out_sems = refs
    copies = sum(fetch_blocks(plan, z_ref, gradient_ref, block_refs, left, right, sems), [])
    if not first:
        copies += copy_rows(before_ref, total, sems, 4 * n_blocks, 4)
    for copy in copies:
        copy.start()
    for copy in copies:
        copy.wait()

    writes = []
    hidden = total.shape[1]
    for i, start in enumerate(range(0, hidden, 512)):
        cols = slice(start, min(start + 512, hidden))
        product = jnp.dot(left[...], right[:, cols], preferred_element_type=F32)
        total[:, cols] = product if first else total[:, cols] + product
        write = pltpu.make_async_copy(total.at[:, cols], out_ref.at[:, cols], out_sems.at[i])
        write.start()
        writes.append(write)
    for write in writes:
        write.wait()


def hidden_kernel(plan, z_ref, gradient_ref, *refs):
    n_blocks = len(plan["blocks"])
    block_refs = refs[:n_blocks]
    (before_hbm, gate_hbm, up_hbm, factors_ref, in_ref, lora_ref, lora_t_ref) = refs[
        n_blocks : n_blocks + 7
    ]
    sums_hbm, mids_ref, total, before_ref, gate_ref, up_ref, silu_ref, scaled_ref, sums_ref = refs[
        n_blocks + 7 : -4
    ]
    left_rows, right_rows, sems, out_sems = refs[-4:]
    tokens, hidden = gate_ref.shape
    sequences = tokens // SEQUENCE_TOKENS
    fetched = fetch_blocks(plan, z_ref, gradient_ref, block_refs, left_rows, right_rows, sems)
    at = 4 * n_blocks
    activations = copy_rows(gate_hbm, gate_ref, sems, at, 4)
    activations += copy_rows(up_hbm, up_ref, sems, at + 4, 4)
    running = copy_rows(before_hbm, before_ref, sems, at + 8, 4)
    for copy in activations + sum(fetched, []) + running:
        copy.start()
    mids_ref[...] = jnp.zeros_like(mids_ref)

    def adapters(j, e, rows, cols, left, right):
        part = slice(j * RANK, (j + 1) * RANK)
        sums_ref[e, part, cols] = SCALE * jnp.dot(left, right, preferred_element_type=F32)
        mids_ref[part, rows] += contract(factors_ref[part, cols], right, 1, 1)

    def each(i, start, width, body):
        for e in range(sequences):
            body(e, slice(e * SEQUENCE_TOKENS, (e + 1) * SEQUENCE_TOKENS), pl.ds(start, width))

    def forward(e, rows, cols):
        gate = gate_ref[rows, cols].astype(F32)
        up = up_ref[rows, cols].astype(F32)
        sigmoid = jax.nn.sigmoid(gate)
        silu = gate * sigmoid
        slope = sigmoid * (1.0 + gate * (1.0 - sigmoid))
        silu_ref[rows, cols] = silu
        scaled_ref[rows, cols] = up * slope
        adapters(2, e, rows, cols, lora_t_ref[:, rows], (silu * up).astype(BF16))

    def backward(e, rows, cols):
        hidden_grad = (
            total[rows, cols]
            + before_ref[rows, cols]
            + SCALE
            * jnp.dot(lora_ref[rows, :], factors_ref[2 * RANK :, cols], preferred_element_type=F32)
        )
        gate_grad = (hidden_grad * scaled_ref[rows, cols]).astype(BF16)
        adapters(0, e, rows, cols, in_ref[:RANK, rows], gate_grad)
        up_grad = (hidden_grad * silu_ref[rows, cols]).astype(BF16)
        adapters(1, e, rows, cols, in_ref[RANK:, rows], up_grad)

    def write(i, cols):
        return pltpu.make_async_copy(
            sums_ref.at[:, :, cols], sums_hbm.at[:, :, cols], out_sems.at[i]
        )

    def last_tile(i, start, width):
        each(i, start, width, backward)
        write(i, pl.ds(start, width)).start()

    for copy in activations:
        copy.wait()
    column_tiles(hidden, hidden, functools.partial(each, body=forward))
    row = 0
    for some in plan["chunks"]:
        for copy in sum(fetched[some], []):
            copy.wait()
        rows = sum(block.shape[0] for block in block_refs[some])
        span = slice(row, row + rows)
        product = jnp.dot(left_rows[:, span], right_rows[span, :], preferred_element_type=F32)
        total[...] = product if row == 0 else total[...] + product
        row += rows
    for copy in running:
        copy.wait()
    spans = column_tiles(hidden, hidden, last_tile)
    for e in range(sequences):
        square = sums_ref[e] * sums_ref[e]
        line = jnp.sum(jnp.sum(square, axis=0, keepdims=True), axis=1, keepdims=True)
        mids_ref[3 * RANK + e : 3 * RANK + e + 1, :] = jnp.broadcast_to(line, (1, tokens))
    for i, (start, width) in enumerate(spans):
        write(i, pl.ds(start, width)).wait()


def quadratic(left, gram):
    product = jnp.zeros((left.shape[0], gram.shape[1]), F32)
    rest = gram
    for _ in range(3):
        part = rest.astype(BF16)
        product = product + jnp.dot(left, part, preferred_element_type=F32)
        rest = rest - part.astype(F32)
    return product * left.astype(F32)


def total_of(values):
    return jnp.sum(jnp.sum(values, axis=0, keepdims=True), axis=1, keepdims=True)


def clip_kernel(
    clip_ref,
    mids_ref,
    sums_ref,
    normed_ref,
    gradient_ref,
    normed_gram_ref,
    gradient_gram_ref,
    out_ref,
    wide,
):
    sequences, _, hidden = sums_ref.shape
    local = wide.shape[1]
    bound = clip_ref[0]
    weights = []
    for e in range(sequences):
        rows = slice(e * SEQUENCE_TOKENS, (e + 1) * SEQUENCE_TOKENS)
        mids = mids_ref[: 3 * RANK, rows].astype(BF16)
        square = total_of(quadratic(mids[: 2 * RANK], normed_gram_ref[e])) + total_of(
            quadratic(mids[2 * RANK :], gradient_gram_ref[e])
        )
        square = SCALE * SCALE * jnp.maximum(square, 0.0)
        square = square + mids_ref[3 * RANK + e : 3 * RANK + e + 1, 0:1]
        weight = bound / jnp.maximum(jnp.sqrt(square), bound)
        weights.append(weight)
        first = weight * (
            SCALE * jnp.dot(mids[: 2 * RANK], normed_ref[rows, :], preferred_element_type=F32)
        )
        second = weight * (
            SCALE * jnp.dot(mids[2 * RANK :], gradient_ref[rows, :], preferred_element_type=F32)
        )
        if e == 0:
            wide[: 2 * RANK] = first
            wide[2 * RANK :] = second
        else:
            wide[: 2 * RANK] += first
            wide[2 * RANK :] += second
    lanes = (local + hidden) // 128
    for t in range(out_ref.shape[0]):
        r, c = divmod(t, lanes)
        rows = slice(8 * r, 8 * r + 8)
        at = c * 128
        if r >= 3 * RANK // 8:
            value = jnp.zeros((8, 128), F32)
        elif at < local:
            value = wide[rows, at : at + 128]
        else:
            at = at - local
            value = weights[0] * sums_ref[0, rows, at : at + 128]
            for e in range(1, sequences):
                value = value + weights[e] * sums_ref[e, rows, at : at + 128]
        out_ref[t] = value


def ring(size, by):
    return [(i, (i + by) % size) for i in range(size)]


def per_device(
    sizes,
    normed,
    output_gradient,
    gate_preactivation,
    upward_preactivation,
    frozen_down_weight,
    adapter_width_factors,
    adapter_hidden_factors,
    clipping_limit,
    width_noise_draw,
    hidden_noise_draw,
):
    tokens, local_width = normed.shape
    hidden = gate_preactivation.shape[1]
    sequences = tokens // SEQUENCE_TOKENS
    n_z = sizes["z"]
    n_tensor = sizes["x"] * sizes["c"]
    z_axes, tensor_axes = "z", ("x", "c")
    spot = lax.axis_index(z_axes).reshape(1).astype(jnp.int32)

    gradient = lax.all_gather(output_gradient, tensor_axes, axis=1, tiled=True)
    block = lax.all_gather(frozen_down_weight.T, "y", axis=0, tiled=True)
    normed_all = lax.all_gather(normed, tensor_axes, axis=1, tiled=True)

    rows = block.shape[0]
    half = rows // 2
    vmem = pl.BlockSpec(memory_space=pltpu.VMEM)
    smem = pl.BlockSpec(memory_space=pltpu.SMEM)
    hbm = pl.BlockSpec(memory_space=pl.ANY)
    params = pltpu.CompilerParams(vmem_limit_bytes=60 * 2**20)

    low, high = {0: block}, {0: block}

    def step(k, low_from, high_from):
        low[k] = lax.ppermute(low_from, z_axes, ring(n_z, 1))
        high[k] = lax.ppermute(high_from, z_axes, ring(n_z, -1))

    def side(values, first, count, name):
        width = values.shape[1]
        chunk = 1024
        return pl.pallas_call(
            functools.partial(side_kernel, sequences // 2),
            out_shape=(
                jax.ShapeDtypeStruct((count, tokens), BF16),
                jax.ShapeDtypeStruct((tokens, count), BF16),
                jax.ShapeDtypeStruct((sequences, SEQUENCE_TOKENS, SEQUENCE_TOKENS), F32),
            ),
            grid=(width // chunk,),
            in_specs=[
                pl.BlockSpec((2 * SEQUENCE_TOKENS, chunk), functools.partial(lambda p, i: (p, i), p))
                for p in range(sequences // 2)
            ]
            + [pl.BlockSpec((count, chunk), lambda i: (first // count, i))],
            out_specs=(
                pl.BlockSpec((count, tokens), lambda i: (0, 0)),
                pl.BlockSpec((tokens, count), lambda i: (0, 0)),
                pl.BlockSpec((sequences, SEQUENCE_TOKENS, SEQUENCE_TOKENS), lambda i: (0, 0, 0)),
            ),
            scratch_shapes=[
                pltpu.VMEM(
                    (sequences // 2, 2 * SEQUENCE_TOKENS + count, 2 * SEQUENCE_TOKENS), F32
                )
            ],
            compiler_params=params,
            cost_estimate=pl.CostEstimate(
                flops=2 * tokens * width * (128 + count),
                bytes_accessed=5 * 2**20,
                transcendentals=0,
            ),
            name=name,
        )(*[values] * (sequences // 2), adapter_width_factors.reshape(3 * RANK, width))

    def scratch(n_rows, n_sems):
        return [
            pltpu.VMEM((tokens, n_rows), BF16),
            pltpu.VMEM((n_rows, hidden), BF16),
            pltpu.SemaphoreType.DMA((n_sems,)),
            pltpu.SemaphoreType.DMA((-(-hidden // 256),)),
        ]

    def at_z(offset):
        return (low if offset < 0 else high)[abs(offset)]

    def part(offsets, before=None):
        blocks = [at_z(offset) for offset in offsets]
        plan = dict(n_z=n_z, rows=rows, blocks=[(offset, 0) for offset in offsets])
        n = len(blocks)
        given = [] if before is None else [before]
        return pl.pallas_call(
            functools.partial(part_kernel, plan, before is None),
            out_shape=jax.ShapeDtypeStruct((tokens, hidden), F32),
            in_specs=[smem] + [hbm] * (n + 1 + len(given)),
            out_specs=hbm,
            scratch_shapes=[pltpu.VMEM((tokens, hidden), F32)] + scratch(n * rows, 4 * n + 4),
            compiler_params=params,
            cost_estimate=pl.CostEstimate(
                flops=2 * tokens * n * rows * hidden,
                bytes_accessed=6 * 2**20,
                transcendentals=0,
            ),
            name="part_product",
        )(spot, gradient, *blocks, *given)

    def after(value, *others):
        return lax.optimization_barrier((value, *others))[0]

    def pairs(first, end):
        return [sign * k for k in range(first, end) for sign in (-1, 1)]

    last = n_z // 2
    for k in range(1, last - 3):
        step(k, low[k - 1], high[k - 1])
    total = part([0] + pairs(1, last - 4))
    at = last - 4
    step(at + 1, after(low[at], total), after(high[at], total))
    lora_t, lora, gradient_gram = side(gradient, 2 * RANK, RANK, "gradient_side")
    at = last - 3
    step(at + 1, after(low[at], lora_t), after(high[at], lora_t))
    step(last - 1, low[last - 2], high[last - 2])
    in_t, _, normed_gram = side(normed_all, 0, 2 * RANK, "normed_side")
    at = last - 1
    low_in, high_in = after(low[at], in_t), after(high[at], in_t)
    step(last, low_in[:half], high_in[half:])
    total = part(pairs(last - 4, last - 1), after(total, low_in, high_in))
    offsets = pairs(last - 1, last)
    blocks = [at_z(offset) for offset in offsets] + [low[last], high[last]]
    plan = dict(
        n_z=n_z,
        rows=rows,
        blocks=[(offset, 0) for offset in offsets] + [(last, 0), (last, half)],
        chunks=[slice(0, 4)],
    )
    sums, mids = pl.pallas_call(
        functools.partial(hidden_kernel, plan),
        out_shape=(
            jax.ShapeDtypeStruct((sequences, 3 * RANK, hidden), F32),
            jax.ShapeDtypeStruct((8 * n_tensor, tokens), F32),
        ),
        in_specs=[smem] + [hbm] * (len(blocks) + 4) + [vmem] * 4,
        out_specs=(hbm, vmem),
        scratch_shapes=[
            pltpu.VMEM((tokens, hidden), F32),
            pltpu.VMEM((tokens, hidden), F32),
            pltpu.VMEM((tokens, hidden), BF16),
            pltpu.VMEM((tokens, hidden), BF16),
            pltpu.VMEM((tokens, hidden), F32),
            pltpu.VMEM((tokens, hidden), F32),
            pltpu.VMEM((sequences, 3 * RANK, hidden), F32),
        ]
        + scratch((len(offsets) + 1) * rows, 4 * len(blocks) + 12),
        compiler_params=params,
        name="hidden_side",
    )(
        spot,
        gradient,
        *blocks,
        total,
        gate_preactivation,
        upward_preactivation,
        adapter_hidden_factors.reshape(3 * RANK, hidden),
        in_t,
        lora,
        lora_t,
    )

    pieces = lax.all_to_all(mids.reshape(n_tensor, 8, tokens), tensor_axes, 0, 0)
    piece = jnp.sum(pieces, axis=0)
    mids = lax.all_to_all(
        jnp.broadcast_to(piece, (n_tensor,) + piece.shape), tensor_axes, 0, 0
    ).reshape(8 * n_tensor, tokens)

    lanes = (local_width + hidden) // 128
    tiles = 6 * lanes
    padded = -(-tiles // 8) * 8
    out = pl.pallas_call(
        clip_kernel,
        out_shape=jax.ShapeDtypeStruct((padded, 8, 128), F32),
        in_specs=[smem] + [vmem] * 6,
        out_specs=vmem,
        scratch_shapes=[pltpu.VMEM((3 * RANK, local_width), F32)],
        compiler_params=params,
        name="clip_side",
    )(
        clipping_limit,
        mids,
        sums,
        normed,
        output_gradient,
        normed_gram,
        gradient_gram,
    )

    n_y = sizes["y"]
    share = jnp.sum(lax.all_to_all(out.reshape(n_y, -1, 128), "y", 0, 0), axis=0)
    share = jnp.sum(lax.all_to_all(share.reshape(n_z, -1, 128), z_axes, 0, 0), axis=0)
    share = lax.all_to_all(
        jnp.broadcast_to(share, (n_z,) + share.shape), z_axes, 0, 0
    ).reshape(-1, 128)
    whole = lax.all_to_all(jnp.broadcast_to(share, (n_y,) + share.shape), "y", 0, 0)
    total = (
        whole.reshape(padded, 8, 128)[:tiles]
        .reshape(6, lanes, 8, 128)
        .transpose(0, 2, 1, 3)
        .reshape(3, RANK, lanes * 128)
    )
    count = sequences * n_z * sizes["y"]
    bound = clipping_limit[0]
    wide = total[:, :, :local_width]
    inner = total[:, :, local_width : local_width + hidden]
    return (
        (wide + bound * width_noise_draw) / count,
        (inner + bound * hidden_noise_draw) / count,
    )


def solution(mesh):
    names = ("z", "y", "x", "c")
    extents = (16, 4, 4, 2)
    fine = Mesh(mesh.devices.reshape(extents), names)
    dp, tensor = ("z", "y"), ("x", "c")
    placed = (
        P(dp, tensor),
        P(dp, tensor),
        P(dp, tensor),
        P(dp, tensor),
        P(tensor, dp),
        P(),
        P(None, None, tensor),
        P(),
        P(None, None, tensor),
        P(None, None, tensor),
    )
    return jax.shard_map(
        functools.partial(per_device, dict(zip(names, extents, strict=True))),
        mesh=fine,
        in_specs=placed,
        out_specs=(P(None, None, tensor), P(None, None, tensor)),
        check_vma=False,
    )
```

```python
import functools

import jax
import jax.numpy as jnp
from jax import lax
from jax.experimental import pallas as pl
from jax.experimental.pallas import tpu as pltpu
from jax.sharding import Mesh
from jax.sharding import PartitionSpec as P

SEQUENCE_TOKENS = 128
RANK = 16
SCALE = 2.0
F32 = jnp.float32
BF16 = jnp.bfloat16


def contract(left, right, left_dim, right_dim):
    return lax.dot_general(
        left, right, (((left_dim,), (right_dim,)), ((), ())), preferred_element_type=F32
    )


def column_tiles(hidden, step, tile):
    whole = hidden // step

    def body(i, carry):
        tile(i, pl.multiple_of(i * step, step), step)
        return carry

    lax.fori_loop(0, whole, body, 0)
    spans = [(i * step, step) for i in range(whole)]
    if hidden > whole * step:
        spans.append((whole * step, hidden - whole * step))
        tile(whole, *spans[-1])
    return spans


def copy_rows(source, target, sems, at, parts):
    rows = source.shape[0] // parts
    copies = []
    for i in range(parts):
        span = pl.ds(i * rows, rows)
        copies.append(
            pltpu.make_async_copy(source.at[span, :], target.at[span, :], sems.at[at + i])
        )
    return copies


def fetch_blocks(plan, z_ref, gradient_ref, block_refs, left, right, sems):
    n_z, rows_z = plan["n_z"], plan["rows"]
    fetched, row, at = [], 0, 0
    for (offset, first), block in zip(plan["blocks"], block_refs, strict=True):
        rows = block.shape[0]
        start = lax.rem(z_ref[0] + (offset + n_z), n_z) * rows_z + first
        columns = pl.ds(pl.multiple_of(start, 128), rows)
        span = pl.ds(row, rows)
        fetched.append(
            copy_rows(gradient_ref.at[:, columns], left.at[:, span], sems, at, 2)
            + copy_rows(block, right.at[span, :], sems, at + 2, 2)
        )
        row += rows
        at += 4
    return fetched


def side_kernel(n_pairs, *refs):
    row_refs = refs[:n_pairs]
    factors_ref, projected_ref, turned_ref, gram_ref, total = refs[n_pairs:]
    step = pl.program_id(0)
    size = SEQUENCE_TOKENS

    @pl.when(step == 0)
    def _():
        total[...] = jnp.zeros_like(total)

    for p, rows_ref in enumerate(row_refs):
        rows = rows_ref[...]
        stacked = jnp.concatenate([rows, factors_ref[...]], axis=0)
        total[p] += contract(stacked, rows, 1, 1)

    @pl.when(step == pl.num_programs(0) - 1)
    def _():
        for p in range(n_pairs):
            gram_ref[2 * p] = total[p, :size, :size]
            gram_ref[2 * p + 1] = total[p, size : 2 * size, size:]
            span = slice(2 * size * p, 2 * size * (p + 1))
            projected = total[p, 2 * size :]
            projected_ref[:, span] = projected.astype(BF16)
            turned_ref[span, :] = projected.T.astype(BF16)


def part_kernel(plan, first, z_ref, gradient_ref, *refs):
    n_blocks = len(plan["blocks"])
    block_refs, refs = refs[:n_blocks], refs[n_blocks:]
    if not first:
        before_ref, refs = refs[0], refs[1:]
    out_ref, total, left, right, sems, out_sems = refs
    copies = sum(fetch_blocks(plan, z_ref, gradient_ref, block_refs, left, right, sems), [])
    if not first:
        copies += copy_rows(before_ref, total, sems, 4 * n_blocks, 4)
    for copy in copies:
        copy.start()
    for copy in copies:
        copy.wait()

    writes = []
    hidden = total.shape[1]
    for i, start in enumerate(range(0, hidden, 512)):
        cols = slice(start, min(start + 512, hidden))
        product = jnp.dot(left[...], right[:, cols], preferred_element_type=F32)
        total[:, cols] = product if first else total[:, cols] + product
        write = pltpu.make_async_copy(total.at[:, cols], out_ref.at[:, cols], out_sems.at[i])
        write.start()
        writes.append(write)
    for write in writes:
        write.wait()


def hidden_kernel(plan, z_ref, gradient_ref, *refs):
    n_blocks = len(plan["blocks"])
    block_refs = refs[:n_blocks]
    (before_hbm, gate_hbm, up_hbm, factors_ref, in_ref, lora_ref, lora_t_ref) = refs[
        n_blocks : n_blocks + 7
    ]
    sums_hbm, mids_ref, total, before_ref, gate_ref, up_ref, silu_ref, scaled_ref, sums_ref = refs[
        n_blocks + 7 : -4
    ]
    left_rows, right_rows, sems, out_sems = refs[-4:]
    tokens, hidden = gate_ref.shape
    sequences = tokens // SEQUENCE_TOKENS
    fetched = fetch_blocks(plan, z_ref, gradient_ref, block_refs, left_rows, right_rows, sems)
    at = 4 * n_blocks
    activations = copy_rows(gate_hbm, gate_ref, sems, at, 4)
    activations += copy_rows(up_hbm, up_ref, sems, at + 4, 4)
    running = copy_rows(before_hbm, before_ref, sems, at + 8, 4)
    for copy in activations + sum(fetched, []) + running:
        copy.start()
    mids_ref[...] = jnp.zeros_like(mids_ref)

    def adapters(j, e, rows, cols, left, right):
        part = slice(j * RANK, (j + 1) * RANK)
        sums_ref[e, part, cols] = SCALE * jnp.dot(left, right, preferred_element_type=F32)
        mids_ref[part, rows] += contract(factors_ref[part, cols], right, 1, 1)

    def each(i, start, width, body):
        for e in range(sequences):
            body(e, slice(e * SEQUENCE_TOKENS, (e + 1) * SEQUENCE_TOKENS), pl.ds(start, width))

    def forward(e, rows, cols):
        gate = gate_ref[rows, cols].astype(F32)
        up = up_ref[rows, cols].astype(F32)
        sigmoid = jax.nn.sigmoid(gate)
        silu = gate * sigmoid
        slope = sigmoid * (1.0 + gate * (1.0 - sigmoid))
        silu_ref[rows, cols] = silu
        scaled_ref[rows, cols] = up * slope
        adapters(2, e, rows, cols, lora_t_ref[:, rows], (silu * up).astype(BF16))

    def backward(e, rows, cols):
        hidden_grad = (
            total[rows, cols]
            + before_ref[rows, cols]
            + SCALE
            * jnp.dot(lora_ref[rows, :], factors_ref[2 * RANK :, cols], preferred_element_type=F32)
        )
        gate_grad = (hidden_grad * scaled_ref[rows, cols]).astype(BF16)
        adapters(0, e, rows, cols, in_ref[:RANK, rows], gate_grad)
        up_grad = (hidden_grad * silu_ref[rows, cols]).astype(BF16)
        adapters(1, e, rows, cols, in_ref[RANK:, rows], up_grad)

    def write(i, cols):
        return pltpu.make_async_copy(
            sums_ref.at[:, :, cols], sums_hbm.at[:, :, cols], out_sems.at[i]
        )

    def last_tile(i, start, width):
        each(i, start, width, backward)
        write(i, pl.ds(start, width)).start()

    for copy in activations:
        copy.wait()
    column_tiles(hidden, hidden, functools.partial(each, body=forward))
    row = 0
    for some in plan["chunks"]:
        for copy in sum(fetched[some], []):
            copy.wait()
        rows = sum(block.shape[0] for block in block_refs[some])
        span = slice(row, row + rows)
        product = jnp.dot(left_rows[:, span], right_rows[span, :], preferred_element_type=F32)
        total[...] = product if row == 0 else total[...] + product
        row += rows
    for copy in running:
        copy.wait()
    spans = column_tiles(hidden, hidden, last_tile)
    for e in range(sequences):
        square = sums_ref[e] * sums_ref[e]
        line = jnp.sum(jnp.sum(square, axis=0, keepdims=True), axis=1, keepdims=True)
        mids_ref[3 * RANK + e : 3 * RANK + e + 1, :] = jnp.broadcast_to(line, (1, tokens))
    for i, (start, width) in enumerate(spans):
        write(i, pl.ds(start, width)).wait()


def quadratic(left, gram):
    product = jnp.zeros((left.shape[0], gram.shape[1]), F32)
    rest = gram
    for _ in range(3):
        part = rest.astype(BF16)
        product = product + jnp.dot(left, part, preferred_element_type=F32)
        rest = rest - part.astype(F32)
    return product * left.astype(F32)


def total_of(values):
    return jnp.sum(jnp.sum(values, axis=0, keepdims=True), axis=1, keepdims=True)


def clip_kernel(
    clip_ref,
    mids_hbm,
    normed_gram_hbm,
    gradient_gram_hbm,
    normed_hbm,
    gradient_hbm,
    sums_hbm,
    out_ref,
    mids_ref,
    normed_gram_ref,
    gradient_gram_ref,
    normed_ref,
    gradient_ref,
    sums_ref,
    wide,
    sems,
):
    copies = [
        pltpu.make_async_copy(source, target, sems.at[i])
        for i, (source, target) in enumerate(
            (
                (mids_hbm, mids_ref),
                (normed_gram_hbm, normed_gram_ref),
                (gradient_gram_hbm, gradient_gram_ref),
                (normed_hbm, normed_ref),
                (gradient_hbm, gradient_ref),
                (sums_hbm, sums_ref),
            )
        )
    ]
    for copy in copies:
        copy.start()
    sequences, _, hidden = sums_ref.shape
    local = wide.shape[1]
    bound = clip_ref[0]
    weights = []
    for copy in copies[:3]:
        copy.wait()
    for e in range(sequences):
        rows = slice(e * SEQUENCE_TOKENS, (e + 1) * SEQUENCE_TOKENS)
        mids = mids_ref[: 3 * RANK, rows].astype(BF16)
        square = total_of(quadratic(mids[: 2 * RANK], normed_gram_ref[e])) + total_of(
            quadratic(mids[2 * RANK :], gradient_gram_ref[e])
        )
        square = SCALE * SCALE * jnp.maximum(square, 0.0)
        square = square + mids_ref[3 * RANK + e : 3 * RANK + e + 1, 0:1]
        weights.append(bound / jnp.maximum(jnp.sqrt(square), bound))
    for copy in copies[3:5]:
        copy.wait()
    for e, weight in enumerate(weights):
        rows = slice(e * SEQUENCE_TOKENS, (e + 1) * SEQUENCE_TOKENS)
        mids = mids_ref[: 3 * RANK, rows].astype(BF16)
        first = weight * (
            SCALE * jnp.dot(mids[: 2 * RANK], normed_ref[rows, :], preferred_element_type=F32)
        )
        second = weight * (
            SCALE * jnp.dot(mids[2 * RANK :], gradient_ref[rows, :], preferred_element_type=F32)
        )
        if e == 0:
            wide[: 2 * RANK] = first
            wide[2 * RANK :] = second
        else:
            wide[: 2 * RANK] += first
            wide[2 * RANK :] += second
    copies[5].wait()
    lanes = (local + hidden) // 128
    for t in range(out_ref.shape[0]):
        r, c = divmod(t, lanes)
        rows = slice(8 * r, 8 * r + 8)
        at = c * 128
        if r >= 3 * RANK // 8:
            value = jnp.zeros((8, 128), F32)
        elif at < local:
            value = wide[rows, at : at + 128]
        else:
            at = at - local
            value = weights[0] * sums_ref[0, rows, at : at + 128]
            for e in range(1, sequences):
                value = value + weights[e] * sums_ref[e, rows, at : at + 128]
        out_ref[t] = value


def share_kernel(shares_ref, out_ref):
    total = shares_ref[0]
    for i in range(1, shares_ref.shape[0]):
        total = total + shares_ref[i]
    for i in range(out_ref.shape[0]):
        out_ref[i] = total


def output_kernel(bound_ref, tiles_ref, wide_noise_ref, hidden_noise_ref, wide_ref, hidden_ref):
    count = bound_ref[1]
    lanes = wide_ref.shape[1] // 128
    every = lanes + hidden_ref.shape[1] // 128
    for t in range(every * wide_ref.shape[0] // 8):
        r, c = divmod(t, every)
        out, noise, c = (
            (wide_ref, wide_noise_ref, c) if c < lanes else (hidden_ref, hidden_noise_ref, c - lanes)
        )
        at = (slice(8 * r, 8 * r + 8), slice(128 * c, 128 * c + 128))
        out[at] = (tiles_ref[t] + bound_ref[0] * noise[at]) / count


def ring(size, by):
    return [(i, (i + by) % size) for i in range(size)]


def per_device(
    sizes,
    normed,
    output_gradient,
    gate_preactivation,
    upward_preactivation,
    frozen_down_weight,
    adapter_width_factors,
    adapter_hidden_factors,
    clipping_limit,
    width_noise_draw,
    hidden_noise_draw,
):
    tokens, local_width = normed.shape
    hidden = gate_preactivation.shape[1]
    sequences = tokens // SEQUENCE_TOKENS
    n_z = sizes["z"]
    n_tensor = sizes["x"] * sizes["c"]
    z_axes, tensor_axes = "z", ("x", "c")
    spot = lax.axis_index(z_axes).reshape(1).astype(jnp.int32)

    gradient = lax.all_gather(output_gradient, tensor_axes, axis=1, tiled=True)
    block = lax.all_gather(frozen_down_weight.T, "y", axis=0, tiled=True)
    normed_all = lax.all_gather(normed, tensor_axes, axis=1, tiled=True)

    rows = block.shape[0]
    half = rows // 2
    vmem = pl.BlockSpec(memory_space=pltpu.VMEM)
    smem = pl.BlockSpec(memory_space=pltpu.SMEM)
    hbm = pl.BlockSpec(memory_space=pl.ANY)
    params = pltpu.CompilerParams(vmem_limit_bytes=60 * 2**20)

    low, high = {0: block}, {0: block}

    def step(k, low_from, high_from):
        low[k] = lax.ppermute(low_from, z_axes, ring(n_z, 1))
        high[k] = lax.ppermute(high_from, z_axes, ring(n_z, -1))

    def side(values, first, count, name):
        width = values.shape[1]
        chunk = 1024
        return pl.pallas_call(
            functools.partial(side_kernel, sequences // 2),
            out_shape=(
                jax.ShapeDtypeStruct((count, tokens), BF16),
                jax.ShapeDtypeStruct((tokens, count), BF16),
                jax.ShapeDtypeStruct((sequences, SEQUENCE_TOKENS, SEQUENCE_TOKENS), F32),
            ),
            grid=(width // chunk,),
            in_specs=[
                pl.BlockSpec((2 * SEQUENCE_TOKENS, chunk), functools.partial(lambda p, i: (p, i), p))
                for p in range(sequences // 2)
            ]
            + [pl.BlockSpec((count, chunk), lambda i: (first // count, i))],
            out_specs=(
                pl.BlockSpec((count, tokens), lambda i: (0, 0)),
                pl.BlockSpec((tokens, count), lambda i: (0, 0)),
                pl.BlockSpec((sequences, SEQUENCE_TOKENS, SEQUENCE_TOKENS), lambda i: (0, 0, 0)),
            ),
            scratch_shapes=[
                pltpu.VMEM(
                    (sequences // 2, 2 * SEQUENCE_TOKENS + count, 2 * SEQUENCE_TOKENS), F32
                )
            ],
            compiler_params=params,
            cost_estimate=pl.CostEstimate(
                flops=2 * tokens * width * (128 + count),
                bytes_accessed=5 * 2**20,
                transcendentals=0,
            ),
            name=name,
        )(*[values] * (sequences // 2), adapter_width_factors.reshape(3 * RANK, width))

    def scratch(n_rows, n_sems):
        return [
            pltpu.VMEM((tokens, n_rows), BF16),
            pltpu.VMEM((n_rows, hidden), BF16),
            pltpu.SemaphoreType.DMA((n_sems,)),
            pltpu.SemaphoreType.DMA((-(-hidden // 256),)),
        ]

    def at_z(offset):
        return (low if offset < 0 else high)[abs(offset)]

    def part(offsets, before=None):
        blocks = [at_z(offset) for offset in offsets]
        plan = dict(n_z=n_z, rows=rows, blocks=[(offset, 0) for offset in offsets])
        n = len(blocks)
        given = [] if before is None else [before]
        return pl.pallas_call(
            functools.partial(part_kernel, plan, before is None),
            out_shape=jax.ShapeDtypeStruct((tokens, hidden), F32),
            in_specs=[smem] + [hbm] * (n + 1 + len(given)),
            out_specs=hbm,
            scratch_shapes=[pltpu.VMEM((tokens, hidden), F32)] + scratch(n * rows, 4 * n + 4),
            compiler_params=params,
            cost_estimate=pl.CostEstimate(
                flops=2 * tokens * n * rows * hidden,
                bytes_accessed=6 * 2**20,
                transcendentals=0,
            ),
            name="part_product",
        )(spot, gradient, *blocks, *given)

    def after(value, *others):
        return lax.optimization_barrier((value, *others))[0]

    def pairs(first, end):
        return [sign * k for k in range(first, end) for sign in (-1, 1)]

    last = n_z // 2
    for k in range(1, last - 3):
        step(k, low[k - 1], high[k - 1])
    total = part([0] + pairs(1, last - 4))
    at = last - 4
    step(at + 1, after(low[at], total), after(high[at], total))
    lora_t, lora, gradient_gram = side(gradient, 2 * RANK, RANK, "gradient_side")
    at = last - 3
    step(at + 1, after(low[at], lora_t), after(high[at], lora_t))
    step(last - 1, low[last - 2], high[last - 2])
    in_t, _, normed_gram = side(normed_all, 0, 2 * RANK, "normed_side")
    at = last - 1
    low_in, high_in = after(low[at], in_t), after(high[at], in_t)
    step(last, low_in[:half], high_in[half:])
    total = part(pairs(last - 4, last - 1), after(total, low_in, high_in))
    offsets = pairs(last - 1, last)
    blocks = [at_z(offset) for offset in offsets] + [low[last], high[last]]
    plan = dict(
        n_z=n_z,
        rows=rows,
        blocks=[(offset, 0) for offset in offsets] + [(last, 0), (last, half)],
        chunks=[slice(0, 4)],
    )
    sums, mids = pl.pallas_call(
        functools.partial(hidden_kernel, plan),
        out_shape=(
            jax.ShapeDtypeStruct((sequences, 3 * RANK, hidden), F32),
            jax.ShapeDtypeStruct((8 * n_tensor, tokens), F32),
        ),
        in_specs=[smem] + [hbm] * (len(blocks) + 4) + [vmem] * 4,
        out_specs=(hbm, vmem),
        scratch_shapes=[
            pltpu.VMEM((tokens, hidden), F32),
            pltpu.VMEM((tokens, hidden), F32),
            pltpu.VMEM((tokens, hidden), BF16),
            pltpu.VMEM((tokens, hidden), BF16),
            pltpu.VMEM((tokens, hidden), F32),
            pltpu.VMEM((tokens, hidden), F32),
            pltpu.VMEM((sequences, 3 * RANK, hidden), F32),
        ]
        + scratch((len(offsets) + 1) * rows, 4 * len(blocks) + 12),
        compiler_params=params,
        name="hidden_side",
    )(
        spot,
        gradient,
        *blocks,
        total,
        gate_preactivation,
        upward_preactivation,
        adapter_hidden_factors.reshape(3 * RANK, hidden),
        in_t,
        lora,
        lora_t,
    )

    shares = lax.all_to_all(mids.reshape(n_tensor, 8, tokens), tensor_axes, 0, 0)
    shares = pl.pallas_call(
        share_kernel,
        out_shape=jax.ShapeDtypeStruct(shares.shape, F32),
        in_specs=[vmem],
        out_specs=vmem,
        name="share_sum",
    )(shares)
    mids = lax.all_to_all(shares, tensor_axes, 0, 0).reshape(8 * n_tensor, tokens)

    lanes = (local_width + hidden) // 128
    tiles = 6 * lanes
    padded = -(-tiles // 8) * 8
    out = pl.pallas_call(
        clip_kernel,
        out_shape=jax.ShapeDtypeStruct((padded, 8, 128), F32),
        in_specs=[smem] + [hbm] * 6,
        out_specs=vmem,
        scratch_shapes=[
            pltpu.VMEM((8 * n_tensor, tokens), F32),
            pltpu.VMEM((sequences, SEQUENCE_TOKENS, SEQUENCE_TOKENS), F32),
            pltpu.VMEM((sequences, SEQUENCE_TOKENS, SEQUENCE_TOKENS), F32),
            pltpu.VMEM((tokens, local_width), BF16),
            pltpu.VMEM((tokens, local_width), BF16),
            pltpu.VMEM((sequences, 3 * RANK, hidden), F32),
            pltpu.VMEM((3 * RANK, local_width), F32),
            pltpu.SemaphoreType.DMA((6,)),
        ],
        compiler_params=params,
        name="clip_side",
    )(
        clipping_limit,
        mids,
        normed_gram,
        gradient_gram,
        normed,
        output_gradient,
        sums,
    )

    n_y = sizes["y"]
    share = jnp.sum(lax.all_to_all(out.reshape(n_y, -1, 128), "y", 0, 0), axis=0)
    share = jnp.sum(lax.all_to_all(share.reshape(n_z, -1, 128), z_axes, 0, 0), axis=0)
    share = lax.all_to_all(
        jnp.broadcast_to(share, (n_z,) + share.shape), z_axes, 0, 0
    ).reshape(-1, 128)
    whole = lax.all_to_all(jnp.broadcast_to(share, (n_y,) + share.shape), "y", 0, 0)
    count = sequences * n_z * n_y
    wide, inner = pl.pallas_call(
        output_kernel,
        out_shape=(
            jax.ShapeDtypeStruct((3 * RANK, local_width), F32),
            jax.ShapeDtypeStruct((3 * RANK, hidden), F32),
        ),
        in_specs=[smem] + [vmem] * 3,
        out_specs=(vmem, vmem),
        name="outputs",
    )(
        jnp.concatenate([clipping_limit, jnp.full((1,), count, F32)]),
        whole.reshape(padded, 8, 128),
        width_noise_draw.reshape(3 * RANK, local_width),
        hidden_noise_draw.reshape(3 * RANK, hidden),
    )
    return (
        wide.reshape(3, RANK, local_width),
        inner.reshape(3, RANK, hidden),
    )


def solution(mesh):
    names = ("z", "y", "x", "c")
    extents = (16, 4, 4, 2)
    fine = Mesh(mesh.devices.reshape(extents), names)
    dp, tensor = ("z", "y"), ("x", "c")
    placed = (
        P(dp, tensor),
        P(dp, tensor),
        P(dp, tensor),
        P(dp, tensor),
        P(tensor, dp),
        P(),
        P(None, None, tensor),
        P(),
        P(None, None, tensor),
        P(None, None, tensor),
    )
    return jax.shard_map(
        functools.partial(per_device, dict(zip(names, extents, strict=True))),
        mesh=fine,
        in_specs=placed,
        out_specs=(P(None, None, tensor), P(None, None, tensor)),
        check_vma=False,
    )
```

```python
import functools

import jax
import jax.numpy as jnp
from jax import lax
from jax.experimental import pallas as pl
from jax.experimental.pallas import tpu as pltpu
from jax.sharding import Mesh
from jax.sharding import PartitionSpec as P

SEQUENCE_TOKENS = 128
RANK = 16
SCALE = 2.0
F32 = jnp.float32
BF16 = jnp.bfloat16


def contract(left, right, left_dim, right_dim):
    return lax.dot_general(
        left, right, (((left_dim,), (right_dim,)), ((), ())), preferred_element_type=F32
    )


def column_tiles(hidden, step, tile):
    whole = hidden // step

    def body(i, carry):
        tile(i, pl.multiple_of(i * step, step), step)
        return carry

    lax.fori_loop(0, whole, body, 0)
    spans = [(i * step, step) for i in range(whole)]
    if hidden > whole * step:
        spans.append((whole * step, hidden - whole * step))
        tile(whole, *spans[-1])
    return spans


def copy_rows(source, target, sems, at, parts):
    rows = source.shape[0] // parts
    copies = []
    for i in range(parts):
        span = pl.ds(i * rows, rows)
        copies.append(
            pltpu.make_async_copy(source.at[span, :], target.at[span, :], sems.at[at + i])
        )
    return copies


def fetch_blocks(plan, z_ref, gradient_ref, block_refs, left, right, sems):
    n_z, rows_z = plan["n_z"], plan["rows"]
    fetched, row, at = [], 0, 0
    for (offset, first), block in zip(plan["blocks"], block_refs, strict=True):
        rows = block.shape[0]
        start = lax.rem(z_ref[0] + (offset + n_z), n_z) * rows_z + first
        columns = pl.ds(pl.multiple_of(start, 128), rows)
        span = pl.ds(row, rows)
        fetched.append(
            copy_rows(gradient_ref.at[:, columns], left.at[:, span], sems, at, 2)
            + copy_rows(block, right.at[span, :], sems, at + 2, 2)
        )
        row += rows
        at += 4
    return fetched


def side_kernel(n_pairs, *refs):
    row_refs = refs[:n_pairs]
    factors_ref, projected_ref, turned_ref, gram_ref, total = refs[n_pairs:]
    step = pl.program_id(0)
    size = SEQUENCE_TOKENS

    @pl.when(step == 0)
    def _():
        total[...] = jnp.zeros_like(total)

    for p, rows_ref in enumerate(row_refs):
        rows = rows_ref[...]
        stacked = jnp.concatenate([rows, factors_ref[...]], axis=0)
        total[p] += contract(stacked, rows, 1, 1)

    @pl.when(step == pl.num_programs(0) - 1)
    def _():
        for p in range(n_pairs):
            gram_ref[2 * p] = total[p, :size, :size]
            gram_ref[2 * p + 1] = total[p, size : 2 * size, size:]
            span = slice(2 * size * p, 2 * size * (p + 1))
            projected = total[p, 2 * size :]
            projected_ref[:, span] = projected.astype(BF16)
            turned_ref[span, :] = projected.T.astype(BF16)


def part_kernel(plan, first, z_ref, gradient_ref, *refs):
    n_blocks = len(plan["blocks"])
    block_refs, refs = refs[:n_blocks], refs[n_blocks:]
    if not first:
        before_ref, refs = refs[0], refs[1:]
    out_ref, total, front, left, right, sems, out_sems = refs
    fetched = fetch_blocks(plan, z_ref, gradient_ref, block_refs, left, right, sems)
    early = n_blocks // 2 + 1
    head, tail = sum(fetched[:early], []), sum(fetched[early:], [])
    if not first:
        tail += copy_rows(before_ref, total, sems, 4 * n_blocks, 4)
    for copy in head + tail:
        copy.start()
    for copy in head:
        copy.wait()
    split = early * plan["rows"]
    front[...] = jnp.dot(left[:, :split], right[:split, :], preferred_element_type=F32)
    for copy in tail:
        copy.wait()

    writes = []
    hidden = total.shape[1]
    for i, start in enumerate(range(0, hidden, 512)):
        cols = slice(start, min(start + 512, hidden))
        product = front[:, cols] + jnp.dot(
            left[:, split:], right[split:, cols], preferred_element_type=F32
        )
        total[:, cols] = product if first else total[:, cols] + product
        write = pltpu.make_async_copy(total.at[:, cols], out_ref.at[:, cols], out_sems.at[i])
        write.start()
        writes.append(write)
    for write in writes:
        write.wait()


def hidden_kernel(plan, z_ref, gradient_ref, *refs):
    n_blocks = len(plan["blocks"])
    block_refs = refs[:n_blocks]
    (before_hbm, gate_hbm, up_hbm, factors_ref, in_ref, lora_ref, lora_t_ref) = refs[
        n_blocks : n_blocks + 7
    ]
    sums_hbm, mids_ref, total, before_ref, gate_ref, up_ref, silu_ref, scaled_ref, sums_ref = refs[
        n_blocks + 7 : -4
    ]
    left_rows, right_rows, sems, out_sems = refs[-4:]
    tokens, hidden = gate_ref.shape
    sequences = tokens // SEQUENCE_TOKENS
    fetched = fetch_blocks(plan, z_ref, gradient_ref, block_refs, left_rows, right_rows, sems)
    at = 4 * n_blocks
    activations = copy_rows(gate_hbm, gate_ref, sems, at, 4)
    activations += copy_rows(up_hbm, up_ref, sems, at + 4, 4)
    running = copy_rows(before_hbm, before_ref, sems, at + 8, 4)
    for copy in activations + sum(fetched, []) + running:
        copy.start()
    mids_ref[...] = jnp.zeros_like(mids_ref)

    def adapters(j, e, rows, cols, left, right):
        part = slice(j * RANK, (j + 1) * RANK)
        sums_ref[e, part, cols] = SCALE * jnp.dot(left, right, preferred_element_type=F32)
        mids_ref[part, rows] += contract(factors_ref[part, cols], right, 1, 1)

    def each(i, start, width, body):
        for e in range(sequences):
            body(e, slice(e * SEQUENCE_TOKENS, (e + 1) * SEQUENCE_TOKENS), pl.ds(start, width))

    def forward(e, rows, cols):
        gate = gate_ref[rows, cols].astype(F32)
        up = up_ref[rows, cols].astype(F32)
        sigmoid = jax.nn.sigmoid(gate)
        silu = gate * sigmoid
        slope = sigmoid * (1.0 + gate * (1.0 - sigmoid))
        silu_ref[rows, cols] = silu
        scaled_ref[rows, cols] = up * slope
        adapters(2, e, rows, cols, lora_t_ref[:, rows], (silu * up).astype(BF16))

    def backward(e, rows, cols):
        hidden_grad = (
            total[rows, cols]
            + before_ref[rows, cols]
            + SCALE
            * jnp.dot(lora_ref[rows, :], factors_ref[2 * RANK :, cols], preferred_element_type=F32)
        )
        gate_grad = (hidden_grad * scaled_ref[rows, cols]).astype(BF16)
        adapters(0, e, rows, cols, in_ref[:RANK, rows], gate_grad)
        up_grad = (hidden_grad * silu_ref[rows, cols]).astype(BF16)
        adapters(1, e, rows, cols, in_ref[RANK:, rows], up_grad)

    def write(i, cols):
        return pltpu.make_async_copy(
            sums_ref.at[:, :, cols], sums_hbm.at[:, :, cols], out_sems.at[i]
        )

    def last_tile(i, start, width):
        each(i, start, width, backward)
        write(i, pl.ds(start, width)).start()

    for copy in activations:
        copy.wait()
    column_tiles(hidden, hidden, functools.partial(each, body=forward))
    row = 0
    for some in plan["chunks"]:
        for copy in sum(fetched[some], []):
            copy.wait()
        rows = sum(block.shape[0] for block in block_refs[some])
        span = slice(row, row + rows)
        product = jnp.dot(left_rows[:, span], right_rows[span, :], preferred_element_type=F32)
        total[...] = product if row == 0 else total[...] + product
        row += rows
    for copy in running:
        copy.wait()
    spans = column_tiles(hidden, hidden, last_tile)
    for e in range(sequences):
        square = sums_ref[e] * sums_ref[e]
        line = jnp.sum(jnp.sum(square, axis=0, keepdims=True), axis=1, keepdims=True)
        mids_ref[3 * RANK + e : 3 * RANK + e + 1, :] = jnp.broadcast_to(line, (1, tokens))
    for i, (start, width) in enumerate(spans):
        write(i, pl.ds(start, width)).wait()


def quadratic(left, gram):
    product = jnp.zeros((left.shape[0], gram.shape[1]), F32)
    rest = gram
    for _ in range(3):
        part = rest.astype(BF16)
        product = product + jnp.dot(left, part, preferred_element_type=F32)
        rest = rest - part.astype(F32)
    return product * left.astype(F32)


def total_of(values):
    return jnp.sum(jnp.sum(values, axis=0, keepdims=True), axis=1, keepdims=True)


def clip_kernel(
    clip_ref,
    mids_hbm,
    normed_gram_hbm,
    gradient_gram_hbm,
    normed_hbm,
    gradient_hbm,
    sums_hbm,
    out_ref,
    mids_ref,
    normed_gram_ref,
    gradient_gram_ref,
    normed_ref,
    gradient_ref,
    sums_ref,
    wide,
    sems,
):
    copies = [
        pltpu.make_async_copy(source, target, sems.at[i])
        for i, (source, target) in enumerate(
            (
                (mids_hbm, mids_ref),
                (normed_gram_hbm, normed_gram_ref),
                (gradient_gram_hbm, gradient_gram_ref),
                (normed_hbm, normed_ref),
                (gradient_hbm, gradient_ref),
                (sums_hbm, sums_ref),
            )
        )
    ]
    for copy in copies:
        copy.start()
    sequences, _, hidden = sums_ref.shape
    local = wide.shape[1]
    bound = clip_ref[0]
    weights = []
    for copy in copies[:3]:
        copy.wait()
    for e in range(sequences):
        rows = slice(e * SEQUENCE_TOKENS, (e + 1) * SEQUENCE_TOKENS)
        mids = mids_ref[: 3 * RANK, rows].astype(BF16)
        square = total_of(quadratic(mids[: 2 * RANK], normed_gram_ref[e])) + total_of(
            quadratic(mids[2 * RANK :], gradient_gram_ref[e])
        )
        square = SCALE * SCALE * jnp.maximum(square, 0.0)
        square = square + mids_ref[3 * RANK + e : 3 * RANK + e + 1, 0:1]
        weights.append(bound / jnp.maximum(jnp.sqrt(square), bound))
    for copy in copies[3:5]:
        copy.wait()
    for e, weight in enumerate(weights):
        rows = slice(e * SEQUENCE_TOKENS, (e + 1) * SEQUENCE_TOKENS)
        mids = mids_ref[: 3 * RANK, rows].astype(BF16)
        first = weight * (
            SCALE * jnp.dot(mids[: 2 * RANK], normed_ref[rows, :], preferred_element_type=F32)
        )
        second = weight * (
            SCALE * jnp.dot(mids[2 * RANK :], gradient_ref[rows, :], preferred_element_type=F32)
        )
        if e == 0:
            wide[: 2 * RANK] = first
            wide[2 * RANK :] = second
        else:
            wide[: 2 * RANK] += first
            wide[2 * RANK :] += second
    copies[5].wait()
    lanes = (local + hidden) // 128
    for t in range(out_ref.shape[0]):
        r, c = divmod(t, lanes)
        rows = slice(8 * r, 8 * r + 8)
        at = c * 128
        if r >= 3 * RANK // 8:
            value = jnp.zeros((8, 128), F32)
        elif at < local:
            value = wide[rows, at : at + 128]
        else:
            at = at - local
            value = weights[0] * sums_ref[0, rows, at : at + 128]
            for e in range(1, sequences):
                value = value + weights[e] * sums_ref[e, rows, at : at + 128]
        out_ref[t] = value


def ring(size, by):
    return [(i, (i + by) % size) for i in range(size)]


def per_device(
    sizes,
    normed,
    output_gradient,
    gate_preactivation,
    upward_preactivation,
    frozen_down_weight,
    adapter_width_factors,
    adapter_hidden_factors,
    clipping_limit,
    width_noise_draw,
    hidden_noise_draw,
):
    tokens, local_width = normed.shape
    hidden = gate_preactivation.shape[1]
    sequences = tokens // SEQUENCE_TOKENS
    n_z = sizes["z"]
    n_tensor = sizes["x"] * sizes["c"]
    z_axes, tensor_axes = "z", ("x", "c")
    spot = lax.axis_index(z_axes).reshape(1).astype(jnp.int32)

    gradient = lax.all_gather(output_gradient, tensor_axes, axis=1, tiled=True)
    block = lax.all_gather(frozen_down_weight.T, "y", axis=0, tiled=True)
    normed_all = lax.all_gather(normed, tensor_axes, axis=1, tiled=True)

    rows = block.shape[0]
    half = rows // 2
    vmem = pl.BlockSpec(memory_space=pltpu.VMEM)
    smem = pl.BlockSpec(memory_space=pltpu.SMEM)
    hbm = pl.BlockSpec(memory_space=pl.ANY)
    params = pltpu.CompilerParams(vmem_limit_bytes=60 * 2**20)

    low, high = {0: block}, {0: block}

    def step(k, low_from, high_from):
        low[k] = lax.ppermute(low_from, z_axes, ring(n_z, 1))
        high[k] = lax.ppermute(high_from, z_axes, ring(n_z, -1))

    def side(values, first, count, name):
        width = values.shape[1]
        chunk = 2048
        return pl.pallas_call(
            functools.partial(side_kernel, sequences // 2),
            out_shape=(
                jax.ShapeDtypeStruct((count, tokens), BF16),
                jax.ShapeDtypeStruct((tokens, count), BF16),
                jax.ShapeDtypeStruct((sequences, SEQUENCE_TOKENS, SEQUENCE_TOKENS), F32),
            ),
            grid=(width // chunk,),
            in_specs=[
                pl.BlockSpec((2 * SEQUENCE_TOKENS, chunk), functools.partial(lambda p, i: (p, i), p))
                for p in range(sequences // 2)
            ]
            + [pl.BlockSpec((count, chunk), lambda i: (first // count, i))],
            out_specs=(
                pl.BlockSpec((count, tokens), lambda i: (0, 0)),
                pl.BlockSpec((tokens, count), lambda i: (0, 0)),
                pl.BlockSpec((sequences, SEQUENCE_TOKENS, SEQUENCE_TOKENS), lambda i: (0, 0, 0)),
            ),
            scratch_shapes=[
                pltpu.VMEM(
                    (sequences // 2, 2 * SEQUENCE_TOKENS + count, 2 * SEQUENCE_TOKENS), F32
                )
            ],
            compiler_params=params,
            cost_estimate=pl.CostEstimate(
                flops=2 * tokens * width * (128 + count),
                bytes_accessed=5 * 2**20,
                transcendentals=0,
            ),
            name=name,
        )(*[values] * (sequences // 2), adapter_width_factors.reshape(3 * RANK, width))

    def scratch(n_rows, n_sems):
        return [
            pltpu.VMEM((tokens, n_rows), BF16),
            pltpu.VMEM((n_rows, hidden), BF16),
            pltpu.SemaphoreType.DMA((n_sems,)),
            pltpu.SemaphoreType.DMA((-(-hidden // 256),)),
        ]

    def at_z(offset):
        return (low if offset < 0 else high)[abs(offset)]

    def part(offsets, before=None):
        blocks = [at_z(offset) for offset in offsets]
        plan = dict(n_z=n_z, rows=rows, blocks=[(offset, 0) for offset in offsets])
        n = len(blocks)
        given = [] if before is None else [before]
        return pl.pallas_call(
            functools.partial(part_kernel, plan, before is None),
            out_shape=jax.ShapeDtypeStruct((tokens, hidden), F32),
            in_specs=[smem] + [hbm] * (n + 1 + len(given)),
            out_specs=hbm,
            scratch_shapes=[pltpu.VMEM((tokens, hidden), F32)] * 2
            + scratch(n * rows, 4 * n + 4),
            compiler_params=params,
            cost_estimate=pl.CostEstimate(
                flops=2 * tokens * n * rows * hidden,
                bytes_accessed=6 * 2**20,
                transcendentals=0,
            ),
            name="part_product",
        )(spot, gradient, *blocks, *given)

    def after(value, *others):
        return lax.optimization_barrier((value, *others))[0]

    def pairs(first, end):
        return [sign * k for k in range(first, end) for sign in (-1, 1)]

    last = n_z // 2
    for k in range(1, last - 3):
        step(k, low[k - 1], high[k - 1])
    total = part([0] + pairs(1, last - 4))
    at = last - 4
    step(at + 1, after(low[at], total), after(high[at], total))
    lora_t, lora, gradient_gram = side(gradient, 2 * RANK, RANK, "gradient_side")
    at = last - 3
    step(at + 1, after(low[at], lora_t), after(high[at], lora_t))
    step(last - 1, low[last - 2], high[last - 2])
    in_t, _, normed_gram = side(normed_all, 0, 2 * RANK, "normed_side")
    at = last - 1
    low_in, high_in = after(low[at], in_t), after(high[at], in_t)
    step(last, low_in[:half], high_in[half:])
    total = part(pairs(last - 4, last - 1), after(total, low_in, high_in))
    offsets = pairs(last - 1, last)
    blocks = [at_z(offset) for offset in offsets] + [low[last], high[last]]
    plan = dict(
        n_z=n_z,
        rows=rows,
        blocks=[(offset, 0) for offset in offsets] + [(last, 0), (last, half)],
        chunks=[slice(0, 4)],
    )
    sums, mids = pl.pallas_call(
        functools.partial(hidden_kernel, plan),
        out_shape=(
            jax.ShapeDtypeStruct((sequences, 3 * RANK, hidden), F32),
            jax.ShapeDtypeStruct((8 * n_tensor, tokens), F32),
        ),
        in_specs=[smem] + [hbm] * (len(blocks) + 4) + [vmem] * 4,
        out_specs=(hbm, vmem),
        scratch_shapes=[
            pltpu.VMEM((tokens, hidden), F32),
            pltpu.VMEM((tokens, hidden), F32),
            pltpu.VMEM((tokens, hidden), BF16),
            pltpu.VMEM((tokens, hidden), BF16),
            pltpu.VMEM((tokens, hidden), F32),
            pltpu.VMEM((tokens, hidden), F32),
            pltpu.VMEM((sequences, 3 * RANK, hidden), F32),
        ]
        + scratch((len(offsets) + 1) * rows, 4 * len(blocks) + 12),
        compiler_params=params,
        name="hidden_side",
    )(
        spot,
        gradient,
        *blocks,
        total,
        gate_preactivation,
        upward_preactivation,
        adapter_hidden_factors.reshape(3 * RANK, hidden),
        in_t,
        lora,
        lora_t,
    )

    pieces = lax.all_to_all(mids.reshape(n_tensor, 8, tokens), tensor_axes, 0, 0)
    piece = jnp.sum(pieces, axis=0)
    mids = lax.all_to_all(
        jnp.broadcast_to(piece, (n_tensor,) + piece.shape), tensor_axes, 0, 0
    ).reshape(8 * n_tensor, tokens)

    lanes = (local_width + hidden) // 128
    tiles = 6 * lanes
    padded = -(-tiles // 8) * 8
    out = pl.pallas_call(
        clip_kernel,
        out_shape=jax.ShapeDtypeStruct((padded, 8, 128), F32),
        in_specs=[smem] + [hbm] * 6,
        out_specs=vmem,
        scratch_shapes=[
            pltpu.VMEM((8 * n_tensor, tokens), F32),
            pltpu.VMEM((sequences, SEQUENCE_TOKENS, SEQUENCE_TOKENS), F32),
            pltpu.VMEM((sequences, SEQUENCE_TOKENS, SEQUENCE_TOKENS), F32),
            pltpu.VMEM((tokens, local_width), BF16),
            pltpu.VMEM((tokens, local_width), BF16),
            pltpu.VMEM((sequences, 3 * RANK, hidden), F32),
            pltpu.VMEM((3 * RANK, local_width), F32),
            pltpu.SemaphoreType.DMA((6,)),
        ],
        compiler_params=params,
        name="clip_side",
    )(
        clipping_limit,
        mids,
        normed_gram,
        gradient_gram,
        normed,
        output_gradient,
        sums,
    )

    n_y = sizes["y"]
    share = jnp.sum(lax.all_to_all(out.reshape(n_y, -1, 128), "y", 0, 0), axis=0)
    share = jnp.sum(lax.all_to_all(share.reshape(n_z, -1, 128), z_axes, 0, 0), axis=0)
    share = lax.all_to_all(
        jnp.broadcast_to(share, (n_z,) + share.shape), z_axes, 0, 0
    ).reshape(-1, 128)
    whole = lax.all_to_all(jnp.broadcast_to(share, (n_y,) + share.shape), "y", 0, 0)
    total = (
        whole.reshape(padded, 8, 128)[:tiles]
        .reshape(6, lanes, 8, 128)
        .transpose(0, 2, 1, 3)
        .reshape(3, RANK, lanes * 128)
    )
    count = sequences * n_z * sizes["y"]
    bound = clipping_limit[0]
    wide = total[:, :, :local_width]
    inner = total[:, :, local_width : local_width + hidden]
    return (
        (wide + bound * width_noise_draw) / count,
        (inner + bound * hidden_noise_draw) / count,
    )


def solution(mesh):
    names = ("z", "y", "x", "c")
    extents = (16, 4, 4, 2)
    fine = Mesh(mesh.devices.reshape(extents), names)
    dp, tensor = ("z", "y"), ("x", "c")
    placed = (
        P(dp, tensor),
        P(dp, tensor),
        P(dp, tensor),
        P(dp, tensor),
        P(tensor, dp),
        P(),
        P(None, None, tensor),
        P(),
        P(None, None, tensor),
        P(None, None, tensor),
    )
    return jax.shard_map(
        functools.partial(per_device, dict(zip(names, extents, strict=True))),
        mesh=fine,
        in_specs=placed,
        out_specs=(P(None, None, tensor), P(None, None, tensor)),
        check_vma=False,
    )
```

```python
import functools

import jax
import jax.numpy as jnp
from jax import lax
from jax.experimental import pallas as pl
from jax.experimental.pallas import tpu as pltpu
from jax.sharding import Mesh
from jax.sharding import PartitionSpec as P

SEQUENCE_TOKENS = 128
RANK = 16
SCALE = 2.0
F32 = jnp.float32
BF16 = jnp.bfloat16


def contract(left, right, left_dim, right_dim):
    return lax.dot_general(
        left, right, (((left_dim,), (right_dim,)), ((), ())), preferred_element_type=F32
    )


def column_tiles(hidden, step, tile):
    whole = hidden // step

    def body(i, carry):
        tile(i, pl.multiple_of(i * step, step), step)
        return carry

    lax.fori_loop(0, whole, body, 0)
    spans = [(i * step, step) for i in range(whole)]
    if hidden > whole * step:
        spans.append((whole * step, hidden - whole * step))
        tile(whole, *spans[-1])
    return spans


def copy_rows(source, target, sems, at, parts):
    rows = source.shape[0] // parts
    copies = []
    for i in range(parts):
        span = pl.ds(i * rows, rows)
        copies.append(
            pltpu.make_async_copy(source.at[span, :], target.at[span, :], sems.at[at + i])
        )
    return copies


def fetch_blocks(plan, z_ref, gradient_ref, block_refs, left, right, sems):
    n_z, rows_z = plan["n_z"], plan["rows"]
    fetched, row, at = [], 0, 0
    for (offset, first), block in zip(plan["blocks"], block_refs, strict=True):
        rows = block.shape[0]
        start = lax.rem(z_ref[0] + (offset + n_z), n_z) * rows_z + first
        columns = pl.ds(pl.multiple_of(start, 128), rows)
        span = pl.ds(row, rows)
        fetched.append(
            copy_rows(gradient_ref.at[:, columns], left.at[:, span], sems, at, 2)
            + copy_rows(block, right.at[span, :], sems, at + 2, 2)
        )
        row += rows
        at += 4
    return fetched


def side_kernel(n_pairs, *refs):
    row_refs = refs[:n_pairs]
    factors_ref, projected_ref, turned_ref, gram_ref, total = refs[n_pairs:]
    step = pl.program_id(0)
    size = SEQUENCE_TOKENS

    @pl.when(step == 0)
    def _():
        total[...] = jnp.zeros_like(total)

    for p, rows_ref in enumerate(row_refs):
        rows = rows_ref[...]
        stacked = jnp.concatenate([rows, factors_ref[...]], axis=0)
        total[p] += contract(stacked, rows, 1, 1)

    @pl.when(step == pl.num_programs(0) - 1)
    def _():
        for p in range(n_pairs):
            gram_ref[2 * p] = total[p, :size, :size]
            gram_ref[2 * p + 1] = total[p, size : 2 * size, size:]
            span = slice(2 * size * p, 2 * size * (p + 1))
            projected = total[p, 2 * size :]
            projected_ref[:, span] = projected.astype(BF16)
            turned_ref[span, :] = projected.T.astype(BF16)


def part_kernel(plan, first, z_ref, gradient_ref, *refs):
    n_blocks = len(plan["blocks"])
    block_refs, refs = refs[:n_blocks], refs[n_blocks:]
    if not first:
        before_ref, refs = refs[0], refs[1:]
    out_ref, total, front, left, right, sems, out_sems = refs
    fetched = fetch_blocks(plan, z_ref, gradient_ref, block_refs, left, right, sems)
    early = n_blocks // 2 + 1
    head, tail = sum(fetched[:early], []), sum(fetched[early:], [])
    if not first:
        tail += copy_rows(before_ref, total, sems, 4 * n_blocks, 4)
    for copy in head + tail:
        copy.start()
    for copy in head:
        copy.wait()
    split = early * plan["rows"]
    front[...] = jnp.dot(left[:, :split], right[:split, :], preferred_element_type=F32)
    for copy in tail:
        copy.wait()

    writes = []
    hidden = total.shape[1]
    for i, start in enumerate(range(0, hidden, 512)):
        cols = slice(start, min(start + 512, hidden))
        product = front[:, cols] + jnp.dot(
            left[:, split:], right[split:, cols], preferred_element_type=F32
        )
        total[:, cols] = product if first else total[:, cols] + product
        write = pltpu.make_async_copy(total.at[:, cols], out_ref.at[:, cols], out_sems.at[i])
        write.start()
        writes.append(write)
    for write in writes:
        write.wait()


def hidden_kernel(plan, z_ref, gradient_ref, *refs):
    n_blocks = len(plan["blocks"])
    block_refs = refs[:n_blocks]
    (before_hbm, gate_hbm, up_hbm, factors_ref, in_ref, lora_ref, lora_t_ref) = refs[
        n_blocks : n_blocks + 7
    ]
    sums_hbm, mids_ref, total, before_ref, gate_ref, up_ref, silu_ref, scaled_ref, sums_ref = refs[
        n_blocks + 7 : -4
    ]
    left_rows, right_rows, sems, out_sems = refs[-4:]
    tokens, hidden = gate_ref.shape
    sequences = tokens // SEQUENCE_TOKENS
    fetched = fetch_blocks(plan, z_ref, gradient_ref, block_refs, left_rows, right_rows, sems)
    at = 4 * n_blocks
    activations = copy_rows(gate_hbm, gate_ref, sems, at, 4)
    activations += copy_rows(up_hbm, up_ref, sems, at + 4, 4)
    running = copy_rows(before_hbm, before_ref, sems, at + 8, 4)
    for copy in activations + sum(fetched, []) + running:
        copy.start()
    mids_ref[...] = jnp.zeros_like(mids_ref)

    def adapters(j, e, rows, cols, left, right):
        part = slice(j * RANK, (j + 1) * RANK)
        sums_ref[e, part, cols] = SCALE * jnp.dot(left, right, preferred_element_type=F32)
        mids_ref[part, rows] += contract(factors_ref[part, cols], right, 1, 1)

    def each(i, start, width, body):
        for e in range(sequences):
            body(e, slice(e * SEQUENCE_TOKENS, (e + 1) * SEQUENCE_TOKENS), pl.ds(start, width))

    def forward(e, rows, cols):
        gate = gate_ref[rows, cols].astype(F32)
        up = up_ref[rows, cols].astype(F32)
        sigmoid = jax.nn.sigmoid(gate)
        silu = gate * sigmoid
        slope = sigmoid * (1.0 + gate * (1.0 - sigmoid))
        silu_ref[rows, cols] = silu
        scaled_ref[rows, cols] = up * slope
        adapters(2, e, rows, cols, lora_t_ref[:, rows], (silu * up).astype(BF16))

    def backward(e, rows, cols):
        hidden_grad = (
            total[rows, cols]
            + before_ref[rows, cols]
            + SCALE
            * jnp.dot(lora_ref[rows, :], factors_ref[2 * RANK :, cols], preferred_element_type=F32)
        )
        gate_grad = (hidden_grad * scaled_ref[rows, cols]).astype(BF16)
        adapters(0, e, rows, cols, in_ref[:RANK, rows], gate_grad)
        up_grad = (hidden_grad * silu_ref[rows, cols]).astype(BF16)
        adapters(1, e, rows, cols, in_ref[RANK:, rows], up_grad)

    def write(i, cols):
        return pltpu.make_async_copy(
            sums_ref.at[:, :, cols], sums_hbm.at[:, :, cols], out_sems.at[i]
        )

    def last_tile(i, start, width):
        each(i, start, width, backward)
        write(i, pl.ds(start, width)).start()

    for copy in activations:
        copy.wait()
    column_tiles(hidden, hidden, functools.partial(each, body=forward))
    row = 0
    for some in plan["chunks"]:
        for copy in sum(fetched[some], []):
            copy.wait()
        rows = sum(block.shape[0] for block in block_refs[some])
        span = slice(row, row + rows)
        product = jnp.dot(left_rows[:, span], right_rows[span, :], preferred_element_type=F32)
        total[...] = product if row == 0 else total[...] + product
        row += rows
    for copy in running:
        copy.wait()
    spans = column_tiles(hidden, hidden, last_tile)
    for e in range(sequences):
        square = sums_ref[e] * sums_ref[e]
        line = jnp.sum(jnp.sum(square, axis=0, keepdims=True), axis=1, keepdims=True)
        mids_ref[3 * RANK + e : 3 * RANK + e + 1, :] = jnp.broadcast_to(line, (1, tokens))
    for i, (start, width) in enumerate(spans):
        write(i, pl.ds(start, width)).wait()


def quadratic(left, gram):
    product = jnp.zeros((left.shape[0], gram.shape[1]), F32)
    rest = gram
    for _ in range(3):
        part = rest.astype(BF16)
        product = product + jnp.dot(left, part, preferred_element_type=F32)
        rest = rest - part.astype(F32)
    return product * left.astype(F32)


def total_of(values):
    return jnp.sum(jnp.sum(values, axis=0, keepdims=True), axis=1, keepdims=True)


def clip_kernel(
    clip_ref,
    mids_hbm,
    normed_gram_hbm,
    gradient_gram_hbm,
    normed_hbm,
    gradient_hbm,
    sums_hbm,
    out_ref,
    mids_ref,
    normed_gram_ref,
    gradient_gram_ref,
    normed_ref,
    gradient_ref,
    sums_ref,
    wide,
    sems,
):
    copies = [
        pltpu.make_async_copy(source, target, sems.at[i])
        for i, (source, target) in enumerate(
            (
                (mids_hbm, mids_ref),
                (normed_gram_hbm, normed_gram_ref),
                (gradient_gram_hbm, gradient_gram_ref),
                (normed_hbm, normed_ref),
                (gradient_hbm, gradient_ref),
                (sums_hbm, sums_ref),
            )
        )
    ]
    for copy in copies:
        copy.start()
    sequences, _, hidden = sums_ref.shape
    local = wide.shape[1]
    bound = clip_ref[0]
    weights = []
    for copy in copies[:3]:
        copy.wait()
    for e in range(sequences):
        rows = slice(e * SEQUENCE_TOKENS, (e + 1) * SEQUENCE_TOKENS)
        mids = mids_ref[: 3 * RANK, rows].astype(BF16)
        square = total_of(quadratic(mids[: 2 * RANK], normed_gram_ref[e])) + total_of(
            quadratic(mids[2 * RANK :], gradient_gram_ref[e])
        )
        square = SCALE * SCALE * jnp.maximum(square, 0.0)
        square = square + mids_ref[3 * RANK + e : 3 * RANK + e + 1, 0:1]
        weights.append(bound / jnp.maximum(jnp.sqrt(square), bound))
    for copy in copies[3:5]:
        copy.wait()
    for e, weight in enumerate(weights):
        rows = slice(e * SEQUENCE_TOKENS, (e + 1) * SEQUENCE_TOKENS)
        mids = mids_ref[: 3 * RANK, rows].astype(BF16)
        first = weight * (
            SCALE * jnp.dot(mids[: 2 * RANK], normed_ref[rows, :], preferred_element_type=F32)
        )
        second = weight * (
            SCALE * jnp.dot(mids[2 * RANK :], gradient_ref[rows, :], preferred_element_type=F32)
        )
        if e == 0:
            wide[: 2 * RANK] = first
            wide[2 * RANK :] = second
        else:
            wide[: 2 * RANK] += first
            wide[2 * RANK :] += second
    copies[5].wait()
    lanes = (local + hidden) // 128
    for t in range(out_ref.shape[0]):
        r, c = divmod(t, lanes)
        rows = slice(8 * r, 8 * r + 8)
        at = c * 128
        if r >= 3 * RANK // 8:
            value = jnp.zeros((8, 128), F32)
        elif at < local:
            value = wide[rows, at : at + 128]
        else:
            at = at - local
            value = weights[0] * sums_ref[0, rows, at : at + 128]
            for e in range(1, sequences):
                value = value + weights[e] * sums_ref[e, rows, at : at + 128]
        out_ref[t] = value


def ring(size, by):
    return [(i, (i + by) % size) for i in range(size)]


def per_device(
    sizes,
    normed,
    output_gradient,
    gate_preactivation,
    upward_preactivation,
    frozen_down_weight,
    adapter_width_factors,
    adapter_hidden_factors,
    clipping_limit,
    width_noise_draw,
    hidden_noise_draw,
):
    tokens, local_width = normed.shape
    hidden = gate_preactivation.shape[1]
    sequences = tokens // SEQUENCE_TOKENS
    n_z = sizes["z"]
    n_tensor = sizes["x"] * sizes["c"]
    z_axes, tensor_axes = "z", ("x", "c")
    spot = lax.axis_index(z_axes).reshape(1).astype(jnp.int32)

    gradient = lax.all_gather(output_gradient, tensor_axes, axis=1, tiled=True)
    block = lax.all_gather(frozen_down_weight.T, "y", axis=0, tiled=True)
    normed_all = lax.all_gather(normed, tensor_axes, axis=1, tiled=True)

    rows = block.shape[0]
    half = rows // 2
    vmem = pl.BlockSpec(memory_space=pltpu.VMEM)
    smem = pl.BlockSpec(memory_space=pltpu.SMEM)
    hbm = pl.BlockSpec(memory_space=pl.ANY)
    params = pltpu.CompilerParams(vmem_limit_bytes=60 * 2**20)

    low, high = {0: block}, {0: block}

    def step(k, low_from, high_from):
        low[k] = lax.ppermute(low_from, z_axes, ring(n_z, 1))
        high[k] = lax.ppermute(high_from, z_axes, ring(n_z, -1))

    def side(values, first, count, name):
        width = values.shape[1]
        chunk = 2048
        return pl.pallas_call(
            functools.partial(side_kernel, sequences // 2),
            out_shape=(
                jax.ShapeDtypeStruct((count, tokens), BF16),
                jax.ShapeDtypeStruct((tokens, count), BF16),
                jax.ShapeDtypeStruct((sequences, SEQUENCE_TOKENS, SEQUENCE_TOKENS), F32),
            ),
            grid=(width // chunk,),
            in_specs=[
                pl.BlockSpec((2 * SEQUENCE_TOKENS, chunk), functools.partial(lambda p, i: (p, i), p))
                for p in range(sequences // 2)
            ]
            + [pl.BlockSpec((count, chunk), lambda i: (first // count, i))],
            out_specs=(
                pl.BlockSpec((count, tokens), lambda i: (0, 0)),
                pl.BlockSpec((tokens, count), lambda i: (0, 0)),
                pl.BlockSpec((sequences, SEQUENCE_TOKENS, SEQUENCE_TOKENS), lambda i: (0, 0, 0)),
            ),
            scratch_shapes=[
                pltpu.VMEM(
                    (sequences // 2, 2 * SEQUENCE_TOKENS + count, 2 * SEQUENCE_TOKENS), F32
                )
            ],
            compiler_params=params,
            cost_estimate=pl.CostEstimate(
                flops=2 * tokens * width * (128 + count),
                bytes_accessed=5 * 2**20,
                transcendentals=0,
            ),
            name=name,
        )(*[values] * (sequences // 2), adapter_width_factors.reshape(3 * RANK, width))

    def scratch(n_rows, n_sems):
        return [
            pltpu.VMEM((tokens, n_rows), BF16),
            pltpu.VMEM((n_rows, hidden), BF16),
            pltpu.SemaphoreType.DMA((n_sems,)),
            pltpu.SemaphoreType.DMA((-(-hidden // 256),)),
        ]

    def at_z(offset):
        return (low if offset < 0 else high)[abs(offset)]

    def part(offsets, before=None):
        blocks = [at_z(offset) for offset in offsets]
        plan = dict(n_z=n_z, rows=rows, blocks=[(offset, 0) for offset in offsets])
        n = len(blocks)
        given = [] if before is None else [before]
        return pl.pallas_call(
            functools.partial(part_kernel, plan, before is None),
            out_shape=jax.ShapeDtypeStruct((tokens, hidden), F32),
            in_specs=[smem] + [hbm] * (n + 1 + len(given)),
            out_specs=hbm,
            scratch_shapes=[pltpu.VMEM((tokens, hidden), F32)] * 2
            + scratch(n * rows, 4 * n + 4),
            compiler_params=params,
            cost_estimate=pl.CostEstimate(
                flops=2 * tokens * n * rows * hidden,
                bytes_accessed=6 * 2**20,
                transcendentals=0,
            ),
            name="part_product",
        )(spot, gradient, *blocks, *given)

    def after(value, *others):
        return lax.optimization_barrier((value, *others))[0]

    def pairs(first, end):
        return [sign * k for k in range(first, end) for sign in (-1, 1)]

    last = n_z // 2
    for k in range(1, last - 3):
        step(k, low[k - 1], high[k - 1])
    total = part([0] + pairs(1, last - 4))
    at = last - 4
    step(at + 1, after(low[at], total), after(high[at], total))
    lora_t, lora, gradient_gram = side(gradient, 2 * RANK, RANK, "gradient_side")
    at = last - 3
    step(at + 1, after(low[at], lora_t), after(high[at], lora_t))
    step(last - 1, low[last - 2], high[last - 2])
    in_t, _, normed_gram = side(normed_all, 0, 2 * RANK, "normed_side")
    at = last - 1
    low_in, high_in = after(low[at], in_t), after(high[at], in_t)
    step(last, low_in[:half], high_in[half:])
    total = part(pairs(last - 4, last), after(total, low_in, high_in))
    blocks = [low[last], high[last]]
    plan = dict(
        n_z=n_z,
        rows=rows,
        blocks=[(last, 0), (last, half)],
        chunks=[slice(0, 2)],
    )
    sums, mids = pl.pallas_call(
        functools.partial(hidden_kernel, plan),
        out_shape=(
            jax.ShapeDtypeStruct((sequences, 3 * RANK, hidden), F32),
            jax.ShapeDtypeStruct((8 * n_tensor, tokens), F32),
        ),
        in_specs=[smem] + [hbm] * (len(blocks) + 4) + [vmem] * 4,
        out_specs=(hbm, vmem),
        scratch_shapes=[
            pltpu.VMEM((tokens, hidden), F32),
            pltpu.VMEM((tokens, hidden), F32),
            pltpu.VMEM((tokens, hidden), BF16),
            pltpu.VMEM((tokens, hidden), BF16),
            pltpu.VMEM((tokens, hidden), F32),
            pltpu.VMEM((tokens, hidden), F32),
            pltpu.VMEM((sequences, 3 * RANK, hidden), F32),
        ]
        + scratch(rows, 4 * len(blocks) + 12),
        compiler_params=params,
        name="hidden_side",
    )(
        spot,
        gradient,
        *blocks,
        total,
        gate_preactivation,
        upward_preactivation,
        adapter_hidden_factors.reshape(3 * RANK, hidden),
        in_t,
        lora,
        lora_t,
    )

    pieces = lax.all_to_all(mids.reshape(n_tensor, 8, tokens), tensor_axes, 0, 0)
    piece = jnp.sum(pieces, axis=0)
    mids = lax.all_to_all(
        jnp.broadcast_to(piece, (n_tensor,) + piece.shape), tensor_axes, 0, 0
    ).reshape(8 * n_tensor, tokens)

    lanes = (local_width + hidden) // 128
    tiles = 6 * lanes
    padded = -(-tiles // 8) * 8
    out = pl.pallas_call(
        clip_kernel,
        out_shape=jax.ShapeDtypeStruct((padded, 8, 128), F32),
        in_specs=[smem] + [hbm] * 6,
        out_specs=vmem,
        scratch_shapes=[
            pltpu.VMEM((8 * n_tensor, tokens), F32),
            pltpu.VMEM((sequences, SEQUENCE_TOKENS, SEQUENCE_TOKENS), F32),
            pltpu.VMEM((sequences, SEQUENCE_TOKENS, SEQUENCE_TOKENS), F32),
            pltpu.VMEM((tokens, local_width), BF16),
            pltpu.VMEM((tokens, local_width), BF16),
            pltpu.VMEM((sequences, 3 * RANK, hidden), F32),
            pltpu.VMEM((3 * RANK, local_width), F32),
            pltpu.SemaphoreType.DMA((6,)),
        ],
        compiler_params=params,
        name="clip_side",
    )(
        clipping_limit,
        mids,
        normed_gram,
        gradient_gram,
        normed,
        output_gradient,
        sums,
    )

    n_y = sizes["y"]
    share = jnp.sum(lax.all_to_all(out.reshape(n_y, -1, 128), "y", 0, 0), axis=0)
    share = jnp.sum(lax.all_to_all(share.reshape(n_z, -1, 128), z_axes, 0, 0), axis=0)
    share = lax.all_to_all(
        jnp.broadcast_to(share, (n_z,) + share.shape), z_axes, 0, 0
    ).reshape(-1, 128)
    whole = lax.all_to_all(jnp.broadcast_to(share, (n_y,) + share.shape), "y", 0, 0)
    total = (
        whole.reshape(padded, 8, 128)[:tiles]
        .reshape(6, lanes, 8, 128)
        .transpose(0, 2, 1, 3)
        .reshape(3, RANK, lanes * 128)
    )
    count = sequences * n_z * sizes["y"]
    bound = clipping_limit[0]
    wide = total[:, :, :local_width]
    inner = total[:, :, local_width : local_width + hidden]
    return (
        (wide + bound * width_noise_draw) / count,
        (inner + bound * hidden_noise_draw) / count,
    )


def solution(mesh):
    names = ("z", "y", "x", "c")
    extents = (16, 4, 4, 2)
    fine = Mesh(mesh.devices.reshape(extents), names)
    dp, tensor = ("z", "y"), ("x", "c")
    placed = (
        P(dp, tensor),
        P(dp, tensor),
        P(dp, tensor),
        P(dp, tensor),
        P(tensor, dp),
        P(),
        P(None, None, tensor),
        P(),
        P(None, None, tensor),
        P(None, None, tensor),
    )
    return jax.shard_map(
        functools.partial(per_device, dict(zip(names, extents, strict=True))),
        mesh=fine,
        in_specs=placed,
        out_specs=(P(None, None, tensor), P(None, None, tensor)),
        check_vma=False,
    )
```

```python
import functools

import jax
import jax.numpy as jnp
from jax import lax
from jax.experimental import pallas as pl
from jax.experimental.pallas import tpu as pltpu
from jax.sharding import Mesh
from jax.sharding import PartitionSpec as P

SEQUENCE_TOKENS = 128
RANK = 16
SCALE = 2.0
F32 = jnp.float32
BF16 = jnp.bfloat16


def contract(left, right, left_dim, right_dim):
    return lax.dot_general(
        left, right, (((left_dim,), (right_dim,)), ((), ())), preferred_element_type=F32
    )


def column_tiles(hidden, step, tile):
    whole = hidden // step

    def body(i, carry):
        tile(i, pl.multiple_of(i * step, step), step)
        return carry

    lax.fori_loop(0, whole, body, 0)
    spans = [(i * step, step) for i in range(whole)]
    if hidden > whole * step:
        spans.append((whole * step, hidden - whole * step))
        tile(whole, *spans[-1])
    return spans


def copy_rows(source, target, sems, at, parts):
    rows = source.shape[0] // parts
    copies = []
    for i in range(parts):
        span = pl.ds(i * rows, rows)
        copies.append(
            pltpu.make_async_copy(source.at[span, :], target.at[span, :], sems.at[at + i])
        )
    return copies


def fetch_blocks(plan, z_ref, gradient_ref, block_refs, left, right, sems):
    n_z, rows_z = plan["n_z"], plan["rows"]
    fetched, row, at = [], 0, 0
    for (offset, first), block in zip(plan["blocks"], block_refs, strict=True):
        rows = block.shape[0]
        start = lax.rem(z_ref[0] + (offset + n_z), n_z) * rows_z + first
        columns = pl.ds(pl.multiple_of(start, 128), rows)
        span = pl.ds(row, rows)
        fetched.append(
            copy_rows(gradient_ref.at[:, columns], left.at[:, span], sems, at, 2)
            + copy_rows(block, right.at[span, :], sems, at + 2, 2)
        )
        row += rows
        at += 4
    return fetched


def side_kernel(n_pairs, *refs):
    row_refs = refs[:n_pairs]
    factors_ref, projected_ref, turned_ref, gram_ref, total = refs[n_pairs:]
    step = pl.program_id(0)
    size = SEQUENCE_TOKENS

    @pl.when(step == 0)
    def _():
        total[...] = jnp.zeros_like(total)

    for p, rows_ref in enumerate(row_refs):
        rows = rows_ref[...]
        stacked = jnp.concatenate([rows, factors_ref[...]], axis=0)
        total[p] += contract(stacked, rows, 1, 1)

    @pl.when(step == pl.num_programs(0) - 1)
    def _():
        for p in range(n_pairs):
            gram_ref[2 * p] = total[p, :size, :size]
            gram_ref[2 * p + 1] = total[p, size : 2 * size, size:]
            span = slice(2 * size * p, 2 * size * (p + 1))
            projected = total[p, 2 * size :]
            projected_ref[:, span] = projected.astype(BF16)
            turned_ref[span, :] = projected.T.astype(BF16)


def part_kernel(plan, first, z_ref, gradient_ref, *refs):
    n_blocks = len(plan["blocks"])
    block_refs, refs = refs[:n_blocks], refs[n_blocks:]
    if not first:
        before_ref, refs = refs[0], refs[1:]
    out_ref, total, front, left, right, sems, out_sems = refs
    fetched = fetch_blocks(plan, z_ref, gradient_ref, block_refs, left, right, sems)
    early = n_blocks // 2 + 1
    head, tail = sum(fetched[:early], []), sum(fetched[early:], [])
    if not first:
        tail += copy_rows(before_ref, total, sems, 4 * n_blocks, 4)
    for copy in head + tail:
        copy.start()
    for copy in head:
        copy.wait()
    split = early * plan["rows"]
    front[...] = jnp.dot(left[:, :split], right[:split, :], preferred_element_type=F32)
    for copy in tail:
        copy.wait()

    writes = []
    hidden = total.shape[1]
    for i, start in enumerate(range(0, hidden, 512)):
        cols = slice(start, min(start + 512, hidden))
        product = front[:, cols] + jnp.dot(
            left[:, split:], right[split:, cols], preferred_element_type=F32
        )
        total[:, cols] = product if first else total[:, cols] + product
        write = pltpu.make_async_copy(total.at[:, cols], out_ref.at[:, cols], out_sems.at[i])
        write.start()
        writes.append(write)
    for write in writes:
        write.wait()


def hidden_kernel(plan, z_ref, gradient_ref, *refs):
    n_blocks = len(plan["blocks"])
    block_refs = refs[:n_blocks]
    (before_hbm, gate_hbm, up_hbm, factors_ref, in_ref, lora_ref, lora_t_ref) = refs[
        n_blocks : n_blocks + 7
    ]
    sums_hbm, mids_ref, total, before_ref, gate_ref, up_ref, silu_ref, scaled_ref, sums_ref = refs[
        n_blocks + 7 : -4
    ]
    left_rows, right_rows, sems, out_sems = refs[-4:]
    tokens, hidden = gate_ref.shape
    sequences = tokens // SEQUENCE_TOKENS
    fetched = fetch_blocks(plan, z_ref, gradient_ref, block_refs, left_rows, right_rows, sems)
    at = 4 * n_blocks
    activations = copy_rows(gate_hbm, gate_ref, sems, at, 4)
    activations += copy_rows(up_hbm, up_ref, sems, at + 4, 4)
    running = copy_rows(before_hbm, before_ref, sems, at + 8, 4)
    for copy in activations + sum(fetched, []) + running:
        copy.start()
    mids_ref[...] = jnp.zeros_like(mids_ref)

    def adapters(j, e, rows, cols, left, right):
        part = slice(j * RANK, (j + 1) * RANK)
        sums_ref[e, part, cols] = SCALE * jnp.dot(left, right, preferred_element_type=F32)
        mids_ref[part, rows] += contract(factors_ref[part, cols], right, 1, 1)

    def each(i, start, width, body):
        for e in range(sequences):
            body(e, slice(e * SEQUENCE_TOKENS, (e + 1) * SEQUENCE_TOKENS), pl.ds(start, width))

    def forward(e, rows, cols):
        gate = gate_ref[rows, cols].astype(F32)
        up = up_ref[rows, cols].astype(F32)
        sigmoid = jax.nn.sigmoid(gate)
        silu = gate * sigmoid
        slope = sigmoid * (1.0 + gate * (1.0 - sigmoid))
        silu_ref[rows, cols] = silu
        scaled_ref[rows, cols] = up * slope
        adapters(2, e, rows, cols, lora_t_ref[:, rows], (silu * up).astype(BF16))

    def backward(e, rows, cols):
        hidden_grad = (
            total[rows, cols]
            + before_ref[rows, cols]
            + SCALE
            * jnp.dot(lora_ref[rows, :], factors_ref[2 * RANK :, cols], preferred_element_type=F32)
        )
        gate_grad = (hidden_grad * scaled_ref[rows, cols]).astype(BF16)
        adapters(0, e, rows, cols, in_ref[:RANK, rows], gate_grad)
        up_grad = (hidden_grad * silu_ref[rows, cols]).astype(BF16)
        adapters(1, e, rows, cols, in_ref[RANK:, rows], up_grad)

    def write(i, cols):
        return pltpu.make_async_copy(
            sums_ref.at[:, :, cols], sums_hbm.at[:, :, cols], out_sems.at[i]
        )

    def last_tile(i, start, width):
        each(i, start, width, backward)
        write(i, pl.ds(start, width)).start()

    for copy in activations:
        copy.wait()
    column_tiles(hidden, hidden, functools.partial(each, body=forward))
    row = 0
    for some in plan["chunks"]:
        for copy in sum(fetched[some], []):
            copy.wait()
        rows = sum(block.shape[0] for block in block_refs[some])
        span = slice(row, row + rows)
        product = jnp.dot(left_rows[:, span], right_rows[span, :], preferred_element_type=F32)
        total[...] = product if row == 0 else total[...] + product
        row += rows
    for copy in running:
        copy.wait()
    spans = column_tiles(hidden, hidden, last_tile)
    for e in range(sequences):
        square = sums_ref[e] * sums_ref[e]
        line = jnp.sum(jnp.sum(square, axis=0, keepdims=True), axis=1, keepdims=True)
        mids_ref[3 * RANK + e : 3 * RANK + e + 1, :] = jnp.broadcast_to(line, (1, tokens))
    for i, (start, width) in enumerate(spans):
        write(i, pl.ds(start, width)).wait()


def quadratic(left, gram):
    product = jnp.zeros((left.shape[0], gram.shape[1]), F32)
    rest = gram
    for _ in range(3):
        part = rest.astype(BF16)
        product = product + jnp.dot(left, part, preferred_element_type=F32)
        rest = rest - part.astype(F32)
    return product * left.astype(F32)


def total_of(values):
    return jnp.sum(jnp.sum(values, axis=0, keepdims=True), axis=1, keepdims=True)


def clip_kernel(
    clip_ref,
    mids_hbm,
    normed_gram_hbm,
    gradient_gram_hbm,
    normed_hbm,
    gradient_hbm,
    sums_hbm,
    out_ref,
    mids_ref,
    normed_gram_ref,
    gradient_gram_ref,
    normed_ref,
    gradient_ref,
    sums_ref,
    wide,
    sems,
):
    copies = [
        pltpu.make_async_copy(source, target, sems.at[i])
        for i, (source, target) in enumerate(
            (
                (mids_hbm, mids_ref),
                (normed_gram_hbm, normed_gram_ref),
                (gradient_gram_hbm, gradient_gram_ref),
                (normed_hbm, normed_ref),
                (gradient_hbm, gradient_ref),
                (sums_hbm, sums_ref),
            )
        )
    ]
    for copy in copies:
        copy.start()
    sequences, _, hidden = sums_ref.shape
    local = wide.shape[1]
    bound = clip_ref[0]
    weights = []
    for copy in copies[:3]:
        copy.wait()
    for e in range(sequences):
        rows = slice(e * SEQUENCE_TOKENS, (e + 1) * SEQUENCE_TOKENS)
        mids = mids_ref[: 3 * RANK, rows].astype(BF16)
        square = total_of(quadratic(mids[: 2 * RANK], normed_gram_ref[e])) + total_of(
            quadratic(mids[2 * RANK :], gradient_gram_ref[e])
        )
        square = SCALE * SCALE * jnp.maximum(square, 0.0)
        square = square + mids_ref[3 * RANK + e : 3 * RANK + e + 1, 0:1]
        weights.append(bound / jnp.maximum(jnp.sqrt(square), bound))
    for copy in copies[3:5]:
        copy.wait()
    for e, weight in enumerate(weights):
        rows = slice(e * SEQUENCE_TOKENS, (e + 1) * SEQUENCE_TOKENS)
        mids = mids_ref[: 3 * RANK, rows].astype(BF16)
        first = weight * (
            SCALE * jnp.dot(mids[: 2 * RANK], normed_ref[rows, :], preferred_element_type=F32)
        )
        second = weight * (
            SCALE * jnp.dot(mids[2 * RANK :], gradient_ref[rows, :], preferred_element_type=F32)
        )
        if e == 0:
            wide[: 2 * RANK] = first
            wide[2 * RANK :] = second
        else:
            wide[: 2 * RANK] += first
            wide[2 * RANK :] += second
    copies[5].wait()
    lanes = (local + hidden) // 128
    for t in range(out_ref.shape[0]):
        r, c = divmod(t, lanes)
        rows = slice(8 * r, 8 * r + 8)
        at = c * 128
        if r >= 3 * RANK // 8:
            value = jnp.zeros((8, 128), F32)
        elif at < local:
            value = wide[rows, at : at + 128]
        else:
            at = at - local
            value = weights[0] * sums_ref[0, rows, at : at + 128]
            for e in range(1, sequences):
                value = value + weights[e] * sums_ref[e, rows, at : at + 128]
        out_ref[t] = value


def ring(size, by):
    return [(i, (i + by) % size) for i in range(size)]


def per_device(
    sizes,
    normed,
    output_gradient,
    gate_preactivation,
    upward_preactivation,
    frozen_down_weight,
    adapter_width_factors,
    adapter_hidden_factors,
    clipping_limit,
    width_noise_draw,
    hidden_noise_draw,
):
    tokens, local_width = normed.shape
    hidden = gate_preactivation.shape[1]
    sequences = tokens // SEQUENCE_TOKENS
    n_z = sizes["z"]
    n_tensor = sizes["x"] * sizes["c"]
    z_axes, tensor_axes = "z", ("x", "c")
    spot = lax.axis_index(z_axes).reshape(1).astype(jnp.int32)

    gradient = lax.all_gather(output_gradient, tensor_axes, axis=1, tiled=True)
    block = lax.all_gather(frozen_down_weight.T, "y", axis=0, tiled=True)
    normed_all = lax.all_gather(normed, tensor_axes, axis=1, tiled=True)

    rows = block.shape[0]
    half = rows // 2
    vmem = pl.BlockSpec(memory_space=pltpu.VMEM)
    smem = pl.BlockSpec(memory_space=pltpu.SMEM)
    hbm = pl.BlockSpec(memory_space=pl.ANY)
    params = pltpu.CompilerParams(vmem_limit_bytes=60 * 2**20)

    low, high = {0: block}, {0: block}

    def step(k, low_from, high_from):
        low[k] = lax.ppermute(low_from, z_axes, ring(n_z, 1))
        high[k] = lax.ppermute(high_from, z_axes, ring(n_z, -1))

    def side(values, first, count, name):
        width = values.shape[1]
        chunk = 2048
        return pl.pallas_call(
            functools.partial(side_kernel, sequences // 2),
            out_shape=(
                jax.ShapeDtypeStruct((count, tokens), BF16),
                jax.ShapeDtypeStruct((tokens, count), BF16),
                jax.ShapeDtypeStruct((sequences, SEQUENCE_TOKENS, SEQUENCE_TOKENS), F32),
            ),
            grid=(width // chunk,),
            in_specs=[
                pl.BlockSpec((2 * SEQUENCE_TOKENS, chunk), functools.partial(lambda p, i: (p, i), p))
                for p in range(sequences // 2)
            ]
            + [pl.BlockSpec((count, chunk), lambda i: (first // count, i))],
            out_specs=(
                pl.BlockSpec((count, tokens), lambda i: (0, 0)),
                pl.BlockSpec((tokens, count), lambda i: (0, 0)),
                pl.BlockSpec((sequences, SEQUENCE_TOKENS, SEQUENCE_TOKENS), lambda i: (0, 0, 0)),
            ),
            scratch_shapes=[
                pltpu.VMEM(
                    (sequences // 2, 2 * SEQUENCE_TOKENS + count, 2 * SEQUENCE_TOKENS), F32
                )
            ],
            compiler_params=params,
            cost_estimate=pl.CostEstimate(
                flops=2 * tokens * width * (128 + count),
                bytes_accessed=5 * 2**20,
                transcendentals=0,
            ),
            name=name,
        )(*[values] * (sequences // 2), adapter_width_factors.reshape(3 * RANK, width))

    def scratch(n_rows, n_sems):
        return [
            pltpu.VMEM((tokens, n_rows), BF16),
            pltpu.VMEM((n_rows, hidden), BF16),
            pltpu.SemaphoreType.DMA((n_sems,)),
            pltpu.SemaphoreType.DMA((-(-hidden // 256),)),
        ]

    def at_z(offset):
        return (low if offset < 0 else high)[abs(offset)]

    def part(offsets, before=None):
        blocks = [at_z(offset) for offset in offsets]
        plan = dict(n_z=n_z, rows=rows, blocks=[(offset, 0) for offset in offsets])
        n = len(blocks)
        given = [] if before is None else [before]
        return pl.pallas_call(
            functools.partial(part_kernel, plan, before is None),
            out_shape=jax.ShapeDtypeStruct((tokens, hidden), F32),
            in_specs=[smem] + [hbm] * (n + 1 + len(given)),
            out_specs=hbm,
            scratch_shapes=[pltpu.VMEM((tokens, hidden), F32)] * 2
            + scratch(n * rows, 4 * n + 4),
            compiler_params=params,
            cost_estimate=pl.CostEstimate(
                flops=2 * tokens * n * rows * hidden,
                bytes_accessed=6 * 2**20,
                transcendentals=0,
            ),
            name="part_product",
        )(spot, gradient, *blocks, *given)

    def after(value, *others):
        return lax.optimization_barrier((value, *others))[0]

    def pairs(first, end):
        return [sign * k for k in range(first, end) for sign in (-1, 1)]

    last = n_z // 2
    for k in range(1, last - 3):
        step(k, low[k - 1], high[k - 1])
    total = part([0] + pairs(1, last - 4))
    at = last - 4
    step(at + 1, after(low[at], total), after(high[at], total))
    lora_t, lora, gradient_gram = side(gradient, 2 * RANK, RANK, "gradient_side")
    at = last - 3
    step(at + 1, after(low[at], lora_t), after(high[at], lora_t))
    step(last - 1, low[last - 2], high[last - 2])
    in_t, _, normed_gram = side(normed_all, 0, 2 * RANK, "normed_side")
    at = last - 1
    low_in, high_in = after(low[at], in_t), after(high[at], in_t)
    step(last, low_in[:half], high_in[half:])
    total = part(pairs(last - 4, last), after(total, low_in, high_in))
    blocks = [low[last], high[last]]
    plan = dict(
        n_z=n_z,
        rows=rows,
        blocks=[(last, 0), (last, half)],
        chunks=[slice(0, 2)],
    )
    sums, mids = pl.pallas_call(
        functools.partial(hidden_kernel, plan),
        out_shape=(
            jax.ShapeDtypeStruct((sequences, 3 * RANK, hidden), F32),
            jax.ShapeDtypeStruct((8 * n_tensor, tokens), F32),
        ),
        in_specs=[smem] + [hbm] * (len(blocks) + 4) + [vmem] * 4,
        out_specs=(hbm, vmem),
        scratch_shapes=[
            pltpu.VMEM((tokens, hidden), F32),
            pltpu.VMEM((tokens, hidden), F32),
            pltpu.VMEM((tokens, hidden), BF16),
            pltpu.VMEM((tokens, hidden), BF16),
            pltpu.VMEM((tokens, hidden), F32),
            pltpu.VMEM((tokens, hidden), F32),
            pltpu.VMEM((sequences, 3 * RANK, hidden), F32),
        ]
        + scratch(rows, 4 * len(blocks) + 12),
        compiler_params=params,
        name="hidden_side",
    )(
        spot,
        gradient,
        *blocks,
        total,
        gate_preactivation,
        upward_preactivation,
        adapter_hidden_factors.reshape(3 * RANK, hidden),
        in_t,
        lora,
        lora_t,
    )

    pieces = lax.all_to_all(mids.reshape(n_tensor, 8, tokens), tensor_axes, 0, 0)
    piece = jnp.sum(pieces, axis=0)
    mids = lax.all_to_all(
        jnp.broadcast_to(piece, (n_tensor,) + piece.shape), tensor_axes, 0, 0
    ).reshape(8 * n_tensor, tokens)

    lanes = (local_width + hidden) // 128
    tiles = 6 * lanes
    padded = -(-tiles // 8) * 8
    out = pl.pallas_call(
        clip_kernel,
        out_shape=jax.ShapeDtypeStruct((padded, 8, 128), F32),
        in_specs=[smem] + [hbm] * 6,
        out_specs=vmem,
        scratch_shapes=[
            pltpu.VMEM((8 * n_tensor, tokens), F32),
            pltpu.VMEM((sequences, SEQUENCE_TOKENS, SEQUENCE_TOKENS), F32),
            pltpu.VMEM((sequences, SEQUENCE_TOKENS, SEQUENCE_TOKENS), F32),
            pltpu.VMEM((tokens, local_width), BF16),
            pltpu.VMEM((tokens, local_width), BF16),
            pltpu.VMEM((sequences, 3 * RANK, hidden), F32),
            pltpu.VMEM((3 * RANK, local_width), F32),
            pltpu.SemaphoreType.DMA((6,)),
        ],
        compiler_params=pltpu.CompilerParams(vmem_limit_bytes=8 * 2**20),
        name="clip_side",
    )(
        clipping_limit,
        mids,
        normed_gram,
        gradient_gram,
        normed,
        output_gradient,
        sums,
    )

    n_y = sizes["y"]
    share = jnp.sum(lax.all_to_all(out.reshape(n_y, -1, 128), "y", 0, 0), axis=0)
    share = jnp.sum(lax.all_to_all(share.reshape(n_z, -1, 128), z_axes, 0, 0), axis=0)
    share = lax.all_to_all(
        jnp.broadcast_to(share, (n_z,) + share.shape), z_axes, 0, 0
    ).reshape(-1, 128)
    whole = lax.all_to_all(jnp.broadcast_to(share, (n_y,) + share.shape), "y", 0, 0)
    total = (
        whole.reshape(padded, 8, 128)[:tiles]
        .reshape(6, lanes, 8, 128)
        .transpose(0, 2, 1, 3)
        .reshape(3, RANK, lanes * 128)
    )
    count = sequences * n_z * sizes["y"]
    bound = clipping_limit[0]
    wide = total[:, :, :local_width]
    inner = total[:, :, local_width : local_width + hidden]
    return (
        (wide + bound * width_noise_draw) / count,
        (inner + bound * hidden_noise_draw) / count,
    )


def solution(mesh):
    names = ("z", "y", "x", "c")
    extents = (16, 4, 4, 2)
    fine = Mesh(mesh.devices.reshape(extents), names)
    dp, tensor = ("z", "y"), ("x", "c")
    placed = (
        P(dp, tensor),
        P(dp, tensor),
        P(dp, tensor),
        P(dp, tensor),
        P(tensor, dp),
        P(),
        P(None, None, tensor),
        P(),
        P(None, None, tensor),
        P(None, None, tensor),
    )
    return jax.shard_map(
        functools.partial(per_device, dict(zip(names, extents, strict=True))),
        mesh=fine,
        in_specs=placed,
        out_specs=(P(None, None, tensor), P(None, None, tensor)),
        check_vma=False,
    )
```
